256 devices in a mesh: dp: 2 (over z_lo), seq: 128 (over y, z_hi, x, core).
Axes of the slice: x: 4, y: 4, z: 8 (z_hi: 4, z_lo: 2; z = z_hi * 2 + z_lo), core: 2. Of those that a mesh axis runs over, the one named last changes fastest.
Arguments:
- block_input: bfloat16 [2, 1024, 160, 256], P('dp', 'seq'), may hold values from -42 to 42
- cotangent: bfloat16 [2, 1024, 160, 256], P('dp', 'seq'), may hold values from -5.2 to 5.2
- group_norm_gain: float32 [256], replicated, may hold values from 0.5 to 2
- group_norm_bias: float32 [256], replicated, may hold values from -2 to 2
- w_spatial: bfloat16 [9, 256, 256], replicated, may hold values from -0.125 to 0.125
- w_temporal: bfloat16 [3, 256, 256], replicated, may hold values from -0.21875 to 0.21875
Outputs:
- block_grad: bfloat16 [2, 1024, 160, 256], P('dp', 'seq')
- spatial_grad: float32 [9, 256, 256], replicated
- temporal_grad: float32 [3, 256, 256], replicated
- gain_grad: float32 [256], replicated
- bias_grad: float32 [256], replicated
The draws below stay inside these ranges and needn't reach their ends.
All inputs are finite; a program needn't handle non-finite values.
Results may differ from the reference program's by a relative error of at most 0.0051.
Values may be sent and summed in bfloat16 or wider, within the bound.
A program may use at most 64 MiB of HBM per device.

```python
import math
import jax
import jax.numpy as jnp
from jax import lax

CHANNEL_COUNT = 256
NORM_GROUPS = 32
ROWS = 32
COLS = 160
FRAMES = 32
CLIPS = 2


def draw_block_input(key, part):
    key = jax.random.fold_in(key, 11)
    base_key, jitter_key, chan_key, offset_key = jax.random.split(key, 4)
    row_total = FRAMES * ROWS
    position = jnp.arange(row_total, dtype=jnp.float32) / float(max(row_total - 1, 1))
    jitter = jax.random.uniform(jitter_key, (row_total,), jnp.float32)
    row_scale = jnp.exp(math.log(3.0) * position + math.log(10.0 / 3.0) * jitter)
    chan_scale = jnp.exp(math.log(10.0) * jax.random.uniform(chan_key, (CHANNEL_COUNT,), jnp.float32))
    offset = jax.random.uniform(offset_key, (CHANNEL_COUNT,), jnp.float32, -1.0, 1.0) / 3.0
    base = jax.random.truncated_normal(base_key, -4.0, 4.0, (CLIPS, row_total, COLS, CHANNEL_COUNT), jnp.float32)
    values = 0.1 * base * row_scale[None, :, None, None] * chan_scale + offset
    return values.astype(jnp.bfloat16)


def draw_cotangent(key, part):
    key = jax.random.fold_in(key, 23)
    base_key, offset_key = jax.random.split(key, 2)
    row_total = FRAMES * ROWS
    clip_sign = jnp.where(jnp.arange(CLIPS) % 2 == 0, 1.0, -1.0).astype(jnp.float32)
    base = jax.random.truncated_normal(base_key, -4.0, 4.0, (CLIPS, row_total, COLS, CHANNEL_COUNT), jnp.float32)
    offset = jax.random.uniform(offset_key, (CHANNEL_COUNT,), jnp.float32, -1.0, 1.0)
    values = base + clip_sign[:, None, None, None] * offset
    return values.astype(jnp.bfloat16)


def bell_draw(stream_key, dims, scale, reach, kind=jnp.bfloat16):
    result = jax.random.normal(stream_key, dims, jnp.float32) * scale
    return jnp.minimum(jnp.maximum(result, -reach), reach).astype(kind)


def setup_inputs(seed: int = 0) -> dict:
    splits = jax.random.split(jax.random.key(seed), 7)
    block_input = draw_block_input(jax.random.fold_in(splits[6], 71), 0)
    cotangent = draw_cotangent(jax.random.fold_in(splits[6], 71), 0)
    group_norm_gain = jnp.clip(jnp.exp(jax.random.uniform(splits[2], (CHANNEL_COUNT,), jnp.float32, math.log(0.5), math.log(2.0))), 0.5, 2.0)
    group_norm_bias = bell_draw(splits[3], (CHANNEL_COUNT,), 0.5, 2.0, jnp.float32)
    w_spatial = bell_draw(splits[4], (9, CHANNEL_COUNT, CHANNEL_COUNT), (9 * CHANNEL_COUNT) ** -0.5, 0.125)
    w_temporal = bell_draw(splits[5], (3, CHANNEL_COUNT, CHANNEL_COUNT), (3 * CHANNEL_COUNT) ** -0.5, 0.21875)
    return {"block_input": block_input, "cotangent": cotangent, "group_norm_gain": group_norm_gain, "group_norm_bias": group_norm_bias, "w_spatial": w_spatial, "w_temporal": w_temporal}


EPS = 1e-06

def frame_taps(padded):
    width = padded.shape[-1]
    return [padded[:, dy:dy + ROWS, dx:dx + COLS].reshape(-1, width) for dy in range(3) for dx in range(3)]

def temporal_grads(u_frames, g_frames, w_temporal):
    count_frames = u_frames.shape[0]
    width = u_frames.shape[2]
    grads = []
    back = None
    for k in range(3):
        early = u_frames[:count_frames - k].reshape(-1, width)
        late = g_frames[k:].reshape(-1, width)
        grads.append(lax.dot_general(early, late, (((0,), (0,)), ((), ())), preferred_element_type=jnp.float32))
        term = lax.dot_general(late, w_temporal[k], (((1,), (1,)), ((), ())), preferred_element_type=jnp.float32)
        term = term.reshape(count_frames - k, -1, width)
        term = jnp.concatenate([term, jnp.zeros((k,) + term.shape[1:], term.dtype)], 0)
        back = term if k == 0 else back + term
    return (jnp.stack(grads), back)

def clip_grads(x_stored, grad_stored, group_norm_gain, group_norm_bias, w_spatial, w_temporal):
    half_frame = ROWS // 2
    x = jnp.roll(x_stored, half_frame, axis=0)
    grad_out = jnp.roll(grad_stored, half_frame, axis=0)
    pixel_values = FRAMES * ROWS * COLS
    channels_per_group = CHANNEL_COUNT // NORM_GROUPS
    count = pixel_values * channels_per_group
    input_float = x.astype(jnp.float32).reshape(pixel_values, NORM_GROUPS, channels_per_group)
    group_mean = lax.optimization_barrier(jnp.sum(input_float, axis=(0, 2))) / count
    inverse_deviation = lax.rsqrt(lax.optimization_barrier(jnp.sum(input_float * input_float, axis=(0, 2))) / count - group_mean * group_mean + EPS)
    normalized_input = ((input_float - group_mean[None, :, None]) * inverse_deviation[None, :, None]).reshape(pixel_values, CHANNEL_COUNT)
    preactivation = normalized_input * group_norm_gain + group_norm_bias
    sigma = jax.nn.sigmoid(preactivation)
    act = (preactivation * sigma).astype(jnp.bfloat16).reshape(FRAMES, ROWS, COLS, CHANNEL_COUNT)
    act_taps = frame_taps(jnp.pad(act, ((0, 0), (1, 1), (1, 1), (0, 0))))
    conv_out = jnp.dot(act_taps[0], w_spatial[0], preferred_element_type=jnp.float32)
    for tap in range(1, 9):
        conv_out = conv_out + jnp.dot(act_taps[tap], w_spatial[tap], preferred_element_type=jnp.float32)
    conv_out = conv_out.astype(jnp.bfloat16)
    grad_flat = grad_out.reshape(pixel_values, CHANNEL_COUNT)
    temporal_part, back = temporal_grads(conv_out.reshape(FRAMES, ROWS * COLS, CHANNEL_COUNT), grad_flat.reshape(FRAMES, ROWS * COLS, CHANNEL_COUNT), w_temporal)
    conv_grad = back.astype(jnp.bfloat16).reshape(pixel_values, CHANNEL_COUNT)
    grad_taps = frame_taps(jnp.pad(conv_grad.reshape(FRAMES, ROWS, COLS, CHANNEL_COUNT), ((0, 0), (1, 1), (1, 1), (0, 0))))
    act_grad = lax.dot_general(grad_taps[0], w_spatial[8], (((1,), (1,)), ((), ())), preferred_element_type=jnp.float32)
    for tap in range(1, 9):
        act_grad = act_grad + lax.dot_general(grad_taps[tap], w_spatial[8 - tap], (((1,), (1,)), ((), ())), preferred_element_type=jnp.float32)
    spatial_part = jnp.stack([lax.dot_general(act_taps[tap], conv_grad, (((0,), (0,)), ((), ())), preferred_element_type=jnp.float32) for tap in range(9)])
    preactivation_gradient = act_grad * sigma * (1.0 + preactivation * (1.0 - sigma))
    gain_share = lax.optimization_barrier(jnp.sum(preactivation_gradient * normalized_input, axis=0))
    bias_part = lax.optimization_barrier(jnp.sum(preactivation_gradient, axis=0))
    norm_grad = (preactivation_gradient * group_norm_gain).reshape(pixel_values, NORM_GROUPS, channels_per_group)
    input_grouped = normalized_input.reshape(pixel_values, NORM_GROUPS, channels_per_group)
    first = lax.optimization_barrier(jnp.sum(norm_grad, axis=(0, 2))) / count
    second = lax.optimization_barrier(jnp.sum(norm_grad * input_grouped, axis=(0, 2))) / count
    input_grad = inverse_deviation[None, :, None] * (norm_grad - first[None, :, None] - input_grouped * second[None, :, None])
    block_grad = (grad_flat.astype(jnp.float32) + input_grad.reshape(pixel_values, CHANNEL_COUNT)).astype(jnp.bfloat16)
    block_grad = jnp.roll(block_grad.reshape(FRAMES * ROWS, COLS, CHANNEL_COUNT), -half_frame, axis=0)
    return (block_grad, spatial_part, temporal_part, gain_share, bias_part)

def reference(block_input, cotangent, group_norm_gain, group_norm_bias, w_spatial, w_temporal):

    def one_clip(pair):
        return clip_grads(pair[0], pair[1], group_norm_gain, group_norm_bias, w_spatial, w_temporal)
    block_grad, spatial_part, temporal_part, gain_share, bias_part = lax.map(one_clip, (block_input, cotangent))
    scale = 1.0 / math.sqrt(CLIPS * FRAMES * ROWS * COLS)
    return (block_grad, lax.optimization_barrier(jnp.sum(spatial_part, axis=0)) * scale, lax.optimization_barrier(jnp.sum(temporal_part, axis=0)) * scale, lax.optimization_barrier(jnp.sum(gain_share, axis=0)) * scale, lax.optimization_barrier(jnp.sum(bias_part, axis=0)) * scale)
```

```python
import math

import jax
import jax.numpy as jnp
from jax import lax
from jax.experimental import pallas as pl
from jax.experimental.pallas import tpu as pltpu
from jax.sharding import PartitionSpec as P

F32 = jnp.float32
BF16 = jnp.bfloat16
MESH = pl.DeviceIdType.MESH

CHANNELS = 256
GROUP = 8
ROWS_DEV = 8
COLS = 160
PIXELS = ROWS_DEV * COLS
PADDED = PIXELS + 2 * COLS
SEQ = 128
FRAMES = 32
EPS = 1e-06
COUNT = FRAMES * 32 * COLS * GROUP
SCALE = 1.0 / math.sqrt(2 * FRAMES * 32 * COLS)

ORDER = (0, 7, 1, 2, 3, 4, 5, 6)
BLOCK = 2 * COLS

TAPS = 12
HALF_ROWS = TAPS * CHANNELS
PART = HALF_ROWS // 2
QUARTER = PART // 4
SIXTEENTH = PART // 16
SHARD = 2 * SIXTEENTH // 4


def kernel(
    x_hbm, g_hbm, gain_ref, bias_ref, wsp_hbm, wt_hbm,
    grad_out, params_out, gain_out, bias_out,
    xv, cots, act3, act3t, cg3, conv, convt, wsp, wspt, wt, wtt, pre_grad,
    act_halo, cg_halo, stat_a, stat_b, back_a, back_b, clip_sums,
    part, core_in, in1a, in1b, mid_a, mid_b, in2a, in2b, mid2, in3, full,
    load_sem, far_send, far_recv, near_send, near_recv,
    ah_send, ah_recv, ch_send, ch_recv,
    sa_send, sa_recv, sb_send, sb_recv, ba_send, ba_recv, bb_send, bb_recv, clip_sem,
    core_send, core_recv, s1_send, s1_recv, s2_send, s2_recv, s3_send, s3_recv,
    g3_send, g3_recv, g2_send, g2_recv, g1_send, g1_recv, gc_send, gc_recv,
):
    clip = lax.axis_index("dp")
    seq = lax.axis_index("seq")
    core = lax.rem(seq, 2)
    x = lax.rem(seq // 2, 4)
    zh = lax.rem(seq // 8, 4)
    y = seq // 32
    low = lax.rem(seq, 8)
    high = seq // 8
    z = zh * 2 + clip
    slab = lax.rem(seq + 2, SEQ)
    place = lax.rem(slab, 4)
    frame = slab // 4

    def at(s):
        return (clip, s)

    def at_x(o):
        return (clip, seq + 2 * (o - x))

    def at_y(o):
        return (clip, seq + 32 * (o - y))

    def at_zh(o):
        return (clip, seq + 8 * (o - zh))

    def at_z(o):
        return (lax.rem(o, 2), seq + 8 * (o // 2 - zh))

    up = lax.rem(seq + 1, SEQ)
    down = lax.rem(seq + SEQ - 1, SEQ)
    far_to = lax.rem(seq + SEQ - 8, SEQ)
    far_from = lax.rem(seq + 8, SEQ)
    other_core = seq + 1 - 2 * core
    x_high = x // 2
    near_to = seq + 4 - 8 * x_high

    def copy(src, dst, send_sem, recv_sem, device):
        return pltpu.make_async_remote_copy(
            src_ref=src, dst_ref=dst, send_sem=send_sem, recv_sem=recv_sem,
            device_id=device, device_id_type=MESH,
        )

    load_x = pltpu.make_async_copy(x_hbm, xv, load_sem.at[0])
    load_g = pltpu.make_async_copy(g_hbm, cots.at[0], load_sem.at[1])
    load_wsp = pltpu.make_async_copy(wsp_hbm, wsp, load_sem.at[2])
    load_wt = pltpu.make_async_copy(wt_hbm, wt, load_sem.at[3])
    load_x.start()
    load_g.start()
    load_wsp.start()
    load_wt.start()

    barrier = pltpu.get_barrier_semaphore()

    def greet(device):
        pl.semaphore_signal(barrier, inc=1, device_id=device, device_id_type=MESH)

    def greet_low(j, _):
        greet(at(seq - low + lax.rem(low + j, 8)))
        return 0

    def greet_high(j, _):
        greet(at(lax.rem(high + j, 16) * 8 + low))
        return 0

    def greet_z(j, _):
        greet((1 - clip, seq + 8 * (j - zh)))
        return 0

    lax.fori_loop(1, 8, greet_low, 0)
    lax.fori_loop(1, 16, greet_high, 0)
    lax.fori_loop(0, 4, greet_z, 0)
    greet(at(up))
    greet(at(down))
    pl.semaphore_wait(barrier, 7 + 15 + 4 + 2)

    def far_copy(k):
        rows = pl.ds(ORDER[k] * COLS, COLS)
        return copy(
            g_hbm.at[rows], cots.at[2, rows], far_send.at[k], far_recv.at[k], at(far_to)
        )

    def near_copy(k):
        rows = pl.ds(ORDER[k] * COLS, COLS)
        return copy(
            cots.at[2 * (1 - x_high), rows], cots.at[1, rows],
            near_send.at[k], near_recv.at[k], at(near_to),
        )

    for k in range(8):
        far_copy(k).start()

    def exchange(buf, n, me, target, send_sem, recv_sem):
        def body(j, _):
            o = lax.rem(me + j, n)
            copy(buf.at[me], buf.at[me], send_sem.at[o], recv_sem.at[me], at(target(o))).start()
            return 0

        lax.fori_loop(1, n, body, 0)

    def collect(buf, n, me, target, send_sem, recv_sem):
        def body(j, _):
            o = lax.rem(me + j, n)
            arrived = copy(buf.at[o], buf.at[o], send_sem.at[o], recv_sem.at[o], at(target(o)))
            arrived.wait_send()
            arrived.wait_recv()
            return 0

        lax.fori_loop(1, n, body, 0)
        total = buf[0]
        for o in range(1, n):
            total = total + buf[o]
        return total

    def low_of(o):
        return seq - low + o

    def high_of(o):
        return o * 8 + low

    row_id = lax.broadcasted_iota(jnp.int32, (8, CHANNELS), 0)

    def pack_rows(first, second):
        return jnp.where(row_id == 0, first, jnp.where(row_id == 1, second, 0.0))

    group_a = lax.shift_right_logical(lax.broadcasted_iota(jnp.int32, (CHANNELS, CHANNELS), 0), 3)
    group_b = lax.shift_right_logical(lax.broadcasted_iota(jnp.int32, (CHANNELS, CHANNELS), 1), 3)
    same_group = jnp.where(group_a == group_b, 1.0, 0.0).astype(BF16)

    def group_sum(v):
        total = jnp.zeros_like(v)
        rest = v
        for _ in range(3):
            piece = rest.astype(BF16)
            rest = rest - piece.astype(F32)
            total = total + jnp.dot(piece, same_group, preferred_element_type=F32)
        return total

    load_x.wait()

    def stat_body(i, carry):
        a, b = carry
        blk = xv[pl.ds(i * COLS, COLS), :].astype(F32).reshape(COLS // 8, 8, CHANNELS)
        return a + jnp.sum(blk, axis=0), b + jnp.sum(blk * blk, axis=0)

    zero8 = jnp.zeros((8, CHANNELS), F32)
    a, b = lax.fori_loop(0, ROWS_DEV, stat_body, (zero8, zero8))
    stat_a[low] = pack_rows(jnp.sum(a, axis=0, keepdims=True), jnp.sum(b, axis=0, keepdims=True))
    exchange(stat_a, 8, low, low_of, sa_send, sa_recv)

    load_wt.wait()
    load_wsp.wait()
    for k in range(3):
        wtt[k] = wt[k].T

    def turn_weight(i, _):
        wspt[pl.ds(i * CHANNELS, CHANNELS), :] = wsp[pl.ds((8 - i) * CHANNELS, CHANNELS), :].T
        return 0

    lax.fori_loop(0, 9, turn_weight, 0)

    stat_b[high] = collect(stat_a, 8, low, low_of, sa_send, sa_recv)
    exchange(stat_b, 16, high, high_of, sb_send, sb_recv)
    load_g.wait()
    moments = group_sum(collect(stat_b, 16, high, high_of, sb_send, sb_recv)) * (1.0 / COUNT)
    mean = moments[0:1]
    rstd = lax.rsqrt(moments[1:2] - mean * mean + EPS)
    gain = gain_ref[...]
    bias = bias_ref[...]

    def forward(k):
        far_copy(k).wait_recv()
        near_copy(k).start()

    forward(0)
    forward(1)

    col_id = lax.broadcasted_iota(jnp.int32, (COLS, CHANNELS), 0)

    def store_shifts(buf, padded_row, v):
        rows = pl.ds(padded_row * COLS, COLS)
        buf[rows, CHANNELS : 2 * CHANNELS] = v.astype(BF16)
        left = jnp.where(col_id == 0, 0.0, pltpu.roll(v, 1, 0))
        right = jnp.where(col_id == COLS - 1, 0.0, pltpu.roll(v, COLS - 1, 0))
        buf[rows, 0:CHANNELS] = left.astype(BF16)
        buf[rows, 2 * CHANNELS : 3 * CHANNELS] = right.astype(BF16)

    def normalize(rows):
        xhat = (xv[rows, :].astype(F32) - mean) * rstd
        pre = xhat * gain + bias
        return xhat, pre, jax.nn.sigmoid(pre)

    def act_row(r):
        _, pre, sigma = normalize(pl.ds(r * COLS, COLS))
        store_shifts(act3, r + 1, pre * sigma)

    middle = slice(CHANNELS, 2 * CHANNELS)

    def halo_copies(buf, halo, send_sem, recv_sem):
        first = copy(
            buf.at[pl.ds(COLS, COLS), middle], halo.at[1], send_sem.at[0], recv_sem.at[1], at(down)
        )
        last = copy(
            buf.at[pl.ds(PIXELS, COLS), middle], halo.at[0], send_sem.at[1], recv_sem.at[0], at(up)
        )
        return first, last

    def send_halo(buf, halo, send_sem, recv_sem):
        for c in halo_copies(buf, halo, send_sem, recv_sem):
            c.start()

    def take_halo(buf, halo, send_sem, recv_sem):
        for c in halo_copies(buf, halo, send_sem, recv_sem):
            c.wait_send()
            c.wait_recv()
        keep_low = jnp.where(place > 0, 1.0, 0.0).astype(F32)
        keep_high = jnp.where(place < 3, 1.0, 0.0).astype(F32)
        store_shifts(buf, 0, halo[0].astype(F32) * keep_low)
        store_shifts(buf, ROWS_DEV + 1, halo[1].astype(F32) * keep_high)

    act_row(0)
    act_row(ROWS_DEV - 1)
    send_halo(act3, act_halo, ah_send, ah_recv)

    def act_body(r, _):
        act_row(r)
        return 0

    lax.fori_loop(1, ROWS_DEV - 1, act_body, 0)
    take_halo(act3, act_halo, ah_send, ah_recv)
    forward(2)

    def convolve(buf, weights, i):
        total = None
        for dy in range(3):
            term = jnp.dot(
                buf[pl.ds(i * BLOCK + dy * COLS, BLOCK), :],
                weights[dy * 3 * CHANNELS : (dy + 1) * 3 * CHANNELS, :],
                preferred_element_type=F32,
            )
            total = term if total is None else total + term
        return total

    def conv_body(i, _):
        conv[pl.ds(i * BLOCK, BLOCK), :] = convolve(act3, wsp, i).astype(BF16)
        return 0

    lax.fori_loop(0, PIXELS // BLOCK, conv_body, 0)
    forward(3)

    def turn_conv(i, _):
        src = pl.ds(pl.multiple_of(i * 128, 128), 128)
        convt[:, src] = conv[src, :].T
        return 0

    lax.fori_loop(0, PIXELS // 128, turn_conv, 0)

    for dy in range(3):
        def turn_act(i, _):
            dst = pl.ds(pl.multiple_of(i * 128, 128), 128)
            src = pl.ds(pl.multiple_of(dy * COLS + i * 128, 32), 128)
            act3t[dy, :, dst] = act3[src, :].T
            return 0

        lax.fori_loop(0, PIXELS // 128, turn_act, 0)
        forward(4 + dy)

    keep1 = jnp.where(frame < FRAMES - 1, 1.0, 0.0).astype(F32)
    keep2 = jnp.where(frame < FRAMES - 2, 1.0, 0.0).astype(F32)

    def cg_row(k):
        r = ORDER[k]
        near_copy(k).wait_recv()
        rows = pl.ds(r * COLS, COLS)
        total = jnp.dot(cots[0, rows, :], wtt[0], preferred_element_type=F32)
        total = total + keep1 * jnp.dot(cots[1, rows, :], wtt[1], preferred_element_type=F32)
        total = total + keep2 * jnp.dot(cots[2, rows, :], wtt[2], preferred_element_type=F32)
        store_shifts(cg3, r + 1, total.astype(BF16).astype(F32))

    for k in range(8):
        if k == 4:
            forward(7)
        cg_row(k)
        if k == 1:
            send_halo(cg3, cg_halo, ch_send, ch_recv)

    def put(first_row, v):
        part[0, pl.ds(first_row, v.shape[0]), :] = v[:, :128]
        part[1, pl.ds(first_row, v.shape[0]), :] = v[:, 128:]

    chunk_rows = 3 * CHANNELS

    def core_copy(i):
        rows = pl.ds(i * chunk_rows, chunk_rows)
        return copy(
            part.at[1 - core, rows], core_in.at[rows], core_send.at[i], core_recv.at[i],
            at(other_core),
        )

    for k, keep in enumerate((None, keep1, keep2)):
        v = jnp.dot(convt[...], cots[k], preferred_element_type=F32)
        put((9 + k) * CHANNELS, v if keep is None else v * keep)
    core_copy(3).start()
    for dy in range(3):
        put(
            dy * chunk_rows,
            jnp.dot(
                act3t[dy], cg3[COLS : COLS + PIXELS, middle], preferred_element_type=F32
            ),
        )
        core_copy(dy).start()

    take_halo(cg3, cg_halo, ch_send, ch_recv)

    def back_body(i, carry):
        rows = pl.ds(i * BLOCK, BLOCK)
        xhat, pre, sigma = normalize(rows)
        v = convolve(cg3, wspt, i) * sigma * (1.0 + pre * (1.0 - sigma))
        pre_grad[rows, :] = v
        a, b = carry
        a = a + jnp.sum(v.reshape(BLOCK // 8, 8, CHANNELS), axis=0)
        b = b + jnp.sum((v * xhat).reshape(BLOCK // 8, 8, CHANNELS), axis=0)
        return a, b

    a, b = lax.fori_loop(0, PIXELS // BLOCK, back_body, (zero8, zero8))
    back_a[low] = pack_rows(jnp.sum(a, axis=0, keepdims=True), jnp.sum(b, axis=0, keepdims=True))
    exchange(back_a, 8, low, low_of, ba_send, ba_recv)

    def add_core(i):
        core_copy(i).wait_send()
        core_copy(i).wait_recv()
        rows = pl.ds(i * chunk_rows, chunk_rows)
        part[core, rows, :] = part[core, rows, :] + core_in[rows, :]

    def loop3(me, body):
        def step(j, _):
            body(j, lax.rem(me + j, 4))
            return 0

        lax.fori_loop(1, 4, step, 0)

    def s1_copy(which, me, o, peer):
        buf = (in1a, in1b)[which]
        target = (at_x, at_y)[which]
        return copy(
            part.at[core, pl.ds(which * PART + o * QUARTER, QUARTER)], buf.at[me],
            s1_send.at[which, o], s1_recv.at[which, me], target(peer),
        )

    def s1_start(which):
        me = (x, y)[which]
        loop3(me, lambda j, o: s1_copy(which, me, o, o).start())

    add_core(3)
    add_core(2)
    s1_start(1)
    add_core(0)
    add_core(1)
    s1_start(0)

    back_b[high] = collect(back_a, 8, low, low_of, ba_send, ba_recv)
    exchange(back_b, 16, high, high_of, bb_send, bb_recv)

    def s1_finish(which):
        me = (x, y)[which]
        buf = (in1a, in1b)[which]
        mid = (mid_a, mid_b)[which]

        def wait(j, o):
            s1_copy(which, me, o, o).wait_send()
            s1_copy(which, o, o, o).wait_recv()

        loop3(me, wait)
        mine = pl.ds(which * PART + me * QUARTER, QUARTER)
        total = part[core, mine, :]
        for j in range(1, 4):
            total = total + buf[lax.rem(me + j, 4)]
        mid[...] = total

    def s2_copy(which, me, o):
        mid = (mid_a, mid_b)[which]
        buf = (in2a, in2b)[which]
        target = (at_y, at_x)[which]
        return copy(
            mid.at[pl.ds(o * SIXTEENTH, SIXTEENTH)], buf.at[me],
            s2_send.at[which, o], s2_recv.at[which, me], target(o),
        )

    def s2_start(which):
        me = (y, x)[which]
        loop3(me, lambda j, o: s2_copy(which, me, o).start())

    def s2_finish(which):
        me = (y, x)[which]
        mid = (mid_a, mid_b)[which]
        buf = (in2a, in2b)[which]

        def wait(j, o):
            s2_copy(which, me, o).wait_send()
            s2_copy(which, o, o).wait_recv()

        loop3(me, wait)
        total = mid[pl.ds(me * SIXTEENTH, SIXTEENTH), :]
        for j in range(1, 4):
            total = total + buf[lax.rem(me + j, 4)]
        mid2[which * SIXTEENTH : (which + 1) * SIXTEENTH, :] = total

    sums = collect(back_b, 16, high, high_of, bb_send, bb_recv)
    clip_sums[clip] = sums
    clip_copy = copy(
        clip_sums.at[clip], clip_sums.at[clip], clip_sem.at[0], clip_sem.at[1], (1 - clip, seq)
    )
    clip_copy.start()

    s1_finish(1)
    s2_start(1)
    s1_finish(0)
    s2_start(0)

    norm_sums = group_sum(sums * gain) * (1.0 / COUNT)
    m1 = norm_sums[0:1]
    m2 = norm_sums[1:2]

    def out_body(i, _):
        rows = pl.ds(i * COLS, COLS)
        xhat = (xv[rows, :].astype(F32) - mean) * rstd
        v = rstd * (pre_grad[rows, :] * gain - m1 - xhat * m2)
        grad_out[rows, :] = (cots[0, rows, :].astype(F32) + v).astype(BF16)
        return 0

    lax.fori_loop(0, ROWS_DEV, out_body, 0)

    s2_finish(1)
    s2_finish(0)

    def s3_copy(o, slot):
        return copy(
            mid2.at[pl.ds(SHARD * (o // 2), SHARD)], in3.at[slot],
            s3_send.at[o], s3_recv.at[slot], at_z(o),
        )

    def s3_start(j, _):
        s3_copy(lax.rem(z + j, 8), z).start()
        return 0

    def s3_wait(j, _):
        o = lax.rem(z + j, 8)
        s3_copy(o, z).wait_send()
        s3_copy(o, o).wait_recv()
        return 0

    lax.fori_loop(1, 8, s3_start, 0)
    in3[z] = mid2[pl.ds(SHARD * zh, SHARD), :]

    clip_copy.wait_send()
    copy(
        clip_sums.at[1 - clip], clip_sums.at[1 - clip], clip_sem.at[0], clip_sem.at[1],
        (1 - clip, seq),
    ).wait_recv()
    both = (clip_sums[0] + clip_sums[1]) * SCALE
    bias_out[...] = both[0:1]
    gain_out[...] = both[1:2]

    lax.fori_loop(1, 8, s3_wait, 0)
    total = in3[0]
    for o in range(1, 8):
        total = total + in3[o]

    def shard_at(o):
        second = o // 2
        first = 1 - second
        base = second * (PART + QUARTER * y + SIXTEENTH * x)
        base = base + first * (QUARTER * x + SIXTEENTH * y)
        return pl.multiple_of(base + SHARD * lax.rem(o, 2), SHARD)

    full[core, pl.ds(shard_at(zh), SHARD), :] = (total * SCALE).astype(BF16)

    def spread(where, me, target, send_sem, recv_sem, rows):
        def body(j, o):
            place_at = full.at[core, pl.ds(where(me), rows)]
            copy(place_at, place_at, send_sem.at[o], recv_sem.at[me], target(o)).start()

        loop3(me, body)

    def gather(where, me, target, send_sem, recv_sem, rows):
        def body(j, o):
            mine = full.at[core, pl.ds(where(me), rows)]
            theirs = full.at[core, pl.ds(where(o), rows)]
            copy(mine, mine, send_sem.at[o], recv_sem.at[me], target(o)).wait_send()
            copy(theirs, theirs, send_sem.at[o], recv_sem.at[o], target(o)).wait_recv()

        loop3(me, body)

    g3 = (shard_at, zh, at_zh, g3_send, g3_recv, SHARD)
    spread(*g3)
    gather(*g3)

    def sixteenth_a(o):
        return pl.multiple_of(QUARTER * x + SIXTEENTH * o, SIXTEENTH)

    def sixteenth_b(o):
        return pl.multiple_of(PART + QUARTER * y + SIXTEENTH * o, SIXTEENTH)

    def quarter_a(o):
        return pl.multiple_of(QUARTER * o, QUARTER)

    def quarter_b(o):
        return pl.multiple_of(PART + QUARTER * o, QUARTER)

    g2a = (sixteenth_a, y, at_y, g2_send.at[0], g2_recv.at[0], SIXTEENTH)
    g2b = (sixteenth_b, x, at_x, g2_send.at[1], g2_recv.at[1], SIXTEENTH)
    g1a = (quarter_a, x, at_x, g1_send.at[0], g1_recv.at[0], QUARTER)
    g1b = (quarter_b, y, at_y, g1_send.at[1], g1_recv.at[1], QUARTER)
    spread(*g2a)
    spread(*g2b)
    gather(*g2a)
    spread(*g1a)
    gather(*g2b)
    spread(*g1b)

    def to_core(i, half):
        rows = full.at[half, pl.ds(i * PART, PART)]
        return copy(rows, rows, gc_send.at[i], gc_recv.at[i], at(other_core))

    gather(*g1a)
    to_core(0, core).start()
    gather(*g1b)
    to_core(1, core).start()
    for i in range(2):
        to_core(i, core).wait_send()
        to_core(i, 1 - core).wait_recv()
    params_out[...] = full[...]

    for k in range(8):
        far_copy(k).wait_send()
        near_copy(k).wait_send()


def local(block_input, cotangent, group_norm_gain, group_norm_bias, w_spatial, w_temporal):
    any_space = pl.BlockSpec(memory_space=pl.ANY)
    vmem = pl.BlockSpec(memory_space=pltpu.VMEM)
    dma = pltpu.SemaphoreType.DMA
    scratch = [
        pltpu.VMEM((PIXELS, CHANNELS), BF16),
        pltpu.VMEM((3, PIXELS, CHANNELS), BF16),
        pltpu.VMEM((PADDED, 3 * CHANNELS), BF16),
        pltpu.VMEM((3, 3 * CHANNELS, PIXELS), BF16),
        pltpu.VMEM((PADDED, 3 * CHANNELS), BF16),
        pltpu.VMEM((PIXELS, CHANNELS), BF16),
        pltpu.VMEM((CHANNELS, PIXELS), BF16),
        pltpu.VMEM((9 * CHANNELS, CHANNELS), BF16),
        pltpu.VMEM((9 * CHANNELS, CHANNELS), BF16),
        pltpu.VMEM((3, CHANNELS, CHANNELS), BF16),
        pltpu.VMEM((3, CHANNELS, CHANNELS), BF16),
        pltpu.VMEM((PIXELS, CHANNELS), F32),
        pltpu.VMEM((2, COLS, CHANNELS), BF16),
        pltpu.VMEM((2, COLS, CHANNELS), BF16),
        pltpu.VMEM((8, 8, CHANNELS), F32),
        pltpu.VMEM((16, 8, CHANNELS), F32),
        pltpu.VMEM((8, 8, CHANNELS), F32),
        pltpu.VMEM((16, 8, CHANNELS), F32),
        pltpu.VMEM((2, 8, CHANNELS), F32),
        pltpu.VMEM((2, HALF_ROWS, 128), F32),
        pltpu.VMEM((HALF_ROWS, 128), F32),
        pltpu.VMEM((4, QUARTER, 128), F32),
        pltpu.VMEM((4, QUARTER, 128), F32),
        pltpu.VMEM((QUARTER, 128), F32),
        pltpu.VMEM((QUARTER, 128), F32),
        pltpu.VMEM((4, SIXTEENTH, 128), F32),
        pltpu.VMEM((4, SIXTEENTH, 128), F32),
        pltpu.VMEM((2 * SIXTEENTH, 128), F32),
        pltpu.VMEM((8, SHARD, 128), F32),
        pltpu.VMEM((2, HALF_ROWS, 128), BF16),
        dma((4,)),
        dma((8,)), dma((8,)), dma((8,)), dma((8,)),
        dma((2,)), dma((2,)), dma((2,)), dma((2,)),
        dma((8,)), dma((8,)), dma((16,)), dma((16,)),
        dma((8,)), dma((8,)), dma((16,)), dma((16,)),
        dma((2,)),
        dma((4,)), dma((4,)),
        dma((2, 4)), dma((2, 4)), dma((2, 4)), dma((2, 4)),
        dma((8,)), dma((8,)),
        dma((4,)), dma((4,)), dma((2, 4)), dma((2, 4)), dma((2, 4)), dma((2, 4)),
        dma((2,)), dma((2,)),
    ]
    grad, params, gain_grad, bias_grad = pl.pallas_call(
        kernel,
        out_shape=(
            jax.ShapeDtypeStruct((PIXELS, CHANNELS), BF16),
            jax.ShapeDtypeStruct((2, HALF_ROWS, 128), BF16),
            jax.ShapeDtypeStruct((1, CHANNELS), F32),
            jax.ShapeDtypeStruct((1, CHANNELS), F32),
        ),
        in_specs=[any_space, any_space, vmem, vmem, any_space, any_space],
        out_specs=(vmem, vmem, vmem, vmem),
        scratch_shapes=scratch,
        compiler_params=pltpu.CompilerParams(
            collective_id=0, has_side_effects=True, vmem_limit_bytes=56 * 2**20
        ),
    )(
        block_input.reshape(PIXELS, CHANNELS),
        cotangent.reshape(PIXELS, CHANNELS),
        group_norm_gain.reshape(1, CHANNELS),
        group_norm_bias.reshape(1, CHANNELS),
        w_spatial.reshape(9 * CHANNELS, CHANNELS),
        w_temporal,
    )
    params = params.reshape(2, TAPS, CHANNELS, 128).transpose(1, 2, 0, 3)
    params = params.reshape(TAPS, CHANNELS, CHANNELS).astype(F32)
    return (
        grad.reshape(1, ROWS_DEV, COLS, CHANNELS),
        params[:9],
        params[9:],
        gain_grad.reshape(CHANNELS),
        bias_grad.reshape(CHANNELS),
    )


def solution(mesh):
    return jax.shard_map(
        local,
        mesh=mesh,
        in_specs=(P("dp", "seq", None, None), P("dp", "seq", None, None), P(), P(), P(), P()),
        out_specs=(P("dp", "seq", None, None), P(), P(), P(), P()),
        check_vma=False,
    )
```

```python
import math

import jax
import jax.numpy as jnp
from jax import lax
from jax.experimental import pallas as pl
from jax.experimental.pallas import tpu as pltpu
from jax.sharding import PartitionSpec as P

F32 = jnp.float32
BF16 = jnp.bfloat16
MESH = pl.DeviceIdType.MESH

CHANNELS = 256
GROUP = 8
ROWS_DEV = 8
COLS = 160
PIXELS = ROWS_DEV * COLS
PADDED = PIXELS + 2 * COLS
SEQ = 128
FRAMES = 32
EPS = 1e-06
COUNT = FRAMES * 32 * COLS * GROUP
SCALE = 1.0 / math.sqrt(2 * FRAMES * 32 * COLS)

ORDER = (0, 7, 1, 2, 3, 4, 5, 6)
BLOCK = 2 * COLS

TAPS = 12
HALF_ROWS = TAPS * CHANNELS
PART = HALF_ROWS // 2
QUARTER = PART // 4
SIXTEENTH = PART // 16
SHARD = 2 * SIXTEENTH // 4


def kernel(
    x_hbm, g_hbm, gain_ref, bias_ref, wsp_hbm, wt_hbm,
    grad_out, params_out, gain_out, bias_out,
    xv, cots, act3, cg3, conv, convt, wsp, wspt, wt, wtt, pre_grad,
    act_halo, cg_halo, stat_a, stat_b, back_a, back_b, clip_sums,
    part, core_in, in1a, in1b, mid_a, mid_b, in2a, in2b, mid2, in3, full, grad_v,
    load_sem, far_send, far_recv, near_send, near_recv,
    ah_send, ah_recv, ch_send, ch_recv,
    sa_send, sa_recv, sb_send, sb_recv, ba_send, ba_recv, bb_send, bb_recv, clip_sem,
    core_send, core_recv, s1_send, s1_recv, s2_send, s2_recv, s3_send, s3_recv,
    g3_send, g3_recv, g2_send, g2_recv, g1_send, g1_recv, gc_send, gc_recv,
):
    clip = lax.axis_index("dp")
    seq = lax.axis_index("seq")
    core = lax.rem(seq, 2)
    x = lax.rem(seq // 2, 4)
    zh = lax.rem(seq // 8, 4)
    y = seq // 32
    low = lax.rem(seq, 8)
    high = seq // 8
    z = zh * 2 + clip
    slab = lax.rem(seq + 2, SEQ)
    place = lax.rem(slab, 4)
    frame = slab // 4

    def at(s):
        return (clip, s)

    def at_x(o):
        return (clip, seq + 2 * (o - x))

    def at_y(o):
        return (clip, seq + 32 * (o - y))

    def at_zh(o):
        return (clip, seq + 8 * (o - zh))

    def at_z(o):
        return (lax.rem(o, 2), seq + 8 * (o // 2 - zh))

    up = lax.rem(seq + 1, SEQ)
    down = lax.rem(seq + SEQ - 1, SEQ)
    far_to = lax.rem(seq + SEQ - 8, SEQ)
    far_from = lax.rem(seq + 8, SEQ)
    other_core = seq + 1 - 2 * core
    x_high = x // 2
    near_to = seq + 4 - 8 * x_high

    def copy(src, dst, send_sem, recv_sem, device):
        return pltpu.make_async_remote_copy(
            src_ref=src, dst_ref=dst, send_sem=send_sem, recv_sem=recv_sem,
            device_id=device, device_id_type=MESH,
        )

    load_x = pltpu.make_async_copy(x_hbm, xv, load_sem.at[0])
    load_g = pltpu.make_async_copy(g_hbm, cots.at[0], load_sem.at[1])
    load_wsp = pltpu.make_async_copy(wsp_hbm, wsp, load_sem.at[2])
    load_wt = pltpu.make_async_copy(wt_hbm, wt, load_sem.at[3])
    load_x.start()
    load_g.start()
    load_wsp.start()
    load_wt.start()

    barrier = pltpu.get_barrier_semaphore()

    def greet(device):
        pl.semaphore_signal(barrier, inc=1, device_id=device, device_id_type=MESH)

    def greet_low(j, _):
        greet(at(seq - low + lax.rem(low + j, 8)))
        return 0

    def greet_high(j, _):
        greet(at(lax.rem(high + j, 16) * 8 + low))
        return 0

    def greet_z(j, _):
        greet((1 - clip, seq + 8 * (j - zh)))
        return 0

    lax.fori_loop(1, 8, greet_low, 0)
    lax.fori_loop(1, 16, greet_high, 0)
    lax.fori_loop(0, 4, greet_z, 0)
    greet(at(up))
    greet(at(down))
    pl.semaphore_wait(barrier, 7 + 15 + 4 + 2)

    def far_copy(k):
        rows = pl.ds(ORDER[k] * COLS, COLS)
        return copy(
            g_hbm.at[rows], cots.at[2, rows], far_send.at[k], far_recv.at[k], at(far_to)
        )

    def near_copy(k, own):
        rows = pl.ds(ORDER[k] * COLS, COLS)
        return copy(
            (g_hbm if own else cots.at[2]).at[rows], cots.at[1, rows],
            near_send.at[k], near_recv.at[k], at(near_to),
        )

    for k in range(8):
        far_copy(k).start()

    @pl.when(x_high == 1)
    def send_own():
        for k in range(8):
            near_copy(k, True).start()

    def exchange(buf, n, me, target, send_sem, recv_sem):
        def body(j, _):
            o = lax.rem(me + j, n)
            copy(buf.at[me], buf.at[me], send_sem.at[o], recv_sem.at[me], at(target(o))).start()
            return 0

        lax.fori_loop(1, n, body, 0)

    def collect(buf, n, me, target, send_sem, recv_sem):
        def body(j, _):
            o = lax.rem(me + j, n)
            arrived = copy(buf.at[o], buf.at[o], send_sem.at[o], recv_sem.at[o], at(target(o)))
            arrived.wait_recv()
            return 0

        lax.fori_loop(1, n, body, 0)
        total = buf[0]
        for o in range(1, n):
            total = total + buf[o]
        return total

    def drain(buf, n, me, target, send_sem, recv_sem):
        def body(j, _):
            o = lax.rem(me + j, n)
            copy(buf.at[me], buf.at[me], send_sem.at[o], recv_sem.at[me], at(target(o))).wait_send()
            return 0

        lax.fori_loop(1, n, body, 0)

    def low_of(o):
        return seq - low + o

    def high_of(o):
        return o * 8 + low

    row_id = lax.broadcasted_iota(jnp.int32, (8, CHANNELS), 0)

    def pack_rows(first, second):
        return jnp.where(row_id == 0, first, jnp.where(row_id == 1, second, 0.0))

    group_a = lax.shift_right_logical(lax.broadcasted_iota(jnp.int32, (CHANNELS, CHANNELS), 0), 3)
    group_b = lax.shift_right_logical(lax.broadcasted_iota(jnp.int32, (CHANNELS, CHANNELS), 1), 3)
    same_group = jnp.where(group_a == group_b, 1.0, 0.0).astype(BF16)

    def group_sum(v):
        total = jnp.zeros_like(v)
        rest = v
        for _ in range(3):
            piece = rest.astype(BF16)
            rest = rest - piece.astype(F32)
            total = total + jnp.dot(piece, same_group, preferred_element_type=F32)
        return total

    load_x.wait()

    def stat_body(i, carry):
        a, b = carry
        blk = xv[pl.ds(i * COLS, COLS), :].astype(F32).reshape(COLS // 8, 8, CHANNELS)
        return a + jnp.sum(blk, axis=0), b + jnp.sum(blk * blk, axis=0)

    zero8 = jnp.zeros((8, CHANNELS), F32)
    a, b = lax.fori_loop(0, ROWS_DEV, stat_body, (zero8, zero8))
    stat_a[low] = pack_rows(jnp.sum(a, axis=0, keepdims=True), jnp.sum(b, axis=0, keepdims=True))
    exchange(stat_a, 8, low, low_of, sa_send, sa_recv)

    load_wt.wait()
    load_wsp.wait()
    for k in range(3):
        wtt[k] = wt[k].T

    def turn_weight(i, _):
        wspt[pl.ds(i * CHANNELS, CHANNELS), :] = wsp[pl.ds((8 - i) * CHANNELS, CHANNELS), :].T
        return 0

    lax.fori_loop(0, 9, turn_weight, 0)

    stat_b[high] = collect(stat_a, 8, low, low_of, sa_send, sa_recv)
    exchange(stat_b, 16, high, high_of, sb_send, sb_recv)
    load_g.wait()
    moments = group_sum(collect(stat_b, 16, high, high_of, sb_send, sb_recv)) * (1.0 / COUNT)
    mean = moments[0:1]
    rstd = lax.rsqrt(moments[1:2] - mean * mean + EPS)
    gain = gain_ref[...]
    bias = bias_ref[...]

    def forward(k):
        far_copy(k).wait_recv()

        @pl.when(x_high == 0)
        def pass_on():
            near_copy(k, False).start()


    col_id = lax.broadcasted_iota(jnp.int32, (COLS, CHANNELS), 0)

    def store_shifts(buf, padded_row, v):
        rows = pl.ds(padded_row * COLS, COLS)
        buf[rows, CHANNELS : 2 * CHANNELS] = v.astype(BF16)
        left = jnp.where(col_id == 0, 0.0, pltpu.roll(v, 1, 0))
        right = jnp.where(col_id == COLS - 1, 0.0, pltpu.roll(v, COLS - 1, 0))
        buf[rows, 0:CHANNELS] = left.astype(BF16)
        buf[rows, 2 * CHANNELS : 3 * CHANNELS] = right.astype(BF16)

    def normalize(rows):
        xhat = (xv[rows, :].astype(F32) - mean) * rstd
        pre = xhat * gain + bias
        return xhat, pre, jax.nn.sigmoid(pre)

    def act_row(r):
        _, pre, sigma = normalize(pl.ds(r * COLS, COLS))
        store_shifts(act3, r + 1, pre * sigma)

    middle = slice(CHANNELS, 2 * CHANNELS)

    def halo_copies(buf, halo, send_sem, recv_sem):
        first = copy(
            buf.at[pl.ds(COLS, COLS), middle], halo.at[1], send_sem.at[0], recv_sem.at[1], at(down)
        )
        last = copy(
            buf.at[pl.ds(PIXELS, COLS), middle], halo.at[0], send_sem.at[1], recv_sem.at[0], at(up)
        )
        return first, last

    def send_halo(buf, halo, send_sem, recv_sem):
        for c in halo_copies(buf, halo, send_sem, recv_sem):
            c.start()

    def take_halo(buf, halo, send_sem, recv_sem):
        for c in halo_copies(buf, halo, send_sem, recv_sem):
            c.wait_recv()
        keep_low = jnp.where(place > 0, 1.0, 0.0).astype(F32)
        keep_high = jnp.where(place < 3, 1.0, 0.0).astype(F32)
        store_shifts(buf, 0, halo[0].astype(F32) * keep_low)
        store_shifts(buf, ROWS_DEV + 1, halo[1].astype(F32) * keep_high)

    act_row(0)
    act_row(ROWS_DEV - 1)
    send_halo(act3, act_halo, ah_send, ah_recv)

    def act_body(r, _):
        act_row(r)
        return 0

    lax.fori_loop(1, ROWS_DEV - 1, act_body, 0)
    forward(0)
    take_halo(act3, act_halo, ah_send, ah_recv)
    forward(1)

    def convolve(buf, weights, i):
        total = None
        for dy in range(3):
            term = jnp.dot(
                buf[pl.ds(i * BLOCK + dy * COLS, BLOCK), :],
                weights[dy * 3 * CHANNELS : (dy + 1) * 3 * CHANNELS, :],
                preferred_element_type=F32,
            )
            total = term if total is None else total + term
        return total

    def conv_body(i, _):
        conv[pl.ds(i * BLOCK, BLOCK), :] = convolve(act3, wsp, i).astype(BF16)
        return 0

    lax.fori_loop(0, PIXELS // BLOCK, conv_body, 0)
    forward(2)

    def turn_conv(i, _):
        src = pl.ds(pl.multiple_of(i * 128, 128), 128)
        convt[:, src] = conv[src, :].T
        return 0

    lax.fori_loop(0, PIXELS // 128, turn_conv, 0)

    keep1 = jnp.where(frame < FRAMES - 1, 1.0, 0.0).astype(F32)
    keep2 = jnp.where(frame < FRAMES - 2, 1.0, 0.0).astype(F32)

    def cg_row(k):
        r = ORDER[k]
        near_copy(k, True).wait_recv()
        rows = pl.ds(r * COLS, COLS)
        total = jnp.dot(cots[0, rows, :], wtt[0], preferred_element_type=F32)
        total = total + keep1 * jnp.dot(cots[1, rows, :], wtt[1], preferred_element_type=F32)
        total = total + keep2 * jnp.dot(cots[2, rows, :], wtt[2], preferred_element_type=F32)
        store_shifts(cg3, r + 1, total.astype(BF16).astype(F32))

    def put(first_row, v, add):
        rows = pl.ds(first_row, v.shape[0])
        for half in range(2):
            w = v[:, half * 128 : (half + 1) * 128]
            part[half, rows, :] = part[half, rows, :] + w if add else w

    half_pixels = PIXELS // 2

    def temporal_half(h):
        pixels = slice(h * half_pixels, (h + 1) * half_pixels)
        for k, keep in enumerate((None, keep1, keep2)):
            v = jnp.dot(convt[:, pixels], cots[k, pixels, :], preferred_element_type=F32)
            put((9 + k) * CHANNELS, v if keep is None else v * keep, h > 0)

    def spatial_half(h, dy):
        begin = h * half_pixels
        v = lax.dot_general(
            act3[dy * COLS + begin : dy * COLS + begin + half_pixels, :],
            cg3[COLS + begin : COLS + begin + half_pixels, middle],
            (((0,), (0,)), ((), ())),
            preferred_element_type=F32,
        )
        put(dy * chunk_rows, v, h > 0)

    chunk_rows = 3 * CHANNELS

    def core_copy(i):
        rows = pl.ds(i * chunk_rows, chunk_rows)
        return copy(
            part.at[1 - core, rows], core_in.at[rows], core_send.at[i], core_recv.at[i],
            at(other_core),
        )

    forward(3)
    cg_row(0)
    cg_row(1)
    send_halo(cg3, cg_halo, ch_send, ch_recv)
    forward(4)
    cg_row(2)
    forward(5)
    cg_row(3)
    forward(6)
    cg_row(4)
    temporal_half(0)
    forward(7)
    for dy in range(3):
        spatial_half(0, dy)
    cg_row(5)
    take_halo(cg3, cg_halo, ch_send, ch_recv)
    cg_row(6)
    cg_row(7)
    temporal_half(1)
    core_copy(3).start()
    for dy in (0, 1, 2):
        spatial_half(1, dy)
        core_copy(dy).start()

    def back_block(i, carry):
        rows = pl.ds(i * BLOCK, BLOCK)
        xhat, pre, sigma = normalize(rows)
        v = convolve(cg3, wspt, i) * sigma * (1.0 + pre * (1.0 - sigma))
        pre_grad[rows, :] = v
        a, b = carry
        a = a + jnp.sum(v.reshape(BLOCK // 8, 8, CHANNELS), axis=0)
        b = b + jnp.sum((v * xhat).reshape(BLOCK // 8, 8, CHANNELS), axis=0)
        return a, b

    def s1_copy(which, me, o, peer):
        buf = (in1a, in1b)[which]
        target = (at_x, at_y)[which]
        return copy(
            part.at[core, pl.ds(which * PART + o * QUARTER, QUARTER)], buf.at[me],
            s1_send.at[which, o], s1_recv.at[which, me], target(peer),
        )

    def add_core(i):
        core_copy(i).wait_recv()
        rows = pl.ds(i * chunk_rows, chunk_rows)
        part[core, rows, :] = part[core, rows, :] + core_in[rows, :]
        which = i // 2
        me = (x, y)[which]
        for o in (2 * (i % 2), 2 * (i % 2) + 1):
            @pl.when(me != o)
            def send_slice():
                s1_copy(which, me, o, o).start()

    sums = (zero8, zero8)
    for i, chunk in enumerate((3, 0, 1, 2)):
        sums = back_block(i, sums)
        add_core(chunk)
    a, b = sums
    back_a[low] = pack_rows(jnp.sum(a, axis=0, keepdims=True), jnp.sum(b, axis=0, keepdims=True))
    exchange(back_a, 8, low, low_of, ba_send, ba_recv)

    def loop3(me, body):
        def step(j, _):
            body(j, lax.rem(me + j, 4))
            return 0

        lax.fori_loop(1, 4, step, 0)

    back_b[high] = collect(back_a, 8, low, low_of, ba_send, ba_recv)
    exchange(back_b, 16, high, high_of, bb_send, bb_recv)

    def s1_finish(which):
        me = (x, y)[which]
        buf = (in1a, in1b)[which]
        mid = (mid_a, mid_b)[which]

        def wait(j, o):
            s1_copy(which, o, o, o).wait_recv()

        loop3(me, wait)
        mine = pl.ds(which * PART + me * QUARTER, QUARTER)
        total = part[core, mine, :]
        for j in range(1, 4):
            total = total + buf[lax.rem(me + j, 4)]
        mid[...] = total

    def s2_copy(which, me, o):
        mid = (mid_a, mid_b)[which]
        buf = (in2a, in2b)[which]
        target = (at_y, at_x)[which]
        return copy(
            mid.at[pl.ds(o * SIXTEENTH, SIXTEENTH)], buf.at[me],
            s2_send.at[which, o], s2_recv.at[which, me], target(o),
        )

    def s2_start(which):
        me = (y, x)[which]
        loop3(me, lambda j, o: s2_copy(which, me, o).start())

    def s2_finish(which):
        me = (y, x)[which]
        mid = (mid_a, mid_b)[which]
        buf = (in2a, in2b)[which]

        def wait(j, o):
            s2_copy(which, o, o).wait_recv()

        loop3(me, wait)
        total = mid[pl.ds(me * SIXTEENTH, SIXTEENTH), :]
        for j in range(1, 4):
            total = total + buf[lax.rem(me + j, 4)]
        mid2[which * SIXTEENTH : (which + 1) * SIXTEENTH, :] = total

    s1_finish(1)
    s2_start(1)
    s1_finish(0)
    s2_start(0)

    sums = collect(back_b, 16, high, high_of, bb_send, bb_recv)
    clip_sums[clip] = sums
    clip_copy = copy(
        clip_sums.at[clip], clip_sums.at[clip], clip_sem.at[0], clip_sem.at[1], (1 - clip, seq)
    )
    clip_copy.start()
    norm_sums = group_sum(sums * gain) * (1.0 / COUNT)
    m1 = norm_sums[0:1]
    m2 = norm_sums[1:2]

    def out_body(i, _):
        rows = pl.ds(i * COLS, COLS)
        xhat = (xv[rows, :].astype(F32) - mean) * rstd
        v = rstd * (pre_grad[rows, :] * gain - m1 - xhat * m2)
        grad_v[rows, :] = (cots[0, rows, :].astype(F32) + v).astype(BF16)
        return 0

    lax.fori_loop(0, ROWS_DEV, out_body, 0)
    store_grad = pltpu.make_async_copy(grad_v, grad_out, load_sem.at[4])
    store_grad.start()

    def s3_copy(o, slot):
        return copy(
            mid2.at[pl.ds(SHARD * (o // 2), SHARD)], in3.at[slot],
            s3_send.at[o], s3_recv.at[slot], at_z(o),
        )

    def s3_start(which):
        def body(j, _):
            o = 4 * which + j

            @pl.when(o != z)
            def send_shard():
                s3_copy(o, z).start()

            return 0

        lax.fori_loop(0, 4, body, 0)

    def s3_wait(j, _):
        o = lax.rem(z + j, 8)
        s3_copy(o, o).wait_recv()
        return 0

    s2_finish(1)
    s3_start(1)
    s2_finish(0)
    s3_start(0)
    in3[z] = mid2[pl.ds(SHARD * zh, SHARD), :]

    copy(
        clip_sums.at[1 - clip], clip_sums.at[1 - clip], clip_sem.at[0], clip_sem.at[1],
        (1 - clip, seq),
    ).wait_recv()
    both = (clip_sums[0] + clip_sums[1]) * SCALE
    bias_out[...] = both[0:1]
    gain_out[...] = both[1:2]

    lax.fori_loop(1, 8, s3_wait, 0)
    total = in3[0]
    for o in range(1, 8):
        total = total + in3[o]

    def shard_at(o):
        second = o // 2
        first = 1 - second
        base = second * (PART + QUARTER * y + SIXTEENTH * x)
        base = base + first * (QUARTER * x + SIXTEENTH * y)
        return pl.multiple_of(base + SHARD * lax.rem(o, 2), SHARD)

    full[core, pl.ds(shard_at(zh), SHARD), :] = (total * SCALE).astype(BF16)

    def spread(where, me, target, send_sem, recv_sem, rows):
        def body(j, o):
            place_at = full.at[core, pl.ds(where(me), rows)]
            copy(place_at, place_at, send_sem.at[o], recv_sem.at[me], target(o)).start()

        loop3(me, body)

    def gather(where, me, target, send_sem, recv_sem, rows):
        def body(j, o):
            theirs = full.at[core, pl.ds(where(o), rows)]
            copy(theirs, theirs, send_sem.at[o], recv_sem.at[o], target(o)).wait_recv()

        loop3(me, body)

    g3 = (shard_at, zh, at_zh, g3_send, g3_recv, SHARD)
    spread(*g3)
    gather(*g3)

    def sixteenth_a(o):
        return pl.multiple_of(QUARTER * x + SIXTEENTH * o, SIXTEENTH)

    def sixteenth_b(o):
        return pl.multiple_of(PART + QUARTER * y + SIXTEENTH * o, SIXTEENTH)

    def quarter_a(o):
        return pl.multiple_of(QUARTER * o, QUARTER)

    def quarter_b(o):
        return pl.multiple_of(PART + QUARTER * o, QUARTER)

    g2a = (sixteenth_a, y, at_y, g2_send.at[0], g2_recv.at[0], SIXTEENTH)
    g2b = (sixteenth_b, x, at_x, g2_send.at[1], g2_recv.at[1], SIXTEENTH)
    g1a = (quarter_a, x, at_x, g1_send.at[0], g1_recv.at[0], QUARTER)
    g1b = (quarter_b, y, at_y, g1_send.at[1], g1_recv.at[1], QUARTER)
    spread(*g2a)
    spread(*g2b)
    gather(*g2a)
    spread(*g1a)
    gather(*g2b)
    spread(*g1b)

    def to_core(i, half):
        rows = full.at[half, pl.ds(i * PART, PART)]
        return copy(rows, rows, gc_send.at[i], gc_recv.at[i], at(other_core))

    def settle(where, me, target, send_sem, recv_sem, rows):
        def body(j, o):
            mine = full.at[core, pl.ds(where(me), rows)]
            copy(mine, mine, send_sem.at[o], recv_sem.at[me], target(o)).wait_send()

        loop3(me, body)

    def store_params(i, half, slot):
        rows = pl.ds(i * PART, PART)
        return pltpu.make_async_copy(
            full.at[half, rows], params_out.at[half, rows], load_sem.at[5 + slot]
        )

    gather(*g1a)
    to_core(0, core).start()
    gather(*g1b)
    to_core(1, core).start()
    store_mine = pltpu.make_async_copy(full.at[core], params_out.at[core], load_sem.at[5])
    store_mine.start()

    for k in range(8):
        far_copy(k).wait_send()
        near_copy(k, True).wait_send()
    for args in ((act3, act_halo, ah_send, ah_recv), (cg3, cg_halo, ch_send, ch_recv)):
        for c in halo_copies(*args):
            c.wait_send()
    drain(stat_a, 8, low, low_of, sa_send, sa_recv)
    drain(stat_b, 16, high, high_of, sb_send, sb_recv)
    drain(back_a, 8, low, low_of, ba_send, ba_recv)
    drain(back_b, 16, high, high_of, bb_send, bb_recv)
    clip_copy.wait_send()
    for i in range(4):
        core_copy(i).wait_send()
    for which in range(2):
        loop3((x, y)[which], lambda j, o: s1_copy(which, (x, y)[which], o, o).wait_send())
        loop3((y, x)[which], lambda j, o: s2_copy(which, (y, x)[which], o).wait_send())

    def s3_sent(j, _):
        s3_copy(lax.rem(z + j, 8), z).wait_send()
        return 0

    lax.fori_loop(1, 8, s3_sent, 0)
    for args in (g3, g2a, g2b, g1a, g1b):
        settle(*args)

    for i in range(2):
        to_core(i, 1 - core).wait_recv()
        store_params(i, 1 - core, 1 + i).start()
    for i in range(2):
        to_core(i, core).wait_send()
    store_grad.wait()
    store_mine.wait()
    for i in range(2):
        store_params(i, 1 - core, 1 + i).wait()


def finish_kernel(grad, params, gain, bias, grad_out, spatial, temporal, gain_out, bias_out):
    step = pl.program_id(0)
    grad_out[...] = grad[...]

    @pl.when(step < 3)
    def put_spatial():
        for half in range(2):
            spatial[:, :, half * 128 : (half + 1) * 128] = params[half].astype(F32)

    @pl.when(step == 3)
    def put_temporal():
        for half in range(2):
            temporal[:, :, half * 128 : (half + 1) * 128] = params[half].astype(F32)
        gain_out[...] = gain[0]
        bias_out[...] = bias[0]


def local(block_input, cotangent, group_norm_gain, group_norm_bias, w_spatial, w_temporal):
    any_space = pl.BlockSpec(memory_space=pl.ANY)
    vmem = pl.BlockSpec(memory_space=pltpu.VMEM)
    dma = pltpu.SemaphoreType.DMA
    scratch = [
        pltpu.VMEM((PIXELS, CHANNELS), BF16),
        pltpu.VMEM((3, PIXELS, CHANNELS), BF16),
        pltpu.VMEM((PADDED, 3 * CHANNELS), BF16),
        pltpu.VMEM((PADDED, 3 * CHANNELS), BF16),
        pltpu.VMEM((PIXELS, CHANNELS), BF16),
        pltpu.VMEM((CHANNELS, PIXELS), BF16),
        pltpu.VMEM((9 * CHANNELS, CHANNELS), BF16),
        pltpu.VMEM((9 * CHANNELS, CHANNELS), BF16),
        pltpu.VMEM((3, CHANNELS, CHANNELS), BF16),
        pltpu.VMEM((3, CHANNELS, CHANNELS), BF16),
        pltpu.VMEM((PIXELS, CHANNELS), F32),
        pltpu.VMEM((2, COLS, CHANNELS), BF16),
        pltpu.VMEM((2, COLS, CHANNELS), BF16),
        pltpu.VMEM((8, 8, CHANNELS), F32),
        pltpu.VMEM((16, 8, CHANNELS), F32),
        pltpu.VMEM((8, 8, CHANNELS), F32),
        pltpu.VMEM((16, 8, CHANNELS), F32),
        pltpu.VMEM((2, 8, CHANNELS), F32),
        pltpu.VMEM((2, HALF_ROWS, 128), F32),
        pltpu.VMEM((HALF_ROWS, 128), F32),
        pltpu.VMEM((4, QUARTER, 128), F32),
        pltpu.VMEM((4, QUARTER, 128), F32),
        pltpu.VMEM((QUARTER, 128), F32),
        pltpu.VMEM((QUARTER, 128), F32),
        pltpu.VMEM((4, SIXTEENTH, 128), F32),
        pltpu.VMEM((4, SIXTEENTH, 128), F32),
        pltpu.VMEM((2 * SIXTEENTH, 128), F32),
        pltpu.VMEM((8, SHARD, 128), F32),
        pltpu.VMEM((2, HALF_ROWS, 128), BF16),
        pltpu.VMEM((PIXELS, CHANNELS), BF16),
        dma((8,)),
        dma((8,)), dma((8,)), dma((8,)), dma((8,)),
        dma((2,)), dma((2,)), dma((2,)), dma((2,)),
        dma((8,)), dma((8,)), dma((16,)), dma((16,)),
        dma((8,)), dma((8,)), dma((16,)), dma((16,)),
        dma((2,)),
        dma((4,)), dma((4,)),
        dma((2, 4)), dma((2, 4)), dma((2, 4)), dma((2, 4)),
        dma((8,)), dma((8,)),
        dma((4,)), dma((4,)), dma((2, 4)), dma((2, 4)), dma((2, 4)), dma((2, 4)),
        dma((2,)), dma((2,)),
    ]
    grad, params, gain_grad, bias_grad = pl.pallas_call(
        kernel,
        out_shape=(
            jax.ShapeDtypeStruct((PIXELS, CHANNELS), BF16),
            jax.ShapeDtypeStruct((2, HALF_ROWS, 128), BF16),
            jax.ShapeDtypeStruct((1, CHANNELS), F32),
            jax.ShapeDtypeStruct((1, CHANNELS), F32),
        ),
        in_specs=[any_space, any_space, vmem, vmem, any_space, any_space],
        out_specs=(any_space, any_space, vmem, vmem),
        scratch_shapes=scratch,
        compiler_params=pltpu.CompilerParams(
            collective_id=0, has_side_effects=True, vmem_limit_bytes=56 * 2**20
        ),
    )(
        block_input.reshape(PIXELS, CHANNELS),
        cotangent.reshape(PIXELS, CHANNELS),
        group_norm_gain.reshape(1, CHANNELS),
        group_norm_bias.reshape(1, CHANNELS),
        w_spatial.reshape(9 * CHANNELS, CHANNELS),
        w_temporal,
    )
    params = params.reshape(2, TAPS, CHANNELS, 128)
    whole = pl.BlockSpec((1, CHANNELS), lambda i: (0, 0))
    line = pl.BlockSpec((CHANNELS,), lambda i: (0,))
    block = pl.BlockSpec((BLOCK, CHANNELS), lambda i: (i, 0))
    grad, spatial, temporal, gain_grad, bias_grad = pl.pallas_call(
        finish_kernel,
        grid=(4,),
        out_shape=(
            jax.ShapeDtypeStruct((PIXELS, CHANNELS), BF16),
            jax.ShapeDtypeStruct((9, CHANNELS, CHANNELS), F32),
            jax.ShapeDtypeStruct((3, CHANNELS, CHANNELS), F32),
            jax.ShapeDtypeStruct((CHANNELS,), F32),
            jax.ShapeDtypeStruct((CHANNELS,), F32),
        ),
        in_specs=[
            block,
            pl.BlockSpec((2, 3, CHANNELS, 128), lambda i: (0, i, 0, 0)),
            whole,
            whole,
        ],
        out_specs=(
            block,
            pl.BlockSpec((3, CHANNELS, CHANNELS), lambda i: (jnp.minimum(i, 2), 0, 0)),
            pl.BlockSpec((3, CHANNELS, CHANNELS), lambda i: (0, 0, 0)),
            line,
            line,
        ),
        compiler_params=pltpu.CompilerParams(vmem_limit_bytes=32 * 2**20),
    )(grad, params, gain_grad, bias_grad)
    return (
        grad.reshape(1, ROWS_DEV, COLS, CHANNELS),
        spatial,
        temporal,
        gain_grad,
        bias_grad,
    )


def solution(mesh):
    return jax.shard_map(
        local,
        mesh=mesh,
        in_specs=(P("dp", "seq", None, None), P("dp", "seq", None, None), P(), P(), P(), P()),
        out_specs=(P("dp", "seq", None, None), P(), P(), P(), P()),
        check_vma=False,
    )
```

```python
import math

import jax
import jax.numpy as jnp
from jax import lax
from jax.experimental import pallas as pl
from jax.experimental.pallas import tpu as pltpu
from jax.sharding import PartitionSpec as P

F32 = jnp.float32
BF16 = jnp.bfloat16
MESH = pl.DeviceIdType.MESH

CHANNELS = 256
GROUP = 8
ROWS_DEV = 8
COLS = 160
PIXELS = ROWS_DEV * COLS
PADDED = PIXELS + 2 * COLS
SEQ = 128
FRAMES = 32
EPS = 1e-06
COUNT = FRAMES * 32 * COLS * GROUP
SCALE = 1.0 / math.sqrt(2 * FRAMES * 32 * COLS)

ORDER = (0, 7, 1, 2, 3, 4, 5, 6)
BLOCK = 2 * COLS

TAPS = 12
HALF_ROWS = TAPS * CHANNELS
PART = HALF_ROWS // 2
QUARTER = PART // 4
SIXTEENTH = PART // 16
SHARD = 2 * SIXTEENTH // 4


def kernel(
    x_hbm, g_hbm, gain_ref, bias_ref, wsp_hbm, wt_hbm,
    grad_out, params_out, gain_out, bias_out,
    xv, cots, act3, cg3, conv, convt, wsp, wspt, wt, wtt, pre_grad,
    act_halo, cg_halo, stat_a, stat_b, back_a, back_b, clip_sums,
    part, core_in, in1a, in1b, mid_a, mid_b, in2a, in2b, mid2, in3, full, grad_v, passing,
    load_sem, far_send, far_recv, near_send, near_recv, leg_send, leg_recv,
    ah_send, ah_recv, ch_send, ch_recv,
    sa_send, sa_recv, sb_send, sb_recv, ba_send, ba_recv, bb_send, bb_recv, clip_sem,
    core_send, core_recv, s1_send, s1_recv, s2_send, s2_recv, s3_send, s3_recv,
    g3_send, g3_recv, g2_send, g2_recv, g1_send, g1_recv, gc_send, gc_recv,
):
    clip = lax.axis_index("dp")
    seq = lax.axis_index("seq")
    core = lax.rem(seq, 2)
    x = lax.rem(seq // 2, 4)
    zh = lax.rem(seq // 8, 4)
    y = seq // 32
    low = lax.rem(seq, 8)
    high = seq // 8
    z = zh * 2 + clip
    slab = lax.rem(seq + 2, SEQ)
    place = lax.rem(slab, 4)
    frame = slab // 4

    def at(s):
        return (clip, s)

    def at_x(o):
        return (clip, seq + 2 * (o - x))

    def at_y(o):
        return (clip, seq + 32 * (o - y))

    def at_zh(o):
        return (clip, seq + 8 * (o - zh))

    def at_z(o):
        return (lax.rem(o, 2), seq + 8 * (o // 2 - zh))

    up = lax.rem(seq + 1, SEQ)
    down = lax.rem(seq + SEQ - 1, SEQ)
    far_to = lax.rem(seq + SEQ - 8, SEQ)
    far_from = lax.rem(seq + 8, SEQ)
    other_core = seq + 1 - 2 * core
    x_high = x // 2
    near_to = seq + 4 - 8 * x_high

    def copy(src, dst, send_sem, recv_sem, device):
        return pltpu.make_async_remote_copy(
            src_ref=src, dst_ref=dst, send_sem=send_sem, recv_sem=recv_sem,
            device_id=device, device_id_type=MESH,
        )

    load_x = pltpu.make_async_copy(x_hbm, xv, load_sem.at[0])
    load_g = pltpu.make_async_copy(g_hbm, cots.at[0], load_sem.at[1])
    load_wsp = pltpu.make_async_copy(wsp_hbm, wsp, load_sem.at[2])
    load_wt = pltpu.make_async_copy(wt_hbm, wt, load_sem.at[3])
    load_x.start()
    load_g.start()
    load_wsp.start()
    load_wt.start()

    barrier = pltpu.get_barrier_semaphore()

    def greet(device):
        pl.semaphore_signal(barrier, inc=1, device_id=device, device_id_type=MESH)

    def greet_low(j, _):
        greet(at(seq - low + lax.rem(low + j, 8)))
        return 0

    def greet_high(j, _):
        greet(at(lax.rem(high + j, 16) * 8 + low))
        return 0

    def greet_z(j, _):
        greet((1 - clip, seq + 8 * (j - zh)))
        return 0

    z_up = lax.rem(z + 3, 8)
    z_down = lax.rem(z + 5, 8)

    def wrapped(source_z):
        return 1 - jnp.minimum(source_z // 2, 1)

    def at_zy(zz, yy):
        return (lax.rem(zz, 2), seq + 8 * (zz // 2 - zh) + 32 * (yy - y))

    leg1_to = at_zy(z_up, y)
    leg2_to = at_zy(z_up, lax.rem(y + 4 - wrapped(z_down), 4))
    leg2_from = at_zy(z_down, lax.rem(y + wrapped(lax.rem(z + 2, 8)), 4))

    lax.fori_loop(1, 16, greet_high, 0)
    lax.fori_loop(0, 4, greet_z, 0)
    greet(leg2_from)
    greet(at(up))
    greet(at(down))
    lax.fori_loop(1, 8, greet_low, 0)

    def far_copy(k):
        rows = pl.ds(ORDER[k] * COLS, COLS)
        return copy(
            g_hbm.at[rows], cots.at[2, rows], far_send.at[k], far_recv.at[k], at(far_to)
        )

    def near_copy(k, own):
        rows = pl.ds(ORDER[k] * COLS, COLS)
        return copy(
            (g_hbm if own else cots.at[2]).at[rows], cots.at[1, rows],
            near_send.at[k], near_recv.at[k], at(near_to),
        )

    detour_rows = pl.ds(ORDER[7] * COLS, COLS)

    def leg1_copy():
        return copy(g_hbm.at[detour_rows], passing, leg_send.at[0], leg_recv, leg1_to)

    def leg2_copy():
        return copy(passing, cots.at[2, detour_rows], leg_send.at[1], far_recv.at[7], leg2_to)

    def exchange(buf, n, me, target, send_sem, recv_sem):
        def body(j, _):
            o = lax.rem(me + j, n)
            copy(buf.at[me], buf.at[me], send_sem.at[o], recv_sem.at[me], at(target(o))).start()
            return 0

        lax.fori_loop(1, n, body, 0)

    def collect(buf, n, me, target, send_sem, recv_sem):
        def body(j, _):
            o = lax.rem(me + j, n)
            arrived = copy(buf.at[o], buf.at[o], send_sem.at[o], recv_sem.at[o], at(target(o)))
            arrived.wait_recv()
            return 0

        lax.fori_loop(1, n, body, 0)
        total = buf[0]
        for o in range(1, n):
            total = total + buf[o]
        return total

    def drain(buf, n, me, target, send_sem, recv_sem):
        def body(j, _):
            o = lax.rem(me + j, n)
            copy(buf.at[me], buf.at[me], send_sem.at[o], recv_sem.at[me], at(target(o))).wait_send()
            return 0

        lax.fori_loop(1, n, body, 0)

    def low_of(o):
        return seq - low + o

    def high_of(o):
        return o * 8 + low

    row_id = lax.broadcasted_iota(jnp.int32, (8, CHANNELS), 0)

    def pack_rows(first, second):
        return jnp.where(row_id == 0, first, jnp.where(row_id == 1, second, 0.0))

    group_a = lax.shift_right_logical(lax.broadcasted_iota(jnp.int32, (CHANNELS, CHANNELS), 0), 3)
    group_b = lax.shift_right_logical(lax.broadcasted_iota(jnp.int32, (CHANNELS, CHANNELS), 1), 3)
    same_group = jnp.where(group_a == group_b, 1.0, 0.0).astype(BF16)

    def group_sum(v):
        total = jnp.zeros_like(v)
        rest = v
        for _ in range(3):
            piece = rest.astype(BF16)
            rest = rest - piece.astype(F32)
            total = total + jnp.dot(piece, same_group, preferred_element_type=F32)
        return total

    load_x.wait()

    def stat_body(i, carry):
        a, b = carry
        blk = xv[pl.ds(i * COLS, COLS), :].astype(F32).reshape(COLS // 8, 8, CHANNELS)
        return a + jnp.sum(blk, axis=0), b + jnp.sum(blk * blk, axis=0)

    zero8 = jnp.zeros((8, CHANNELS), F32)
    a, b = lax.fori_loop(0, ROWS_DEV, stat_body, (zero8, zero8))
    stat_a[low] = pack_rows(jnp.sum(a, axis=0, keepdims=True), jnp.sum(b, axis=0, keepdims=True))
    pl.semaphore_wait(barrier, 15 + 4 + 1 + 2 + 7)

    exchange(stat_a, 8, low, low_of, sa_send, sa_recv)
    leg1_copy().start()
    far_copy(0).start()

    @pl.when(x_high == 1)
    def send_own():
        for k in range(8):
            near_copy(k, True).start()

    load_wt.wait()
    load_wsp.wait()
    for k in range(3):
        wtt[k] = wt[k].T

    def turn_weight(i, _):
        wspt[pl.ds(i * CHANNELS, CHANNELS), :] = wsp[pl.ds((8 - i) * CHANNELS, CHANNELS), :].T
        return 0

    lax.fori_loop(0, 9, turn_weight, 0)

    stat_b[high] = collect(stat_a, 8, low, low_of, sa_send, sa_recv)
    exchange(stat_b, 16, high, high_of, sb_send, sb_recv)
    for k in (1, 2, 3):
        far_copy(k).start()
    load_g.wait()
    moments = group_sum(collect(stat_b, 16, high, high_of, sb_send, sb_recv)) * (1.0 / COUNT)
    mean = moments[0:1]
    rstd = lax.rsqrt(moments[1:2] - mean * mean + EPS)
    gain = gain_ref[...]
    bias = bias_ref[...]

    def forward(k):
        far_copy(k).wait_recv()

        @pl.when(x_high == 0)
        def pass_on():
            near_copy(k, False).start()


    col_id = lax.broadcasted_iota(jnp.int32, (COLS, CHANNELS), 0)

    def store_shifts(buf, padded_row, v):
        rows = pl.ds(padded_row * COLS, COLS)
        buf[rows, CHANNELS : 2 * CHANNELS] = v.astype(BF16)
        left = jnp.where(col_id == 0, 0.0, pltpu.roll(v, 1, 0))
        right = jnp.where(col_id == COLS - 1, 0.0, pltpu.roll(v, COLS - 1, 0))
        buf[rows, 0:CHANNELS] = left.astype(BF16)
        buf[rows, 2 * CHANNELS : 3 * CHANNELS] = right.astype(BF16)

    def normalize(rows):
        xhat = (xv[rows, :].astype(F32) - mean) * rstd
        pre = xhat * gain + bias
        return xhat, pre, jax.nn.sigmoid(pre)

    def act_row(r):
        _, pre, sigma = normalize(pl.ds(r * COLS, COLS))
        store_shifts(act3, r + 1, pre * sigma)

    middle = slice(CHANNELS, 2 * CHANNELS)

    def halo_copies(buf, halo, send_sem, recv_sem):
        first = copy(
            buf.at[pl.ds(COLS, COLS), middle], halo.at[1], send_sem.at[0], recv_sem.at[1], at(down)
        )
        last = copy(
            buf.at[pl.ds(PIXELS, COLS), middle], halo.at[0], send_sem.at[1], recv_sem.at[0], at(up)
        )
        return first, last

    def send_halo(buf, halo, send_sem, recv_sem):
        for c in halo_copies(buf, halo, send_sem, recv_sem):
            c.start()

    def take_halo(buf, halo, send_sem, recv_sem):
        for c in halo_copies(buf, halo, send_sem, recv_sem):
            c.wait_recv()
        keep_low = jnp.where(place > 0, 1.0, 0.0).astype(F32)
        keep_high = jnp.where(place < 3, 1.0, 0.0).astype(F32)
        store_shifts(buf, 0, halo[0].astype(F32) * keep_low)
        store_shifts(buf, ROWS_DEV + 1, halo[1].astype(F32) * keep_high)

    act_row(0)
    act_row(ROWS_DEV - 1)
    send_halo(act3, act_halo, ah_send, ah_recv)
    leg1_copy().wait_recv()
    leg2_copy().start()
    far_copy(4).start()
    far_copy(5).start()

    def act_body(r, _):
        act_row(r)
        return 0

    lax.fori_loop(1, ROWS_DEV - 1, act_body, 0)

    def convolve(buf, weights, i):
        total = None
        for dy in range(3):
            term = jnp.dot(
                buf[pl.ds(i * BLOCK + dy * COLS, BLOCK), :],
                weights[dy * 3 * CHANNELS : (dy + 1) * 3 * CHANNELS, :],
                preferred_element_type=F32,
            )
            total = term if total is None else total + term
        return total

    keep1 = jnp.where(frame < FRAMES - 1, 1.0, 0.0).astype(F32)
    keep2 = jnp.where(frame < FRAMES - 2, 1.0, 0.0).astype(F32)

    def cg_row(k):
        r = ORDER[k]
        near_copy(k, True).wait_recv()
        rows = pl.ds(r * COLS, COLS)
        total = jnp.dot(cots[0, rows, :], wtt[0], preferred_element_type=F32)
        total = total + keep1 * jnp.dot(cots[1, rows, :], wtt[1], preferred_element_type=F32)
        total = total + keep2 * jnp.dot(cots[2, rows, :], wtt[2], preferred_element_type=F32)
        store_shifts(cg3, r + 1, total.astype(BF16).astype(F32))

    def put(first_row, v, add):
        rows = pl.ds(first_row, v.shape[0])
        for half in range(2):
            w = v[:, half * 128 : (half + 1) * 128]
            part[half, rows, :] = part[half, rows, :] + w if add else w

    half_pixels = PIXELS // 2

    def temporal_half(h):
        pixels = slice(h * half_pixels, (h + 1) * half_pixels)
        for k, keep in enumerate((None, keep1, keep2)):
            v = jnp.dot(convt[:, pixels], cots[k, pixels, :], preferred_element_type=F32)
            put((9 + k) * CHANNELS, v if keep is None else v * keep, h > 0)

    def spatial_half(h, dy):
        begin = h * half_pixels
        v = lax.dot_general(
            act3[dy * COLS + begin : dy * COLS + begin + half_pixels, :],
            cg3[COLS + begin : COLS + begin + half_pixels, middle],
            (((0,), (0,)), ((), ())),
            preferred_element_type=F32,
        )
        put(dy * chunk_rows, v, h > 0)

    chunk_rows = 3 * CHANNELS

    def core_copy(i):
        rows = pl.ds(i * chunk_rows, chunk_rows)
        return copy(
            part.at[1 - core, rows], core_in.at[rows], core_send.at[i], core_recv.at[i],
            at(other_core),
        )

    forward(0)
    forward(1)
    cg_row(0)
    cg_row(1)
    send_halo(cg3, cg_halo, ch_send, ch_recv)
    far_copy(6).start()
    forward(2)
    take_halo(act3, act_halo, ah_send, ah_recv)

    def conv_body(i, _):
        conv[pl.ds(i * BLOCK, BLOCK), :] = convolve(act3, wsp, i).astype(BF16)
        return 0

    lax.fori_loop(0, PIXELS // BLOCK, conv_body, 0)
    forward(3)

    def turn_conv(i, _):
        src = pl.ds(pl.multiple_of(i * 128, 128), 128)
        convt[:, src] = conv[src, :].T
        return 0

    lax.fori_loop(0, PIXELS // 128, turn_conv, 0)
    cg_row(2)
    forward(4)
    cg_row(3)
    forward(5)
    cg_row(4)
    temporal_half(0)
    for dy in range(3):
        spatial_half(0, dy)
    forward(6)
    cg_row(5)
    forward(7)
    cg_row(6)
    take_halo(cg3, cg_halo, ch_send, ch_recv)
    cg_row(7)
    temporal_half(1)
    core_copy(3).start()
    for dy in (0, 1, 2):
        spatial_half(1, dy)
        core_copy(dy).start()

    def back_block(i, carry):
        rows = pl.ds(i * BLOCK, BLOCK)
        xhat, pre, sigma = normalize(rows)
        v = convolve(cg3, wspt, i) * sigma * (1.0 + pre * (1.0 - sigma))
        pre_grad[rows, :] = v
        a, b = carry
        a = a + jnp.sum(v.reshape(BLOCK // 8, 8, CHANNELS), axis=0)
        b = b + jnp.sum((v * xhat).reshape(BLOCK // 8, 8, CHANNELS), axis=0)
        return a, b

    def s1_copy(which, me, o, peer):
        buf = (in1a, in1b)[which]
        target = (at_x, at_y)[which]
        return copy(
            part.at[core, pl.ds(which * PART + o * QUARTER, QUARTER)], buf.at[me],
            s1_send.at[which, o], s1_recv.at[which, me], target(peer),
        )

    def add_core(i):
        core_copy(i).wait_recv()
        rows = pl.ds(i * chunk_rows, chunk_rows)
        part[core, rows, :] = part[core, rows, :] + core_in[rows, :]
        which = i // 2
        me = (x, y)[which]
        for o in (2 * (i % 2), 2 * (i % 2) + 1):
            @pl.when(me != o)
            def send_slice():
                s1_copy(which, me, o, o).start()

    sums = (zero8, zero8)
    for i, chunk in enumerate((3, 0, 1, 2)):
        sums = back_block(i, sums)
        add_core(chunk)
    a, b = sums
    back_a[low] = pack_rows(jnp.sum(a, axis=0, keepdims=True), jnp.sum(b, axis=0, keepdims=True))
    exchange(back_a, 8, low, low_of, ba_send, ba_recv)

    def loop3(me, body):
        def step(j, _):
            body(j, lax.rem(me + j, 4))
            return 0

        lax.fori_loop(1, 4, step, 0)

    back_b[high] = collect(back_a, 8, low, low_of, ba_send, ba_recv)
    exchange(back_b, 16, high, high_of, bb_send, bb_recv)

    def s1_finish(which):
        me = (x, y)[which]
        buf = (in1a, in1b)[which]
        mid = (mid_a, mid_b)[which]

        def wait(j, o):
            s1_copy(which, o, o, o).wait_recv()

        loop3(me, wait)
        mine = pl.ds(which * PART + me * QUARTER, QUARTER)
        total = part[core, mine, :]
        for j in range(1, 4):
            total = total + buf[lax.rem(me + j, 4)]
        mid[...] = total

    def s2_copy(which, me, o):
        mid = (mid_a, mid_b)[which]
        buf = (in2a, in2b)[which]
        target = (at_y, at_x)[which]
        return copy(
            mid.at[pl.ds(o * SIXTEENTH, SIXTEENTH)], buf.at[me],
            s2_send.at[which, o], s2_recv.at[which, me], target(o),
        )

    def s2_start(which):
        me = (y, x)[which]
        loop3(me, lambda j, o: s2_copy(which, me, o).start())

    def s2_finish(which):
        me = (y, x)[which]
        mid = (mid_a, mid_b)[which]
        buf = (in2a, in2b)[which]

        def wait(j, o):
            s2_copy(which, o, o).wait_recv()

        loop3(me, wait)
        total = mid[pl.ds(me * SIXTEENTH, SIXTEENTH), :]
        for j in range(1, 4):
            total = total + buf[lax.rem(me + j, 4)]
        mid2[which * SIXTEENTH : (which + 1) * SIXTEENTH, :] = total

    s1_finish(1)
    s2_start(1)
    s1_finish(0)
    s2_start(0)

    sums = collect(back_b, 16, high, high_of, bb_send, bb_recv)
    clip_sums[clip] = sums
    clip_copy = copy(
        clip_sums.at[clip], clip_sums.at[clip], clip_sem.at[0], clip_sem.at[1], (1 - clip, seq)
    )
    clip_copy.start()
    norm_sums = group_sum(sums * gain) * (1.0 / COUNT)
    m1 = norm_sums[0:1]
    m2 = norm_sums[1:2]

    def out_body(i, _):
        rows = pl.ds(i * COLS, COLS)
        xhat = (xv[rows, :].astype(F32) - mean) * rstd
        v = rstd * (pre_grad[rows, :] * gain - m1 - xhat * m2)
        grad_v[rows, :] = (cots[0, rows, :].astype(F32) + v).astype(BF16)
        return 0

    lax.fori_loop(0, ROWS_DEV, out_body, 0)
    store_grad = pltpu.make_async_copy(grad_v, grad_out, load_sem.at[4])
    store_grad.start()

    def s3_copy(o, slot):
        return copy(
            mid2.at[pl.ds(SHARD * (o // 2), SHARD)], in3.at[slot],
            s3_send.at[o], s3_recv.at[slot], at_z(o),
        )

    def s3_start(which):
        def body(j, _):
            o = 4 * which + j

            @pl.when(o != z)
            def send_shard():
                s3_copy(o, z).start()

            return 0

        lax.fori_loop(0, 4, body, 0)

    def s3_wait(j, _):
        o = lax.rem(z + j, 8)
        s3_copy(o, o).wait_recv()
        return 0

    s2_finish(1)
    s3_start(1)
    s2_finish(0)
    s3_start(0)
    in3[z] = mid2[pl.ds(SHARD * zh, SHARD), :]

    copy(
        clip_sums.at[1 - clip], clip_sums.at[1 - clip], clip_sem.at[0], clip_sem.at[1],
        (1 - clip, seq),
    ).wait_recv()
    both = (clip_sums[0] + clip_sums[1]) * SCALE
    bias_out[...] = both[0:1]
    gain_out[...] = both[1:2]

    lax.fori_loop(1, 8, s3_wait, 0)
    total = in3[0]
    for o in range(1, 8):
        total = total + in3[o]

    def shard_at(o):
        second = o // 2
        first = 1 - second
        base = second * (PART + QUARTER * y + SIXTEENTH * x)
        base = base + first * (QUARTER * x + SIXTEENTH * y)
        return pl.multiple_of(base + SHARD * lax.rem(o, 2), SHARD)

    full[core, pl.ds(shard_at(zh), SHARD), :] = (total * SCALE).astype(BF16)

    def spread(where, me, target, send_sem, recv_sem, rows):
        def body(j, o):
            place_at = full.at[core, pl.ds(where(me), rows)]
            copy(place_at, place_at, send_sem.at[o], recv_sem.at[me], target(o)).start()

        loop3(me, body)

    def gather(where, me, target, send_sem, recv_sem, rows):
        def body(j, o):
            theirs = full.at[core, pl.ds(where(o), rows)]
            copy(theirs, theirs, send_sem.at[o], recv_sem.at[o], target(o)).wait_recv()

        loop3(me, body)

    g3 = (shard_at, zh, at_zh, g3_send, g3_recv, SHARD)
    spread(*g3)
    gather(*g3)

    def sixteenth_a(o):
        return pl.multiple_of(QUARTER * x + SIXTEENTH * o, SIXTEENTH)

    def sixteenth_b(o):
        return pl.multiple_of(PART + QUARTER * y + SIXTEENTH * o, SIXTEENTH)

    def quarter_a(o):
        return pl.multiple_of(QUARTER * o, QUARTER)

    def quarter_b(o):
        return pl.multiple_of(PART + QUARTER * o, QUARTER)

    g2a = (sixteenth_a, y, at_y, g2_send.at[0], g2_recv.at[0], SIXTEENTH)
    g2b = (sixteenth_b, x, at_x, g2_send.at[1], g2_recv.at[1], SIXTEENTH)
    g1a = (quarter_a, x, at_x, g1_send.at[0], g1_recv.at[0], QUARTER)
    g1b = (quarter_b, y, at_y, g1_send.at[1], g1_recv.at[1], QUARTER)
    spread(*g2a)
    spread(*g2b)
    gather(*g2a)
    spread(*g1a)
    gather(*g2b)
    spread(*g1b)

    def to_core(i, half):
        rows = full.at[half, pl.ds(i * PART, PART)]
        return copy(rows, rows, gc_send.at[i], gc_recv.at[i], at(other_core))

    def settle(where, me, target, send_sem, recv_sem, rows):
        def body(j, o):
            mine = full.at[core, pl.ds(where(me), rows)]
            copy(mine, mine, send_sem.at[o], recv_sem.at[me], target(o)).wait_send()

        loop3(me, body)

    def store_params(i, half, slot):
        rows = pl.ds(i * PART, PART)
        return pltpu.make_async_copy(
            full.at[half, rows], params_out.at[half, rows], load_sem.at[5 + slot]
        )

    gather(*g1a)
    to_core(0, core).start()
    gather(*g1b)
    to_core(1, core).start()
    store_mine = pltpu.make_async_copy(full.at[core], params_out.at[core], load_sem.at[5])
    store_mine.start()

    for k in range(8):
        near_copy(k, True).wait_send()
    for k in range(7):
        far_copy(k).wait_send()
    leg1_copy().wait_send()
    leg2_copy().wait_send()
    for args in ((act3, act_halo, ah_send, ah_recv), (cg3, cg_halo, ch_send, ch_recv)):
        for c in halo_copies(*args):
            c.wait_send()
    drain(stat_a, 8, low, low_of, sa_send, sa_recv)
    drain(stat_b, 16, high, high_of, sb_send, sb_recv)
    drain(back_a, 8, low, low_of, ba_send, ba_recv)
    drain(back_b, 16, high, high_of, bb_send, bb_recv)
    clip_copy.wait_send()
    for i in range(4):
        core_copy(i).wait_send()
    for which in range(2):
        loop3((x, y)[which], lambda j, o: s1_copy(which, (x, y)[which], o, o).wait_send())
        loop3((y, x)[which], lambda j, o: s2_copy(which, (y, x)[which], o).wait_send())

    def s3_sent(j, _):
        s3_copy(lax.rem(z + j, 8), z).wait_send()
        return 0

    lax.fori_loop(1, 8, s3_sent, 0)
    for args in (g3, g2a, g2b, g1a, g1b):
        settle(*args)

    for i in range(2):
        to_core(i, 1 - core).wait_recv()
        store_params(i, 1 - core, 1 + i).start()
    for i in range(2):
        to_core(i, core).wait_send()
    store_grad.wait()
    store_mine.wait()
    for i in range(2):
        store_params(i, 1 - core, 1 + i).wait()


def finish_kernel(grad, params, gain, bias, grad_out, spatial, temporal, gain_out, bias_out):
    step = pl.program_id(0)
    grad_out[...] = grad[...]

    @pl.when(step < 3)
    def put_spatial():
        for half in range(2):
            spatial[:, :, half * 128 : (half + 1) * 128] = params[half].astype(F32)

    @pl.when(step == 3)
    def put_temporal():
        for half in range(2):
            temporal[:, :, half * 128 : (half + 1) * 128] = params[half].astype(F32)
        gain_out[...] = gain[0]
        bias_out[...] = bias[0]


def local(block_input, cotangent, group_norm_gain, group_norm_bias, w_spatial, w_temporal):
    any_space = pl.BlockSpec(memory_space=pl.ANY)
    vmem = pl.BlockSpec(memory_space=pltpu.VMEM)
    dma = pltpu.SemaphoreType.DMA
    scratch = [
        pltpu.VMEM((PIXELS, CHANNELS), BF16),
        pltpu.VMEM((3, PIXELS, CHANNELS), BF16),
        pltpu.VMEM((PADDED, 3 * CHANNELS), BF16),
        pltpu.VMEM((PADDED, 3 * CHANNELS), BF16),
        pltpu.VMEM((PIXELS, CHANNELS), BF16),
        pltpu.VMEM((CHANNELS, PIXELS), BF16),
        pltpu.VMEM((9 * CHANNELS, CHANNELS), BF16),
        pltpu.VMEM((9 * CHANNELS, CHANNELS), BF16),
        pltpu.VMEM((3, CHANNELS, CHANNELS), BF16),
        pltpu.VMEM((3, CHANNELS, CHANNELS), BF16),
        pltpu.VMEM((PIXELS, CHANNELS), F32),
        pltpu.VMEM((2, COLS, CHANNELS), BF16),
        pltpu.VMEM((2, COLS, CHANNELS), BF16),
        pltpu.VMEM((8, 8, CHANNELS), F32),
        pltpu.VMEM((16, 8, CHANNELS), F32),
        pltpu.VMEM((8, 8, CHANNELS), F32),
        pltpu.VMEM((16, 8, CHANNELS), F32),
        pltpu.VMEM((2, 8, CHANNELS), F32),
        pltpu.VMEM((2, HALF_ROWS, 128), F32),
        pltpu.VMEM((HALF_ROWS, 128), F32),
        pltpu.VMEM((4, QUARTER, 128), F32),
        pltpu.VMEM((4, QUARTER, 128), F32),
        pltpu.VMEM((QUARTER, 128), F32),
        pltpu.VMEM((QUARTER, 128), F32),
        pltpu.VMEM((4, SIXTEENTH, 128), F32),
        pltpu.VMEM((4, SIXTEENTH, 128), F32),
        pltpu.VMEM((2 * SIXTEENTH, 128), F32),
        pltpu.VMEM((8, SHARD, 128), F32),
        pltpu.VMEM((2, HALF_ROWS, 128), BF16),
        pltpu.VMEM((PIXELS, CHANNELS), BF16),
        pltpu.VMEM((COLS, CHANNELS), BF16),
        dma((8,)),
        dma((8,)), dma((8,)), dma((8,)), dma((8,)), dma((2,)), dma,
        dma((2,)), dma((2,)), dma((2,)), dma((2,)),
        dma((8,)), dma((8,)), dma((16,)), dma((16,)),
        dma((8,)), dma((8,)), dma((16,)), dma((16,)),
        dma((2,)),
        dma((4,)), dma((4,)),
        dma((2, 4)), dma((2, 4)), dma((2, 4)), dma((2, 4)),
        dma((8,)), dma((8,)),
        dma((4,)), dma((4,)), dma((2, 4)), dma((2, 4)), dma((2, 4)), dma((2, 4)),
        dma((2,)), dma((2,)),
    ]
    grad, params, gain_grad, bias_grad = pl.pallas_call(
        kernel,
        out_shape=(
            jax.ShapeDtypeStruct((PIXELS, CHANNELS), BF16),
            jax.ShapeDtypeStruct((2, HALF_ROWS, 128), BF16),
            jax.ShapeDtypeStruct((1, CHANNELS), F32),
            jax.ShapeDtypeStruct((1, CHANNELS), F32),
        ),
        in_specs=[any_space, any_space, vmem, vmem, any_space, any_space],
        out_specs=(any_space, any_space, vmem, vmem),
        scratch_shapes=scratch,
        compiler_params=pltpu.CompilerParams(
            collective_id=0, has_side_effects=True, vmem_limit_bytes=56 * 2**20
        ),
    )(
        block_input.reshape(PIXELS, CHANNELS),
        cotangent.reshape(PIXELS, CHANNELS),
        group_norm_gain.reshape(1, CHANNELS),
        group_norm_bias.reshape(1, CHANNELS),
        w_spatial.reshape(9 * CHANNELS, CHANNELS),
        w_temporal,
    )
    params = params.reshape(2, TAPS, CHANNELS, 128)
    whole = pl.BlockSpec((1, CHANNELS), lambda i: (0, 0))
    line = pl.BlockSpec((CHANNELS,), lambda i: (0,))
    block = pl.BlockSpec((BLOCK, CHANNELS), lambda i: (i, 0))
    grad, spatial, temporal, gain_grad, bias_grad = pl.pallas_call(
        finish_kernel,
        grid=(4,),
        out_shape=(
            jax.ShapeDtypeStruct((PIXELS, CHANNELS), BF16),
            jax.ShapeDtypeStruct((9, CHANNELS, CHANNELS), F32),
            jax.ShapeDtypeStruct((3, CHANNELS, CHANNELS), F32),
            jax.ShapeDtypeStruct((CHANNELS,), F32),
            jax.ShapeDtypeStruct((CHANNELS,), F32),
        ),
        in_specs=[
            block,
            pl.BlockSpec((2, 3, CHANNELS, 128), lambda i: (0, i, 0, 0)),
            whole,
            whole,
        ],
        out_specs=(
            block,
            pl.BlockSpec((3, CHANNELS, CHANNELS), lambda i: (jnp.minimum(i, 2), 0, 0)),
            pl.BlockSpec((3, CHANNELS, CHANNELS), lambda i: (0, 0, 0)),
            line,
            line,
        ),
        compiler_params=pltpu.CompilerParams(vmem_limit_bytes=60 * 2**20),
    )(grad, params, gain_grad, bias_grad)
    return (
        grad.reshape(1, ROWS_DEV, COLS, CHANNELS),
        spatial,
        temporal,
        gain_grad,
        bias_grad,
    )


def solution(mesh):
    return jax.shard_map(
        local,
        mesh=mesh,
        in_specs=(P("dp", "seq", None, None), P("dp", "seq", None, None), P(), P(), P(), P()),
        out_specs=(P("dp", "seq", None, None), P(), P(), P(), P()),
        check_vma=False,
    )
```

```python
import math

import jax
import jax.numpy as jnp
from jax import lax
from jax.experimental import pallas as pl
from jax.experimental.pallas import tpu as pltpu
from jax.sharding import PartitionSpec as P

F32 = jnp.float32
BF16 = jnp.bfloat16
MESH = pl.DeviceIdType.MESH

CHANNELS = 256
GROUP = 8
ROWS_DEV = 8
COLS = 160
PIXELS = ROWS_DEV * COLS
PADDED = PIXELS + 2 * COLS
SEQ = 128
FRAMES = 32
EPS = 1e-06
COUNT = FRAMES * 32 * COLS * GROUP
SCALE = 1.0 / math.sqrt(2 * FRAMES * 32 * COLS)

ORDER = (0, 7, 1, 2, 3, 4, 5, 6)
BLOCK = 2 * COLS

TAPS = 12
HALF_ROWS = TAPS * CHANNELS
PARTS = 4
PART = HALF_ROWS // PARTS
QUARTER = PART // 4
SHARD = QUARTER // 4
PART_ORDER = (3, 0, 2, 1)


def kernel(
    x_hbm, g_hbm, gain_ref, bias_ref, wsp_hbm, wt_hbm,
    grad_out, params_out, gain_out, bias_out,
    xv, cots, act3, cg3, conv, convt, wsp, wspt, wt, wtt, pre_grad,
    act_halo, cg_halo, stat_a, stat_b, back_a, back_b, clip_sums,
    part, core_in, in1, mid, in2, mid2, in3, full, grad_v, passing,
    load_sem, store_sem, far_send, far_recv, near_send, near_recv, leg1_send, leg1_recv, leg2_send,
    ah_send, ah_recv, ch_send, ch_recv,
    sa_send, sa_recv, sb_send, sb_recv, ba_send, ba_recv, bb_send, bb_recv, clip_sem,
    core_send, core_recv, s1_send, s1_recv, s2_send, s2_recv, s3_send, s3_recv,
    g3_send, g3_recv, g2_send, g2_recv, g1_send, g1_recv, gc_send, gc_recv,
):
    clip = lax.axis_index("dp")
    seq = lax.axis_index("seq")
    core = lax.rem(seq, 2)
    x = lax.rem(seq // 2, 4)
    zh = lax.rem(seq // 8, 4)
    y = seq // 32
    low = lax.rem(seq, 8)
    high = seq // 8
    z = zh * 2 + clip
    slab = lax.rem(seq + 2, SEQ)
    place = lax.rem(slab, 4)
    frame = slab // 4

    def at(s):
        return (clip, s)

    def at_x(o):
        return (clip, seq + 2 * (o - x))

    def at_y(o):
        return (clip, seq + 32 * (o - y))

    def at_zh(o):
        return (clip, seq + 8 * (o - zh))

    def at_z(o):
        return (lax.rem(o, 2), seq + 8 * (o // 2 - zh))

    up = lax.rem(seq + 1, SEQ)
    down = lax.rem(seq + SEQ - 1, SEQ)
    far_to = lax.rem(seq + SEQ - 8, SEQ)
    far_from = lax.rem(seq + 8, SEQ)
    other_core = seq + 1 - 2 * core
    x_high = x // 2
    near_to = seq + 4 - 8 * x_high

    def copy(src, dst, send_sem, recv_sem, device):
        return pltpu.make_async_remote_copy(
            src_ref=src, dst_ref=dst, send_sem=send_sem, recv_sem=recv_sem,
            device_id=device, device_id_type=MESH,
        )

    load_x = pltpu.make_async_copy(x_hbm, xv, load_sem.at[0])
    load_g = pltpu.make_async_copy(g_hbm, cots.at[0], load_sem.at[1])
    load_wsp = pltpu.make_async_copy(wsp_hbm, wsp, load_sem.at[2])
    load_wt = pltpu.make_async_copy(wt_hbm, wt, load_sem.at[3])
    load_x.start()
    load_g.start()
    load_wsp.start()
    load_wt.start()

    barrier = pltpu.get_barrier_semaphore()

    def greet(device):
        pl.semaphore_signal(barrier, inc=1, device_id=device, device_id_type=MESH)

    def greet_low(j, _):
        greet(at(seq - low + lax.rem(low + j, 8)))
        return 0

    def greet_high(j, _):
        greet(at(lax.rem(high + j, 16) * 8 + low))
        return 0

    def greet_z(j, _):
        greet((1 - clip, seq + 8 * (j - zh)))
        return 0

    z_up = lax.rem(z + 3, 8)
    z_down = lax.rem(z + 5, 8)

    def wrapped(source_z):
        return 1 - jnp.minimum(source_z // 2, 1)

    def at_zy(zz, yy):
        return (lax.rem(zz, 2), seq + 8 * (zz // 2 - zh) + 32 * (yy - y))

    leg1_to = at_zy(z_up, y)
    leg2_to = at_zy(z_up, lax.rem(y + 4 - wrapped(z_down), 4))
    leg2_from = at_zy(z_down, lax.rem(y + wrapped(lax.rem(z + 2, 8)), 4))

    lax.fori_loop(1, 16, greet_high, 0)
    lax.fori_loop(0, 4, greet_z, 0)
    greet(leg2_from)
    greet(at(up))
    greet(at(down))
    lax.fori_loop(1, 8, greet_low, 0)

    def far_copy(k):
        rows = pl.ds(ORDER[k] * COLS, COLS)
        return copy(
            g_hbm.at[rows], cots.at[2, rows], far_send.at[k], far_recv.at[k], at(far_to)
        )

    def near_copy(k, own):
        rows = pl.ds(ORDER[k] * COLS, COLS)
        return copy(
            (g_hbm if own else cots.at[2]).at[rows], cots.at[1, rows],
            near_send.at[k], near_recv.at[k], at(near_to),
        )

    def leg1_copy(i):
        rows = pl.ds(ORDER[6 + i] * COLS, COLS)
        return copy(g_hbm.at[rows], passing.at[i], leg1_send.at[i], leg1_recv.at[i], leg1_to)

    def leg2_copy(i):
        rows = pl.ds(ORDER[6 + i] * COLS, COLS)
        return copy(
            passing.at[i], cots.at[2, rows], leg2_send.at[i], far_recv.at[6 + i], leg2_to
        )

    def pass_detour(i):
        leg1_copy(i).wait_recv()
        leg2_copy(i).start()

    def exchange(buf, n, me, target, send_sem, recv_sem):
        def body(j, _):
            o = lax.rem(me + j, n)
            copy(buf.at[me], buf.at[me], send_sem.at[o], recv_sem.at[me], at(target(o))).start()
            return 0

        lax.fori_loop(1, n, body, 0)

    def collect(buf, n, me, target, send_sem, recv_sem):
        def body(j, _):
            o = lax.rem(me + j, n)
            arrived = copy(buf.at[o], buf.at[o], send_sem.at[o], recv_sem.at[o], at(target(o)))
            arrived.wait_recv()
            return 0

        lax.fori_loop(1, n, body, 0)
        total = buf[0]
        for o in range(1, n):
            total = total + buf[o]
        return total

    def drain(buf, n, me, target, send_sem, recv_sem):
        def body(j, _):
            o = lax.rem(me + j, n)
            copy(buf.at[me], buf.at[me], send_sem.at[o], recv_sem.at[me], at(target(o))).wait_send()
            return 0

        lax.fori_loop(1, n, body, 0)

    def low_of(o):
        return seq - low + o

    def high_of(o):
        return o * 8 + low

    row_id = lax.broadcasted_iota(jnp.int32, (8, CHANNELS), 0)

    def pack_rows(first, second):
        return jnp.where(row_id == 0, first, jnp.where(row_id == 1, second, 0.0))

    group_a = lax.shift_right_logical(lax.broadcasted_iota(jnp.int32, (CHANNELS, CHANNELS), 0), 3)
    group_b = lax.shift_right_logical(lax.broadcasted_iota(jnp.int32, (CHANNELS, CHANNELS), 1), 3)
    same_group = jnp.where(group_a == group_b, 1.0, 0.0).astype(BF16)

    def group_sum(v):
        total = jnp.zeros_like(v)
        rest = v
        for _ in range(3):
            piece = rest.astype(BF16)
            rest = rest - piece.astype(F32)
            total = total + jnp.dot(piece, same_group, preferred_element_type=F32)
        return total

    load_x.wait()

    def stat_body(i, carry):
        a, b = carry
        blk = xv[pl.ds(i * COLS, COLS), :].astype(F32).reshape(COLS // 8, 8, CHANNELS)
        return a + jnp.sum(blk, axis=0), b + jnp.sum(blk * blk, axis=0)

    zero8 = jnp.zeros((8, CHANNELS), F32)
    a, b = lax.fori_loop(0, ROWS_DEV, stat_body, (zero8, zero8))
    stat_a[low] = pack_rows(jnp.sum(a, axis=0, keepdims=True), jnp.sum(b, axis=0, keepdims=True))
    pl.semaphore_wait(barrier, 15 + 4 + 1 + 2 + 7)

    exchange(stat_a, 8, low, low_of, sa_send, sa_recv)
    leg1_copy(0).start()
    far_copy(0).start()
    leg1_copy(1).start()

    @pl.when(x_high == 1)
    def send_own():
        for k in range(8):
            near_copy(k, True).start()

    load_wt.wait()
    load_wsp.wait()
    for k in range(3):
        wtt[k] = wt[k].T

    def turn_weight(i, _):
        wspt[pl.ds(i * CHANNELS, CHANNELS), :] = wsp[pl.ds((8 - i) * CHANNELS, CHANNELS), :].T
        return 0

    lax.fori_loop(0, 9, turn_weight, 0)

    stat_b[high] = collect(stat_a, 8, low, low_of, sa_send, sa_recv)
    exchange(stat_b, 16, high, high_of, sb_send, sb_recv)
    for k in (1, 2, 3):
        far_copy(k).start()
    load_g.wait()
    moments = group_sum(collect(stat_b, 16, high, high_of, sb_send, sb_recv)) * (1.0 / COUNT)
    mean = moments[0:1]
    rstd = lax.rsqrt(moments[1:2] - mean * mean + EPS)
    gain = gain_ref[...]
    bias = bias_ref[...]

    def forward(k):
        far_copy(k).wait_recv()

        @pl.when(x_high == 0)
        def pass_on():
            near_copy(k, False).start()


    col_id = lax.broadcasted_iota(jnp.int32, (COLS, CHANNELS), 0)

    def store_shifts(buf, padded_row, v):
        rows = pl.ds(padded_row * COLS, COLS)
        buf[rows, CHANNELS : 2 * CHANNELS] = v.astype(BF16)
        left = jnp.where(col_id == 0, 0.0, pltpu.roll(v, 1, 0))
        right = jnp.where(col_id == COLS - 1, 0.0, pltpu.roll(v, COLS - 1, 0))
        buf[rows, 0:CHANNELS] = left.astype(BF16)
        buf[rows, 2 * CHANNELS : 3 * CHANNELS] = right.astype(BF16)

    def normalize(rows):
        xhat = (xv[rows, :].astype(F32) - mean) * rstd
        pre = xhat * gain + bias
        return xhat, pre, jax.nn.sigmoid(pre)

    def act_row(r):
        _, pre, sigma = normalize(pl.ds(r * COLS, COLS))
        store_shifts(act3, r + 1, pre * sigma)

    middle = slice(CHANNELS, 2 * CHANNELS)

    def halo_copies(buf, halo, send_sem, recv_sem):
        first = copy(
            buf.at[pl.ds(COLS, COLS), middle], halo.at[1], send_sem.at[0], recv_sem.at[1], at(down)
        )
        last = copy(
            buf.at[pl.ds(PIXELS, COLS), middle], halo.at[0], send_sem.at[1], recv_sem.at[0], at(up)
        )
        return first, last

    def send_halo(buf, halo, send_sem, recv_sem):
        for c in halo_copies(buf, halo, send_sem, recv_sem):
            c.start()

    def take_halo(buf, halo, send_sem, recv_sem):
        for c in halo_copies(buf, halo, send_sem, recv_sem):
            c.wait_recv()
        keep_low = jnp.where(place > 0, 1.0, 0.0).astype(F32)
        keep_high = jnp.where(place < 3, 1.0, 0.0).astype(F32)
        store_shifts(buf, 0, halo[0].astype(F32) * keep_low)
        store_shifts(buf, ROWS_DEV + 1, halo[1].astype(F32) * keep_high)

    act_row(0)
    act_row(ROWS_DEV - 1)
    send_halo(act3, act_halo, ah_send, ah_recv)
    far_copy(4).start()
    far_copy(5).start()
    pass_detour(0)

    def act_body(r, _):
        act_row(r)
        return 0

    lax.fori_loop(1, ROWS_DEV - 1, act_body, 0)

    def convolve(buf, weights, i):
        total = None
        for dy in range(3):
            term = jnp.dot(
                buf[pl.ds(i * BLOCK + dy * COLS, BLOCK), :],
                weights[dy * 3 * CHANNELS : (dy + 1) * 3 * CHANNELS, :],
                preferred_element_type=F32,
            )
            total = term if total is None else total + term
        return total

    keep1 = jnp.where(frame < FRAMES - 1, 1.0, 0.0).astype(F32)
    keep2 = jnp.where(frame < FRAMES - 2, 1.0, 0.0).astype(F32)

    def cg_row(k):
        r = ORDER[k]
        near_copy(k, True).wait_recv()
        rows = pl.ds(r * COLS, COLS)
        total = jnp.dot(cots[0, rows, :], wtt[0], preferred_element_type=F32)
        total = total + keep1 * jnp.dot(cots[1, rows, :], wtt[1], preferred_element_type=F32)
        total = total + keep2 * jnp.dot(cots[2, rows, :], wtt[2], preferred_element_type=F32)
        store_shifts(cg3, r + 1, total.astype(BF16).astype(F32))

    def put(first_row, v, add):
        rows = pl.ds(first_row, v.shape[0])
        for half in range(2):
            w = v[:, half * 128 : (half + 1) * 128]
            part[half, rows, :] = part[half, rows, :] + w if add else w

    half_pixels = PIXELS // 2

    def temporal_half(h):
        pixels = slice(h * half_pixels, (h + 1) * half_pixels)
        for k, keep in enumerate((None, keep1, keep2)):
            v = jnp.dot(convt[:, pixels], cots[k, pixels, :], preferred_element_type=F32)
            put((9 + k) * CHANNELS, v if keep is None else v * keep, h > 0)

    def spatial_half(h, dy):
        begin = h * half_pixels
        v = lax.dot_general(
            act3[dy * COLS + begin : dy * COLS + begin + half_pixels, :],
            cg3[COLS + begin : COLS + begin + half_pixels, middle],
            (((0,), (0,)), ((), ())),
            preferred_element_type=F32,
        )
        put(dy * chunk_rows, v, h > 0)

    chunk_rows = PART

    def core_copy(i):
        rows = pl.ds(i * chunk_rows, chunk_rows)
        return copy(
            part.at[1 - core, rows], core_in.at[rows], core_send.at[i], core_recv.at[i],
            at(other_core),
        )

    forward(0)
    pass_detour(1)
    forward(1)
    cg_row(0)
    cg_row(1)
    send_halo(cg3, cg_halo, ch_send, ch_recv)
    forward(2)
    take_halo(act3, act_halo, ah_send, ah_recv)

    def conv_body(i, _):
        conv[pl.ds(i * BLOCK, BLOCK), :] = convolve(act3, wsp, i).astype(BF16)
        return 0

    lax.fori_loop(0, PIXELS // BLOCK, conv_body, 0)
    forward(3)

    def turn_conv(i, _):
        src = pl.ds(pl.multiple_of(i * 128, 128), 128)
        convt[:, src] = conv[src, :].T
        return 0

    lax.fori_loop(0, PIXELS // 128, turn_conv, 0)
    cg_row(2)
    forward(4)
    cg_row(3)
    forward(5)
    cg_row(4)
    temporal_half(0)
    for dy in range(3):
        spatial_half(0, dy)
    forward(6)
    cg_row(5)
    forward(7)
    cg_row(6)
    take_halo(cg3, cg_halo, ch_send, ch_recv)
    cg_row(7)
    temporal_half(1)
    core_copy(3).start()
    for dy in PART_ORDER[1:]:
        spatial_half(1, dy)
        core_copy(dy).start()

    def back_block(i, carry):
        rows = pl.ds(i * BLOCK, BLOCK)
        xhat, pre, sigma = normalize(rows)
        v = convolve(cg3, wspt, i) * sigma * (1.0 + pre * (1.0 - sigma))
        pre_grad[rows, :] = v
        a, b = carry
        a = a + jnp.sum(v.reshape(BLOCK // 8, 8, CHANNELS), axis=0)
        b = b + jnp.sum((v * xhat).reshape(BLOCK // 8, 8, CHANNELS), axis=0)
        return a, b

    def first_axis(p):
        return ((x, at_x), (y, at_y))[p // 2]

    def second_axis(p):
        return ((y, at_y), (x, at_x))[p // 2]

    def loop3(me, body):
        def step(j, _):
            body(lax.rem(me + j, 4))
            return 0

        lax.fori_loop(1, 4, step, 0)

    def s1_copy(p, o):
        me, target = first_axis(p)
        return copy(
            part.at[core, pl.ds(p * PART + o * QUARTER, QUARTER)], in1.at[p, me],
            s1_send.at[p, o], s1_recv.at[p, me], target(o),
        )

    def s1_arrived(p, o):
        _, target = first_axis(p)
        return copy(in1.at[p, o], in1.at[p, o], s1_send.at[p, o], s1_recv.at[p, o], target(o))

    def s2_copy(p, o):
        me, target = second_axis(p)
        return copy(
            mid.at[p, pl.ds(o * SHARD, SHARD)], in2.at[p, me],
            s2_send.at[p, o], s2_recv.at[p, me], target(o),
        )

    def s2_arrived(p, o):
        _, target = second_axis(p)
        return copy(in2.at[p, o], in2.at[p, o], s2_send.at[p, o], s2_recv.at[p, o], target(o))

    def add_core(p):
        core_copy(p).wait_recv()
        rows = pl.ds(p * PART, PART)
        part[core, rows, :] = part[core, rows, :] + core_in[rows, :]
        loop3(first_axis(p)[0], lambda o: s1_copy(p, o).start())

    sums = (zero8, zero8)
    for i, p in enumerate(PART_ORDER):
        sums = back_block(i, sums)
        add_core(p)
    a, b = sums
    back_a[low] = pack_rows(jnp.sum(a, axis=0, keepdims=True), jnp.sum(b, axis=0, keepdims=True))
    exchange(back_a, 8, low, low_of, ba_send, ba_recv)

    def s1_finish(p):
        me, _ = first_axis(p)
        loop3(me, lambda o: s1_arrived(p, o).wait_recv())
        total = part[core, pl.ds(p * PART + me * QUARTER, QUARTER), :]
        for j in range(1, 4):
            total = total + in1[p, lax.rem(me + j, 4)]
        mid[p] = total
        loop3(second_axis(p)[0], lambda o: s2_copy(p, o).start())

    def s3_copy(o, slot):
        return copy(mid2.at[o // 2], in3.at[slot], s3_send.at[o], s3_recv.at[slot], at_z(o))

    def s2_finish(p):
        me, _ = second_axis(p)
        loop3(me, lambda o: s2_arrived(p, o).wait_recv())
        total = mid[p, pl.ds(me * SHARD, SHARD), :]
        for j in range(1, 4):
            total = total + in2[p, lax.rem(me + j, 4)]
        mid2[p] = total
        for o in (2 * p, 2 * p + 1):
            @pl.when(z != o)
            def send_shard():
                s3_copy(o, z).start()

    for p in PART_ORDER:
        s1_finish(p)

    back_b[high] = collect(back_a, 8, low, low_of, ba_send, ba_recv)
    exchange(back_b, 16, high, high_of, bb_send, bb_recv)

    for p in PART_ORDER:
        s2_finish(p)

    sums = collect(back_b, 16, high, high_of, bb_send, bb_recv)
    clip_sums[clip] = sums
    clip_copy = copy(
        clip_sums.at[clip], clip_sums.at[clip], clip_sem.at[0], clip_sem.at[1], (1 - clip, seq)
    )
    clip_copy.start()
    norm_sums = group_sum(sums * gain) * (1.0 / COUNT)
    m1 = norm_sums[0:1]
    m2 = norm_sums[1:2]

    def out_body(i, _):
        rows = pl.ds(i * COLS, COLS)
        xhat = (xv[rows, :].astype(F32) - mean) * rstd
        v = rstd * (pre_grad[rows, :] * gain - m1 - xhat * m2)
        grad_v[rows, :] = (cots[0, rows, :].astype(F32) + v).astype(BF16)
        return 0

    lax.fori_loop(0, ROWS_DEV, out_body, 0)
    store_grad = pltpu.make_async_copy(grad_v, grad_out, store_sem.at[0])
    store_grad.start()

    def quarter_at(p, first):
        return pl.multiple_of(p * PART + QUARTER * first, QUARTER)

    def shard_at(p, first, second):
        return pl.multiple_of(p * PART + QUARTER * first + SHARD * second, SHARD)

    def own_shard(p):
        return full.at[core, pl.ds(shard_at(p, first_axis(p)[0], second_axis(p)[0]), SHARD)]

    def g3_copy(p, o):
        rows = own_shard(p)
        return copy(rows, rows, g3_send.at[o], g3_recv.at[p], at_zh(o))

    def g2_copy(p, o, sender):
        rows = full.at[core, pl.ds(shard_at(p, first_axis(p)[0], sender), SHARD)]
        return copy(rows, rows, g2_send.at[p, o], g2_recv.at[p, sender], second_axis(p)[1](o))

    def g1_copy(p, o, sender):
        rows = full.at[core, pl.ds(quarter_at(p, sender), QUARTER)]
        return copy(rows, rows, g1_send.at[p, o], g1_recv.at[p, sender], first_axis(p)[1](o))

    def to_core(p, half):
        rows = full.at[half, pl.ds(p * PART, PART)]
        return copy(rows, rows, gc_send.at[p], gc_recv.at[p], at(other_core))

    def store_params(p, half, slot):
        rows = pl.ds(p * PART, PART)
        return pltpu.make_async_copy(
            full.at[half, rows], params_out.at[half, rows], store_sem.at[1 + slot * PARTS + p]
        )

    for p in PART_ORDER:
        @pl.when(zh == p)
        def finish_part():
            in3[z] = mid2[p]

            def arrived(j, _):
                o = lax.rem(z + j, 8)
                copy(in3.at[o], in3.at[o], s3_send.at[o], s3_recv.at[o], at_z(o)).wait_recv()
                return 0

            lax.fori_loop(1, 8, arrived, 0)
            total = in3[0]
            for o in range(1, 8):
                total = total + in3[o]
            where = pl.ds(shard_at(p, first_axis(p)[0], second_axis(p)[0]), SHARD)
            full[core, where, :] = (total * SCALE).astype(BF16)
            loop3(zh, lambda o: g3_copy(p, o).start())

        @pl.when(zh != p)
        def take_part():
            g3_copy(p, zh + 1 - 2 * lax.rem(zh, 2)).wait_recv()

        me, _ = second_axis(p)
        loop3(me, lambda o: g2_copy(p, o, me).start())

    copy(
        clip_sums.at[1 - clip], clip_sums.at[1 - clip], clip_sem.at[0], clip_sem.at[1],
        (1 - clip, seq),
    ).wait_recv()
    both = (clip_sums[0] + clip_sums[1]) * SCALE
    bias_out[...] = both[0:1]
    gain_out[...] = both[1:2]

    for p in PART_ORDER:
        loop3(second_axis(p)[0], lambda o: g2_copy(p, o, o).wait_recv())
        me, _ = first_axis(p)
        loop3(me, lambda o: g1_copy(p, o, me).start())

    for p in PART_ORDER:
        loop3(first_axis(p)[0], lambda o: g1_copy(p, o, o).wait_recv())
        to_core(p, core).start()
        store_params(p, core, 0).start()

    for k in range(8):
        near_copy(k, True).wait_send()
    for k in range(6):
        far_copy(k).wait_send()
    for i in range(2):
        leg1_copy(i).wait_send()
        leg2_copy(i).wait_send()
    for args in ((act3, act_halo, ah_send, ah_recv), (cg3, cg_halo, ch_send, ch_recv)):
        for c in halo_copies(*args):
            c.wait_send()
    drain(stat_a, 8, low, low_of, sa_send, sa_recv)
    drain(stat_b, 16, high, high_of, sb_send, sb_recv)
    drain(back_a, 8, low, low_of, ba_send, ba_recv)
    drain(back_b, 16, high, high_of, bb_send, bb_recv)
    clip_copy.wait_send()

    def s3_sent(j, _):
        s3_copy(lax.rem(z + j, 8), z).wait_send()
        return 0

    lax.fori_loop(1, 8, s3_sent, 0)
    for p in range(PARTS):
        @pl.when(zh == p)
        def sent_part():
            loop3(zh, lambda o: g3_copy(p, o).wait_send())

    for p in range(PARTS):
        core_copy(p).wait_send()
        loop3(first_axis(p)[0], lambda o: s1_copy(p, o).wait_send())
        loop3(second_axis(p)[0], lambda o: s2_copy(p, o).wait_send())
        loop3(second_axis(p)[0], lambda o: g2_copy(p, o, second_axis(p)[0]).wait_send())
        loop3(first_axis(p)[0], lambda o: g1_copy(p, o, first_axis(p)[0]).wait_send())

    for p in PART_ORDER:
        to_core(p, 1 - core).wait_recv()
        store_params(p, 1 - core, 1).start()
    store_grad.wait()
    for p in PART_ORDER:
        to_core(p, core).wait_send()
        store_params(p, core, 0).wait()
        store_params(p, 1 - core, 1).wait()


def finish_kernel(
    grad, params, gain, bias, grad_out, spatial, temporal, gain_out, bias_out,
    params_v, out_v, sem,
):
    move_grad = pltpu.make_async_copy(grad, grad_out, sem.at[0])

    def load(i):
        taps = pl.ds(3 * i, 3)
        return pltpu.make_async_copy(params.at[:, taps], params_v.at[:, taps], sem.at[1 + i])

    def store(i):
        target = spatial.at[pl.ds(3 * i, 3)] if i < 3 else temporal
        return pltpu.make_async_copy(out_v.at[pl.ds(3 * i, 3)], target, sem.at[5 + i])

    for i in range(4):
        load(i).start()
    move_grad.start()
    gain_out[...] = gain[0]
    bias_out[...] = bias[0]
    for i in range(4):
        load(i).wait()
        for half in range(2):
            out_v[3 * i : 3 * i + 3, :, half * 128 : (half + 1) * 128] = params_v[
                half, 3 * i : 3 * i + 3
            ].astype(F32)
        store(i).start()
    move_grad.wait()
    for i in range(4):
        store(i).wait()


def local(block_input, cotangent, group_norm_gain, group_norm_bias, w_spatial, w_temporal):
    any_space = pl.BlockSpec(memory_space=pl.ANY)
    vmem = pl.BlockSpec(memory_space=pltpu.VMEM)
    dma = pltpu.SemaphoreType.DMA
    scratch = [
        pltpu.VMEM((PIXELS, CHANNELS), BF16),
        pltpu.VMEM((3, PIXELS, CHANNELS), BF16),
        pltpu.VMEM((PADDED, 3 * CHANNELS), BF16),
        pltpu.VMEM((PADDED, 3 * CHANNELS), BF16),
        pltpu.VMEM((PIXELS, CHANNELS), BF16),
        pltpu.VMEM((CHANNELS, PIXELS), BF16),
        pltpu.VMEM((9 * CHANNELS, CHANNELS), BF16),
        pltpu.VMEM((9 * CHANNELS, CHANNELS), BF16),
        pltpu.VMEM((3, CHANNELS, CHANNELS), BF16),
        pltpu.VMEM((3, CHANNELS, CHANNELS), BF16),
        pltpu.VMEM((PIXELS, CHANNELS), F32),
        pltpu.VMEM((2, COLS, CHANNELS), BF16),
        pltpu.VMEM((2, COLS, CHANNELS), BF16),
        pltpu.VMEM((8, 8, CHANNELS), F32),
        pltpu.VMEM((16, 8, CHANNELS), F32),
        pltpu.VMEM((8, 8, CHANNELS), F32),
        pltpu.VMEM((16, 8, CHANNELS), F32),
        pltpu.VMEM((2, 8, CHANNELS), F32),
        pltpu.VMEM((2, HALF_ROWS, 128), F32),
        pltpu.VMEM((HALF_ROWS, 128), F32),
        pltpu.VMEM((PARTS, 4, QUARTER, 128), F32),
        pltpu.VMEM((PARTS, QUARTER, 128), F32),
        pltpu.VMEM((PARTS, 4, SHARD, 128), F32),
        pltpu.VMEM((PARTS, SHARD, 128), F32),
        pltpu.VMEM((8, SHARD, 128), F32),
        pltpu.VMEM((2, HALF_ROWS, 128), BF16),
        pltpu.VMEM((PIXELS, CHANNELS), BF16),
        pltpu.VMEM((2, COLS, CHANNELS), BF16),
        dma((4,)), dma((1 + 2 * PARTS,)),
        dma((8,)), dma((8,)), dma((8,)), dma((8,)),
        dma((2,)), dma((2,)), dma((2,)),
        dma((2,)), dma((2,)), dma((2,)), dma((2,)),
        dma((8,)), dma((8,)), dma((16,)), dma((16,)),
        dma((8,)), dma((8,)), dma((16,)), dma((16,)),
        dma((2,)),
        dma((4,)), dma((4,)),
        dma((4, 4)), dma((4, 4)), dma((4, 4)), dma((4, 4)),
        dma((8,)), dma((8,)),
        dma((4,)), dma((4,)), dma((4, 4)), dma((4, 4)), dma((4, 4)), dma((4, 4)),
        dma((4,)), dma((4,)),
    ]
    grad, params, gain_grad, bias_grad = pl.pallas_call(
        kernel,
        out_shape=(
            jax.ShapeDtypeStruct((PIXELS, CHANNELS), BF16),
            jax.ShapeDtypeStruct((2, HALF_ROWS, 128), BF16),
            jax.ShapeDtypeStruct((1, CHANNELS), F32),
            jax.ShapeDtypeStruct((1, CHANNELS), F32),
        ),
        in_specs=[any_space, any_space, vmem, vmem, any_space, any_space],
        out_specs=(any_space, any_space, vmem, vmem),
        scratch_shapes=scratch,
        compiler_params=pltpu.CompilerParams(
            collective_id=0, has_side_effects=True, vmem_limit_bytes=56 * 2**20
        ),
    )(
        block_input.reshape(PIXELS, CHANNELS),
        cotangent.reshape(PIXELS, CHANNELS),
        group_norm_gain.reshape(1, CHANNELS),
        group_norm_bias.reshape(1, CHANNELS),
        w_spatial.reshape(9 * CHANNELS, CHANNELS),
        w_temporal,
    )
    params = params.reshape(2, TAPS, CHANNELS, 128)
    grad, spatial, temporal, gain_grad, bias_grad = pl.pallas_call(
        finish_kernel,
        out_shape=(
            jax.ShapeDtypeStruct((PIXELS, CHANNELS), BF16),
            jax.ShapeDtypeStruct((9, CHANNELS, CHANNELS), F32),
            jax.ShapeDtypeStruct((3, CHANNELS, CHANNELS), F32),
            jax.ShapeDtypeStruct((CHANNELS,), F32),
            jax.ShapeDtypeStruct((CHANNELS,), F32),
        ),
        in_specs=[any_space, any_space, vmem, vmem],
        out_specs=(any_space, any_space, any_space, vmem, vmem),
        scratch_shapes=[
            pltpu.VMEM((2, TAPS, CHANNELS, 128), BF16),
            pltpu.VMEM((TAPS, CHANNELS, CHANNELS), F32),
            dma((9,)),
        ],
        compiler_params=pltpu.CompilerParams(vmem_limit_bytes=60 * 2**20),
    )(grad, params, gain_grad, bias_grad)
    return (
        grad.reshape(1, ROWS_DEV, COLS, CHANNELS),
        spatial,
        temporal,
        gain_grad,
        bias_grad,
    )


def solution(mesh):
    return jax.shard_map(
        local,
        mesh=mesh,
        in_specs=(P("dp", "seq", None, None), P("dp", "seq", None, None), P(), P(), P(), P()),
        out_specs=(P("dp", "seq", None, None), P(), P(), P(), P()),
        check_vma=False,
    )
```

```python
import math

import jax
import jax.numpy as jnp
from jax import lax
from jax.experimental import pallas as pl
from jax.experimental.pallas import tpu as pltpu
from jax.sharding import PartitionSpec as P

F32 = jnp.float32
BF16 = jnp.bfloat16
MESH = pl.DeviceIdType.MESH

CHANNELS = 256
GROUP = 8
ROWS_DEV = 8
COLS = 160
PIXELS = ROWS_DEV * COLS
PADDED = PIXELS + 2 * COLS
SEQ = 128
FRAMES = 32
EPS = 1e-06
COUNT = FRAMES * 32 * COLS * GROUP
SCALE = 1.0 / math.sqrt(2 * FRAMES * 32 * COLS)

ORDER = (0, 7, 1, 2, 3, 4, 5, 6)
BLOCK = 2 * COLS

TAPS = 12
HALF_ROWS = TAPS * CHANNELS
PARTS = 4
PART = HALF_ROWS // PARTS
QUARTER = PART // 4
SHARD = QUARTER // 4
PART_ORDER = (3, 0, 2, 1)


def kernel(
    x_hbm, g_hbm, gain_hbm, bias_hbm, wsp_hbm, wt_hbm,
    grad_out, params_out, sums_out,
    xv, cots, act3, cg3, conv, convt, wsp, wspt, wt, wtt, pre_grad,
    act_halo, cg_halo, stat_a, stat_b, back_a, back_b, clip_sums,
    part, core_in, in1, mid, in2, mid2, in3, full, grad_v, passing, affine, sums_v,
    load_sem, store_sem, far_send, far_recv, near_send, near_recv, leg1_send, leg1_recv, leg2_send,
    ah_send, ah_recv, ch_send, ch_recv,
    sa_send, sa_recv, sb_send, sb_recv, ba_send, ba_recv, bb_send, bb_recv, clip_sem,
    core_send, core_recv, s1_send, s1_recv, s2_send, s2_recv, s3_send, s3_recv,
    g3_send, g3_recv, g2_send, g2_recv, g1_send, g1_recv, gc_send, gc_recv,
):
    clip = lax.axis_index("dp")
    seq = lax.axis_index("seq")
    core = lax.rem(seq, 2)
    x = lax.rem(seq // 2, 4)
    zh = lax.rem(seq // 8, 4)
    y = seq // 32
    low = lax.rem(seq, 8)
    high = seq // 8
    z = zh * 2 + clip
    slab = lax.rem(seq + 2, SEQ)
    place = lax.rem(slab, 4)
    frame = slab // 4

    def at(s):
        return (clip, s)

    def at_x(o):
        return (clip, seq + 2 * (o - x))

    def at_y(o):
        return (clip, seq + 32 * (o - y))

    def at_zh(o):
        return (clip, seq + 8 * (o - zh))

    def at_z(o):
        return (lax.rem(o, 2), seq + 8 * (o // 2 - zh))

    up = lax.rem(seq + 1, SEQ)
    down = lax.rem(seq + SEQ - 1, SEQ)
    far_to = lax.rem(seq + SEQ - 8, SEQ)
    far_from = lax.rem(seq + 8, SEQ)
    other_core = seq + 1 - 2 * core
    x_high = x // 2
    near_to = seq + 4 - 8 * x_high

    def copy(src, dst, send_sem, recv_sem, device):
        return pltpu.make_async_remote_copy(
            src_ref=src, dst_ref=dst, send_sem=send_sem, recv_sem=recv_sem,
            device_id=device, device_id_type=MESH,
        )

    load_x = pltpu.make_async_copy(x_hbm, xv, load_sem.at[0])
    load_g = pltpu.make_async_copy(g_hbm, cots.at[0], load_sem.at[1])
    load_wsp = pltpu.make_async_copy(wsp_hbm, wsp, load_sem.at[2])
    load_wt = pltpu.make_async_copy(wt_hbm, wt, load_sem.at[3])
    load_x.start()
    load_g.start()
    load_wsp.start()
    load_wt.start()
    load_gain = pltpu.make_async_copy(gain_hbm, affine.at[0], load_sem.at[4])
    load_bias = pltpu.make_async_copy(bias_hbm, affine.at[1], load_sem.at[5])
    load_gain.start()
    load_bias.start()

    barrier = pltpu.get_barrier_semaphore()

    def greet(device):
        pl.semaphore_signal(barrier, inc=1, device_id=device, device_id_type=MESH)

    def greet_low(j, _):
        greet(at(seq - low + lax.rem(low + j, 8)))
        return 0

    def greet_high(j, _):
        greet(at(lax.rem(high + j, 16) * 8 + low))
        return 0

    def greet_z(j, _):
        greet((1 - clip, seq + 8 * (j - zh)))
        return 0

    z_up = lax.rem(z + 3, 8)
    z_down = lax.rem(z + 5, 8)

    def wrapped(source_z):
        return 1 - jnp.minimum(source_z // 2, 1)

    def at_zy(zz, yy):
        return (lax.rem(zz, 2), seq + 8 * (zz // 2 - zh) + 32 * (yy - y))

    leg1_to = at_zy(z_up, y)
    leg2_to = at_zy(z_up, lax.rem(y + 4 - wrapped(z_down), 4))
    leg2_from = at_zy(z_down, lax.rem(y + wrapped(lax.rem(z + 2, 8)), 4))

    lax.fori_loop(1, 16, greet_high, 0)
    lax.fori_loop(0, 4, greet_z, 0)
    greet(leg2_from)
    greet(at(up))
    greet(at(down))
    lax.fori_loop(1, 8, greet_low, 0)

    def far_copy(k):
        rows = pl.ds(ORDER[k] * COLS, COLS)
        return copy(
            g_hbm.at[rows], cots.at[2, rows], far_send.at[k], far_recv.at[k], at(far_to)
        )

    def near_copy(k, own):
        rows = pl.ds(ORDER[k] * COLS, COLS)
        return copy(
            (g_hbm if own else cots.at[2]).at[rows], cots.at[1, rows],
            near_send.at[k], near_recv.at[k], at(near_to),
        )

    def leg1_copy(i):
        rows = pl.ds(ORDER[6 + i] * COLS, COLS)
        return copy(g_hbm.at[rows], passing.at[i], leg1_send.at[i], leg1_recv.at[i], leg1_to)

    def leg2_copy(i):
        rows = pl.ds(ORDER[6 + i] * COLS, COLS)
        return copy(
            passing.at[i], cots.at[2, rows], leg2_send.at[i], far_recv.at[6 + i], leg2_to
        )

    def pass_detour(i):
        leg1_copy(i).wait_recv()
        leg2_copy(i).start()

    def exchange(buf, n, me, target, send_sem, recv_sem):
        def body(j, _):
            o = lax.rem(me + j, n)
            copy(buf.at[me], buf.at[me], send_sem.at[o], recv_sem.at[me], at(target(o))).start()
            return 0

        lax.fori_loop(1, n, body, 0)

    def collect(buf, n, me, target, send_sem, recv_sem):
        def body(j, _):
            o = lax.rem(me + j, n)
            arrived = copy(buf.at[o], buf.at[o], send_sem.at[o], recv_sem.at[o], at(target(o)))
            arrived.wait_recv()
            return 0

        lax.fori_loop(1, n, body, 0)
        total = buf[0]
        for o in range(1, n):
            total = total + buf[o]
        return total

    def drain(buf, n, me, target, send_sem, recv_sem):
        def body(j, _):
            o = lax.rem(me + j, n)
            copy(buf.at[me], buf.at[me], send_sem.at[o], recv_sem.at[me], at(target(o))).wait_send()
            return 0

        lax.fori_loop(1, n, body, 0)

    def low_of(o):
        return seq - low + o

    def high_of(o):
        return o * 8 + low

    row_id = lax.broadcasted_iota(jnp.int32, (8, CHANNELS), 0)

    def pack_rows(first, second):
        return jnp.where(row_id == 0, first, jnp.where(row_id == 1, second, 0.0))

    group_a = lax.shift_right_logical(lax.broadcasted_iota(jnp.int32, (CHANNELS, CHANNELS), 0), 3)
    group_b = lax.shift_right_logical(lax.broadcasted_iota(jnp.int32, (CHANNELS, CHANNELS), 1), 3)
    same_group = jnp.where(group_a == group_b, 1.0, 0.0).astype(BF16)

    def group_sum(v):
        total = jnp.zeros_like(v)
        rest = v
        for _ in range(3):
            piece = rest.astype(BF16)
            rest = rest - piece.astype(F32)
            total = total + jnp.dot(piece, same_group, preferred_element_type=F32)
        return total

    load_x.wait()

    def stat_body(i, carry):
        a, b = carry
        blk = xv[pl.ds(i * COLS, COLS), :].astype(F32).reshape(COLS // 8, 8, CHANNELS)
        return a + jnp.sum(blk, axis=0), b + jnp.sum(blk * blk, axis=0)

    zero8 = jnp.zeros((8, CHANNELS), F32)
    a, b = lax.fori_loop(0, ROWS_DEV, stat_body, (zero8, zero8))
    stat_a[low] = pack_rows(jnp.sum(a, axis=0, keepdims=True), jnp.sum(b, axis=0, keepdims=True))
    pl.semaphore_wait(barrier, 15 + 4 + 1 + 2 + 7)

    exchange(stat_a, 8, low, low_of, sa_send, sa_recv)
    leg1_copy(0).start()
    far_copy(0).start()
    leg1_copy(1).start()

    @pl.when(x_high == 1)
    def send_own():
        for k in range(8):
            near_copy(k, True).start()

    load_wt.wait()
    load_wsp.wait()
    for k in range(3):
        wtt[k] = wt[k].T

    def turn_weight(i, _):
        wspt[pl.ds(i * CHANNELS, CHANNELS), :] = wsp[pl.ds((8 - i) * CHANNELS, CHANNELS), :].T
        return 0

    lax.fori_loop(0, 9, turn_weight, 0)

    stat_b[high] = collect(stat_a, 8, low, low_of, sa_send, sa_recv)
    exchange(stat_b, 16, high, high_of, sb_send, sb_recv)
    for k in (1, 2, 3):
        far_copy(k).start()
    load_g.wait()
    moments = group_sum(collect(stat_b, 16, high, high_of, sb_send, sb_recv)) * (1.0 / COUNT)
    mean = moments[0:1]
    rstd = lax.rsqrt(moments[1:2] - mean * mean + EPS)
    load_gain.wait()
    load_bias.wait()
    gain = affine[0]
    bias = affine[1]

    def forward(k):
        far_copy(k).wait_recv()

        @pl.when(x_high == 0)
        def pass_on():
            near_copy(k, False).start()


    col_id = lax.broadcasted_iota(jnp.int32, (COLS, CHANNELS), 0)

    def store_shifts(buf, padded_row, v):
        rows = pl.ds(padded_row * COLS, COLS)
        buf[rows, CHANNELS : 2 * CHANNELS] = v.astype(BF16)
        left = jnp.where(col_id == 0, 0.0, pltpu.roll(v, 1, 0))
        right = jnp.where(col_id == COLS - 1, 0.0, pltpu.roll(v, COLS - 1, 0))
        buf[rows, 0:CHANNELS] = left.astype(BF16)
        buf[rows, 2 * CHANNELS : 3 * CHANNELS] = right.astype(BF16)

    def normalize(rows):
        xhat = (xv[rows, :].astype(F32) - mean) * rstd
        pre = xhat * gain + bias
        return xhat, pre, jax.nn.sigmoid(pre)

    def act_row(r):
        _, pre, sigma = normalize(pl.ds(r * COLS, COLS))
        store_shifts(act3, r + 1, pre * sigma)

    middle = slice(CHANNELS, 2 * CHANNELS)

    def halo_copies(buf, halo, send_sem, recv_sem):
        first = copy(
            buf.at[pl.ds(COLS, COLS), middle], halo.at[1], send_sem.at[0], recv_sem.at[1], at(down)
        )
        last = copy(
            buf.at[pl.ds(PIXELS, COLS), middle], halo.at[0], send_sem.at[1], recv_sem.at[0], at(up)
        )
        return first, last

    def send_halo(buf, halo, send_sem, recv_sem):
        for c in halo_copies(buf, halo, send_sem, recv_sem):
            c.start()

    def take_halo(buf, halo, send_sem, recv_sem):
        for c in halo_copies(buf, halo, send_sem, recv_sem):
            c.wait_recv()
        keep_low = jnp.where(place > 0, 1.0, 0.0).astype(F32)
        keep_high = jnp.where(place < 3, 1.0, 0.0).astype(F32)
        store_shifts(buf, 0, halo[0].astype(F32) * keep_low)
        store_shifts(buf, ROWS_DEV + 1, halo[1].astype(F32) * keep_high)

    act_row(0)
    act_row(ROWS_DEV - 1)
    send_halo(act3, act_halo, ah_send, ah_recv)
    far_copy(4).start()
    far_copy(5).start()
    pass_detour(0)

    def act_body(r, _):
        act_row(r)
        return 0

    lax.fori_loop(1, ROWS_DEV - 1, act_body, 0)

    def convolve(buf, weights, i):
        total = None
        for dy in range(3):
            term = jnp.dot(
                buf[pl.ds(i * BLOCK + dy * COLS, BLOCK), :],
                weights[dy * 3 * CHANNELS : (dy + 1) * 3 * CHANNELS, :],
                preferred_element_type=F32,
            )
            total = term if total is None else total + term
        return total

    keep1 = jnp.where(frame < FRAMES - 1, 1.0, 0.0).astype(F32)
    keep2 = jnp.where(frame < FRAMES - 2, 1.0, 0.0).astype(F32)

    def cg_row(k):
        r = ORDER[k]
        near_copy(k, True).wait_recv()
        rows = pl.ds(r * COLS, COLS)
        total = jnp.dot(cots[0, rows, :], wtt[0], preferred_element_type=F32)
        total = total + keep1 * jnp.dot(cots[1, rows, :], wtt[1], preferred_element_type=F32)
        total = total + keep2 * jnp.dot(cots[2, rows, :], wtt[2], preferred_element_type=F32)
        store_shifts(cg3, r + 1, total.astype(BF16).astype(F32))

    def put(first_row, v, add):
        rows = pl.ds(first_row, v.shape[0])
        for half in range(2):
            w = v[:, half * 128 : (half + 1) * 128]
            part[half, rows, :] = part[half, rows, :] + w if add else w

    half_pixels = PIXELS // 2

    def temporal_half(h):
        pixels = slice(h * half_pixels, (h + 1) * half_pixels)
        for k, keep in enumerate((None, keep1, keep2)):
            v = jnp.dot(convt[:, pixels], cots[k, pixels, :], preferred_element_type=F32)
            put((9 + k) * CHANNELS, v if keep is None else v * keep, h > 0)

    def spatial_half(h, dy):
        begin = h * half_pixels
        v = lax.dot_general(
            act3[dy * COLS + begin : dy * COLS + begin + half_pixels, :],
            cg3[COLS + begin : COLS + begin + half_pixels, middle],
            (((0,), (0,)), ((), ())),
            preferred_element_type=F32,
        )
        put(dy * chunk_rows, v, h > 0)

    chunk_rows = PART

    def core_copy(i):
        rows = pl.ds(i * chunk_rows, chunk_rows)
        return copy(
            part.at[1 - core, rows], core_in.at[rows], core_send.at[i], core_recv.at[i],
            at(other_core),
        )

    forward(0)
    pass_detour(1)
    forward(1)
    cg_row(0)
    cg_row(1)
    send_halo(cg3, cg_halo, ch_send, ch_recv)
    forward(2)
    take_halo(act3, act_halo, ah_send, ah_recv)

    def conv_body(i, _):
        conv[pl.ds(i * BLOCK, BLOCK), :] = convolve(act3, wsp, i).astype(BF16)
        return 0

    lax.fori_loop(0, PIXELS // BLOCK, conv_body, 0)
    forward(3)

    def turn_conv(i, _):
        src = pl.ds(pl.multiple_of(i * 128, 128), 128)
        convt[:, src] = conv[src, :].T
        return 0

    lax.fori_loop(0, PIXELS // 128, turn_conv, 0)
    cg_row(2)
    forward(4)
    cg_row(3)
    drain(stat_a, 8, low, low_of, sa_send, sa_recv)
    drain(stat_b, 16, high, high_of, sb_send, sb_recv)
    for c in halo_copies(act3, act_halo, ah_send, ah_recv):
        c.wait_send()
    forward(5)
    cg_row(4)
    temporal_half(0)
    for dy in range(3):
        spatial_half(0, dy)
    forward(6)
    cg_row(5)
    forward(7)
    cg_row(6)
    take_halo(cg3, cg_halo, ch_send, ch_recv)
    cg_row(7)
    temporal_half(1)
    core_copy(3).start()
    for dy in PART_ORDER[1:]:
        spatial_half(1, dy)
        core_copy(dy).start()

    def back_block(i, carry):
        rows = pl.ds(i * BLOCK, BLOCK)
        xhat, pre, sigma = normalize(rows)
        v = convolve(cg3, wspt, i) * sigma * (1.0 + pre * (1.0 - sigma))
        pre_grad[rows, :] = v
        a, b = carry
        a = a + jnp.sum(v.reshape(BLOCK // 8, 8, CHANNELS), axis=0)
        b = b + jnp.sum((v * xhat).reshape(BLOCK // 8, 8, CHANNELS), axis=0)
        return a, b

    def first_axis(p):
        return ((x, at_x), (y, at_y))[p // 2]

    def second_axis(p):
        return ((y, at_y), (x, at_x))[p // 2]

    def loop3(me, body):
        def step(j, _):
            body(lax.rem(me + j, 4))
            return 0

        lax.fori_loop(1, 4, step, 0)

    def s1_copy(p, o):
        me, target = first_axis(p)
        return copy(
            part.at[core, pl.ds(p * PART + o * QUARTER, QUARTER)], in1.at[p, me],
            s1_send.at[p, o], s1_recv.at[p, me], target(o),
        )

    def s1_arrived(p, o):
        _, target = first_axis(p)
        return copy(in1.at[p, o], in1.at[p, o], s1_send.at[p, o], s1_recv.at[p, o], target(o))

    def s2_copy(p, o):
        me, target = second_axis(p)
        return copy(
            mid.at[p, pl.ds(o * SHARD, SHARD)], in2.at[p, me],
            s2_send.at[p, o], s2_recv.at[p, me], target(o),
        )

    def s2_arrived(p, o):
        _, target = second_axis(p)
        return copy(in2.at[p, o], in2.at[p, o], s2_send.at[p, o], s2_recv.at[p, o], target(o))

    def add_core(p):
        core_copy(p).wait_recv()
        rows = pl.ds(p * PART, PART)
        part[core, rows, :] = part[core, rows, :] + core_in[rows, :]
        loop3(first_axis(p)[0], lambda o: s1_copy(p, o).start())

    sums = (zero8, zero8)
    for i, p in enumerate(PART_ORDER):
        sums = back_block(i, sums)
        add_core(p)
    a, b = sums
    back_a[low] = pack_rows(jnp.sum(a, axis=0, keepdims=True), jnp.sum(b, axis=0, keepdims=True))
    exchange(back_a, 8, low, low_of, ba_send, ba_recv)

    def s1_finish(p):
        me, _ = first_axis(p)
        loop3(me, lambda o: s1_arrived(p, o).wait_recv())
        total = part[core, pl.ds(p * PART + me * QUARTER, QUARTER), :]
        for j in range(1, 4):
            total = total + in1[p, lax.rem(me + j, 4)]
        mid[p] = total
        loop3(second_axis(p)[0], lambda o: s2_copy(p, o).start())

    def s3_copy(o, slot):
        return copy(mid2.at[o // 2], in3.at[slot], s3_send.at[o], s3_recv.at[slot], at_z(o))

    def s2_finish(p):
        me, _ = second_axis(p)
        loop3(me, lambda o: s2_arrived(p, o).wait_recv())
        total = mid[p, pl.ds(me * SHARD, SHARD), :]
        for j in range(1, 4):
            total = total + in2[p, lax.rem(me + j, 4)]
        mid2[p] = total
        for o in (2 * p, 2 * p + 1):
            @pl.when(z != o)
            def send_shard():
                s3_copy(o, z).start()

    for k in range(8):
        near_copy(k, True).wait_send()
    for k in range(6):
        far_copy(k).wait_send()
    for i in range(2):
        leg1_copy(i).wait_send()
        leg2_copy(i).wait_send()
    for c in halo_copies(cg3, cg_halo, ch_send, ch_recv):
        c.wait_send()

    for p in PART_ORDER:
        s1_finish(p)

    for p in PART_ORDER:
        s2_finish(p)

    back_b[high] = collect(back_a, 8, low, low_of, ba_send, ba_recv)
    exchange(back_b, 16, high, high_of, bb_send, bb_recv)

    for p in PART_ORDER:
        core_copy(p).wait_send()
        loop3(first_axis(p)[0], lambda o: s1_copy(p, o).wait_send())
    drain(back_a, 8, low, low_of, ba_send, ba_recv)

    def quarter_at(p, first):
        return pl.multiple_of(p * PART + QUARTER * first, QUARTER)

    def shard_at(p, first, second):
        return pl.multiple_of(p * PART + QUARTER * first + SHARD * second, SHARD)

    def own_shard(p):
        return full.at[core, pl.ds(shard_at(p, first_axis(p)[0], second_axis(p)[0]), SHARD)]

    def g3_copy(p, o):
        rows = own_shard(p)
        return copy(rows, rows, g3_send.at[o], g3_recv.at[p], at_zh(o))

    def g2_copy(p, o, sender):
        rows = full.at[core, pl.ds(shard_at(p, first_axis(p)[0], sender), SHARD)]
        return copy(rows, rows, g2_send.at[p, o], g2_recv.at[p, sender], second_axis(p)[1](o))

    def g1_copy(p, o, sender):
        rows = full.at[core, pl.ds(quarter_at(p, sender), QUARTER)]
        return copy(rows, rows, g1_send.at[p, o], g1_recv.at[p, sender], first_axis(p)[1](o))

    def to_core(p, half):
        rows = full.at[half, pl.ds(p * PART, PART)]
        return copy(rows, rows, gc_send.at[p], gc_recv.at[p], at(other_core))

    def store_params(p, half, slot):
        rows = pl.ds(p * PART, PART)
        return pltpu.make_async_copy(
            full.at[half, rows], params_out.at[half, rows], store_sem.at[1 + slot * PARTS + p]
        )

    for p in PART_ORDER:
        @pl.when(zh == p)
        def finish_part():
            in3[z] = mid2[p]

            def arrived(j, _):
                o = lax.rem(z + j, 8)
                copy(in3.at[o], in3.at[o], s3_send.at[o], s3_recv.at[o], at_z(o)).wait_recv()
                return 0

            lax.fori_loop(1, 8, arrived, 0)
            total = in3[0]
            for o in range(1, 8):
                total = total + in3[o]
            where = pl.ds(shard_at(p, first_axis(p)[0], second_axis(p)[0]), SHARD)
            full[core, where, :] = (total * SCALE).astype(BF16)
            loop3(zh, lambda o: g3_copy(p, o).start())

    for p in PART_ORDER:
        @pl.when(zh != p)
        def take_part():
            g3_copy(p, zh + 1 - 2 * lax.rem(zh, 2)).wait_recv()

        me, _ = second_axis(p)
        loop3(me, lambda o: g2_copy(p, o, me).start())

    for p in PART_ORDER:
        loop3(second_axis(p)[0], lambda o: s2_copy(p, o).wait_send())

    for p in PART_ORDER:
        loop3(second_axis(p)[0], lambda o: g2_copy(p, o, o).wait_recv())
        me, _ = first_axis(p)
        loop3(me, lambda o: g1_copy(p, o, me).start())

    sums = collect(back_b, 16, high, high_of, bb_send, bb_recv)
    clip_sums[clip] = sums
    clip_copy = copy(
        clip_sums.at[clip], clip_sums.at[clip], clip_sem.at[0], clip_sem.at[1], (1 - clip, seq)
    )
    clip_copy.start()
    norm_sums = group_sum(sums * gain) * (1.0 / COUNT)
    m1 = norm_sums[0:1]
    m2 = norm_sums[1:2]

    def out_body(i, _):
        rows = pl.ds(i * COLS, COLS)
        xhat = (xv[rows, :].astype(F32) - mean) * rstd
        v = rstd * (pre_grad[rows, :] * gain - m1 - xhat * m2)
        grad_v[rows, :] = (cots[0, rows, :].astype(F32) + v).astype(BF16)
        return 0

    lax.fori_loop(0, ROWS_DEV, out_body, 0)
    store_grad = pltpu.make_async_copy(grad_v, grad_out, store_sem.at[0])
    store_grad.start()

    def s3_sent(j, _):
        s3_copy(lax.rem(z + j, 8), z).wait_send()
        return 0

    lax.fori_loop(1, 8, s3_sent, 0)
    drain(back_b, 16, high, high_of, bb_send, bb_recv)
    for p in PART_ORDER:
        @pl.when(zh == p)
        def sent_part():
            loop3(zh, lambda o: g3_copy(p, o).wait_send())

        loop3(second_axis(p)[0], lambda o: g2_copy(p, o, second_axis(p)[0]).wait_send())

    for p in PART_ORDER:
        loop3(first_axis(p)[0], lambda o: g1_copy(p, o, o).wait_recv())
        to_core(p, core).start()
        store_params(p, core, 0).start()

    for p in PART_ORDER:
        loop3(first_axis(p)[0], lambda o: g1_copy(p, o, first_axis(p)[0]).wait_send())

    for p in PART_ORDER:
        to_core(p, 1 - core).wait_recv()
        store_params(p, 1 - core, 1).start()
    copy(
        clip_sums.at[1 - clip], clip_sums.at[1 - clip], clip_sem.at[0], clip_sem.at[1],
        (1 - clip, seq),
    ).wait_recv()
    sums_v[...] = (clip_sums[0] + clip_sums[1]) * SCALE
    store_sums = pltpu.make_async_copy(sums_v, sums_out, store_sem.at[1 + 2 * PARTS])
    store_sums.start()

    clip_copy.wait_send()
    store_grad.wait()
    store_sums.wait()
    for p in PART_ORDER:
        to_core(p, core).wait_send()
        store_params(p, core, 0).wait()
        store_params(p, 1 - core, 1).wait()


def finish_kernel(
    grad, params, sums, grad_out, spatial, temporal, gain_out, bias_out,
    grad_v, params_v, out_v, sums_v, bias_v, gain_v, sem,
):
    load_grad = pltpu.make_async_copy(grad, grad_v, sem.at[0])
    store_grad = pltpu.make_async_copy(grad_v, grad_out, sem.at[9])

    def load(i):
        taps = pl.ds(3 * i, 3)
        return pltpu.make_async_copy(params.at[:, taps], params_v.at[:, taps], sem.at[1 + i])

    def store(i):
        target = spatial.at[pl.ds(3 * i, 3)] if i < 3 else temporal
        return pltpu.make_async_copy(out_v.at[pl.ds(3 * i, 3)], target, sem.at[5 + i])

    for i in range(4):
        load(i).start()
    load_grad.start()
    load_sums = pltpu.make_async_copy(sums, sums_v, sem.at[10])
    load_sums.start()
    store_bias = pltpu.make_async_copy(bias_v, bias_out, sem.at[11])
    store_gain = pltpu.make_async_copy(gain_v, gain_out, sem.at[12])
    for i in range(4):
        load(i).wait()
        for half in range(2):
            out_v[3 * i : 3 * i + 3, :, half * 128 : (half + 1) * 128] = params_v[
                half, 3 * i : 3 * i + 3
            ].astype(F32)
        store(i).start()
    load_grad.wait()
    store_grad.start()
    load_sums.wait()
    bias_v[...] = sums_v[0]
    gain_v[...] = sums_v[1]
    store_bias.start()
    store_gain.start()
    store_grad.wait()
    store_bias.wait()
    store_gain.wait()
    for i in range(4):
        store(i).wait()


def local(block_input, cotangent, group_norm_gain, group_norm_bias, w_spatial, w_temporal):
    any_space = pl.BlockSpec(memory_space=pl.ANY)
    dma = pltpu.SemaphoreType.DMA
    scratch = [
        pltpu.VMEM((PIXELS, CHANNELS), BF16),
        pltpu.VMEM((3, PIXELS, CHANNELS), BF16),
        pltpu.VMEM((PADDED, 3 * CHANNELS), BF16),
        pltpu.VMEM((PADDED, 3 * CHANNELS), BF16),
        pltpu.VMEM((PIXELS, CHANNELS), BF16),
        pltpu.VMEM((CHANNELS, PIXELS), BF16),
        pltpu.VMEM((9 * CHANNELS, CHANNELS), BF16),
        pltpu.VMEM((9 * CHANNELS, CHANNELS), BF16),
        pltpu.VMEM((3, CHANNELS, CHANNELS), BF16),
        pltpu.VMEM((3, CHANNELS, CHANNELS), BF16),
        pltpu.VMEM((PIXELS, CHANNELS), F32),
        pltpu.VMEM((2, COLS, CHANNELS), BF16),
        pltpu.VMEM((2, COLS, CHANNELS), BF16),
        pltpu.VMEM((8, 8, CHANNELS), F32),
        pltpu.VMEM((16, 8, CHANNELS), F32),
        pltpu.VMEM((8, 8, CHANNELS), F32),
        pltpu.VMEM((16, 8, CHANNELS), F32),
        pltpu.VMEM((2, 8, CHANNELS), F32),
        pltpu.VMEM((2, HALF_ROWS, 128), F32),
        pltpu.VMEM((HALF_ROWS, 128), F32),
        pltpu.VMEM((PARTS, 4, QUARTER, 128), F32),
        pltpu.VMEM((PARTS, QUARTER, 128), F32),
        pltpu.VMEM((PARTS, 4, SHARD, 128), F32),
        pltpu.VMEM((PARTS, SHARD, 128), F32),
        pltpu.VMEM((8, SHARD, 128), F32),
        pltpu.VMEM((2, HALF_ROWS, 128), BF16),
        pltpu.VMEM((PIXELS, CHANNELS), BF16),
        pltpu.VMEM((2, COLS, CHANNELS), BF16),
        pltpu.VMEM((2, 1, CHANNELS), F32),
        pltpu.VMEM((8, CHANNELS), F32),
        dma((6,)), dma((2 + 2 * PARTS,)),
        dma((8,)), dma((8,)), dma((8,)), dma((8,)),
        dma((2,)), dma((2,)), dma((2,)),
        dma((2,)), dma((2,)), dma((2,)), dma((2,)),
        dma((8,)), dma((8,)), dma((16,)), dma((16,)),
        dma((8,)), dma((8,)), dma((16,)), dma((16,)),
        dma((2,)),
        dma((4,)), dma((4,)),
        dma((4, 4)), dma((4, 4)), dma((4, 4)), dma((4, 4)),
        dma((8,)), dma((8,)),
        dma((4,)), dma((4,)), dma((4, 4)), dma((4, 4)), dma((4, 4)), dma((4, 4)),
        dma((4,)), dma((4,)),
    ]
    grad, params, sums = pl.pallas_call(
        kernel,
        out_shape=(
            jax.ShapeDtypeStruct((PIXELS, CHANNELS), BF16),
            jax.ShapeDtypeStruct((2, HALF_ROWS, 128), BF16),
            jax.ShapeDtypeStruct((8, CHANNELS), F32),
        ),
        in_specs=[any_space] * 6,
        out_specs=(any_space, any_space, any_space),
        scratch_shapes=scratch,
        compiler_params=pltpu.CompilerParams(
            collective_id=0, has_side_effects=True, vmem_limit_bytes=56 * 2**20
        ),
    )(
        block_input.reshape(PIXELS, CHANNELS),
        cotangent.reshape(PIXELS, CHANNELS),
        group_norm_gain.reshape(1, CHANNELS),
        group_norm_bias.reshape(1, CHANNELS),
        w_spatial.reshape(9 * CHANNELS, CHANNELS),
        w_temporal,
    )
    params = params.reshape(2, TAPS, CHANNELS, 128)
    grad, spatial, temporal, gain_grad, bias_grad = pl.pallas_call(
        finish_kernel,
        out_shape=(
            jax.ShapeDtypeStruct((PIXELS, CHANNELS), BF16),
            jax.ShapeDtypeStruct((9, CHANNELS, CHANNELS), F32),
            jax.ShapeDtypeStruct((3, CHANNELS, CHANNELS), F32),
            jax.ShapeDtypeStruct((CHANNELS,), F32),
            jax.ShapeDtypeStruct((CHANNELS,), F32),
        ),
        in_specs=[any_space] * 3,
        out_specs=(any_space,) * 5,
        scratch_shapes=[
            pltpu.VMEM((PIXELS, CHANNELS), BF16),
            pltpu.VMEM((2, TAPS, CHANNELS, 128), BF16),
            pltpu.VMEM((TAPS, CHANNELS, CHANNELS), F32),
            pltpu.VMEM((8, CHANNELS), F32),
            pltpu.VMEM((CHANNELS,), F32),
            pltpu.VMEM((CHANNELS,), F32),
            dma((13,)),
        ],
        compiler_params=pltpu.CompilerParams(vmem_limit_bytes=60 * 2**20),
    )(grad, params, sums)
    return (
        grad.reshape(1, ROWS_DEV, COLS, CHANNELS),
        spatial,
        temporal,
        gain_grad,
        bias_grad,
    )


def solution(mesh):
    return jax.shard_map(
        local,
        mesh=mesh,
        in_specs=(P("dp", "seq", None, None), P("dp", "seq", None, None), P(), P(), P(), P()),
        out_specs=(P("dp", "seq", None, None), P(), P(), P(), P()),
        check_vma=False,
    )
```

```python
import math

import jax
import jax.numpy as jnp
from jax import lax
from jax.experimental import pallas as pl
from jax.experimental.pallas import tpu as pltpu
from jax.sharding import PartitionSpec as P

F32 = jnp.float32
BF16 = jnp.bfloat16
MESH = pl.DeviceIdType.MESH

CHANNELS = 256
GROUP = 8
ROWS_DEV = 8
COLS = 160
PIXELS = ROWS_DEV * COLS
PADDED = PIXELS + 2 * COLS
SEQ = 128
FRAMES = 32
EPS = 1e-06
COUNT = FRAMES * 32 * COLS * GROUP
SCALE = 1.0 / math.sqrt(2 * FRAMES * 32 * COLS)

ORDER = (0, 7, 1, 2, 3, 4, 5, 6)
BLOCK = 2 * COLS

TAPS = 12
HALF_ROWS = TAPS * CHANNELS
PARTS = 4
PART = HALF_ROWS // PARTS
QUARTER = PART // 4
SHARD = QUARTER // 4
PART_ORDER = (3, 0, 2, 1)


def kernel(
    x_hbm, g_hbm, gain_hbm, bias_hbm, wsp_hbm, wt_hbm,
    grad_out, params_out, sums_out,
    xv, cots, act3, cg3, conv, convt, wsp, wspt, wt, wtt, pre_grad,
    act_halo, cg_halo, stat_a, stat_b, back_a, back_b, clip_sums,
    part, core_in, in1, mid, in2, mid2, in3, full, grad_v, passing, affine, sums_v,
    load_sem, store_sem, far_send, far_recv, near_send, near_recv, leg1_send, leg1_recv, leg2_send,
    ah_send, ah_recv, ch_send, ch_recv,
    sa_send, sa_recv, sb_send, sb_recv, ba_send, ba_recv, bb_send, bb_recv, clip_sem,
    core_send, core_recv, s1_send, s1_recv, s2_send, s2_recv, s3_send, s3_recv,
    g3_send, g3_recv, g2_send, g2_recv, g1_send, g1_recv, gc_send, gc_recv,
):
    clip = lax.axis_index("dp")
    seq = lax.axis_index("seq")
    core = lax.rem(seq, 2)
    x = lax.rem(seq // 2, 4)
    zh = lax.rem(seq // 8, 4)
    y = seq // 32
    low = lax.rem(seq, 8)
    high = seq // 8
    z = zh * 2 + clip
    slab = lax.rem(seq + 2, SEQ)
    place = lax.rem(slab, 4)
    frame = slab // 4

    def at(s):
        return (clip, s)

    def at_x(o):
        return (clip, seq + 2 * (o - x))

    def at_y(o):
        return (clip, seq + 32 * (o - y))

    def at_zh(o):
        return (clip, seq + 8 * (o - zh))

    def at_z(o):
        return (lax.rem(o, 2), seq + 8 * (o // 2 - zh))

    up = lax.rem(seq + 1, SEQ)
    down = lax.rem(seq + SEQ - 1, SEQ)
    far_to = lax.rem(seq + SEQ - 8, SEQ)
    far_from = lax.rem(seq + 8, SEQ)
    other_core = seq + 1 - 2 * core
    x_high = x // 2
    near_to = seq + 4 - 8 * x_high

    def copy(src, dst, send_sem, recv_sem, device):
        return pltpu.make_async_remote_copy(
            src_ref=src, dst_ref=dst, send_sem=send_sem, recv_sem=recv_sem,
            device_id=device, device_id_type=MESH,
        )

    load_x = pltpu.make_async_copy(x_hbm, xv, load_sem.at[0])
    load_g = pltpu.make_async_copy(g_hbm, cots.at[0], load_sem.at[1])
    load_wsp = pltpu.make_async_copy(wsp_hbm, wsp, load_sem.at[2])
    load_wt = pltpu.make_async_copy(wt_hbm, wt, load_sem.at[3])
    load_x.start()
    load_g.start()
    load_wsp.start()
    load_wt.start()
    load_gain = pltpu.make_async_copy(gain_hbm, affine.at[0], load_sem.at[4])
    load_bias = pltpu.make_async_copy(bias_hbm, affine.at[1], load_sem.at[5])
    load_gain.start()
    load_bias.start()

    barrier = pltpu.get_barrier_semaphore()

    def greet(device):
        pl.semaphore_signal(barrier, inc=1, device_id=device, device_id_type=MESH)

    def greet_low(j, _):
        greet(at(seq - low + lax.rem(low + j, 8)))
        return 0

    def greet_high(j, _):
        greet(at(lax.rem(high + j, 16) * 8 + low))
        return 0

    def greet_z(j, _):
        greet((1 - clip, seq + 8 * (j - zh)))
        return 0

    z_up = lax.rem(z + 3, 8)
    z_down = lax.rem(z + 5, 8)

    def wrapped(source_z):
        return 1 - jnp.minimum(source_z // 2, 1)

    def at_zy(zz, yy):
        return (lax.rem(zz, 2), seq + 8 * (zz // 2 - zh) + 32 * (yy - y))

    leg1_to = at_zy(z_up, y)
    leg2_to = at_zy(z_up, lax.rem(y + 4 - wrapped(z_down), 4))
    leg2_from = at_zy(z_down, lax.rem(y + wrapped(lax.rem(z + 2, 8)), 4))

    lax.fori_loop(1, 16, greet_high, 0)
    lax.fori_loop(0, 4, greet_z, 0)
    greet(leg2_from)
    greet(at(up))
    greet(at(down))
    lax.fori_loop(1, 8, greet_low, 0)

    def far_copy(k):
        rows = pl.ds(ORDER[k] * COLS, COLS)
        return copy(
            g_hbm.at[rows], cots.at[2, rows], far_send.at[k], far_recv.at[k], at(far_to)
        )

    def near_copy(k, own):
        rows = pl.ds(ORDER[k] * COLS, COLS)
        return copy(
            (g_hbm if own else cots.at[2]).at[rows], cots.at[1, rows],
            near_send.at[k], near_recv.at[k], at(near_to),
        )

    def leg1_copy(i):
        rows = pl.ds(ORDER[6 + i] * COLS, COLS)
        return copy(g_hbm.at[rows], passing.at[i], leg1_send.at[i], leg1_recv.at[i], leg1_to)

    def leg2_copy(i):
        rows = pl.ds(ORDER[6 + i] * COLS, COLS)
        return copy(
            passing.at[i], cots.at[2, rows], leg2_send.at[i], far_recv.at[6 + i], leg2_to
        )

    def pass_detour(i):
        leg1_copy(i).wait_recv()
        leg2_copy(i).start()

    def exchange(buf, n, me, target, send_sem, recv_sem):
        def body(j, _):
            o = lax.rem(me + j, n)
            copy(buf.at[me], buf.at[me], send_sem.at[o], recv_sem.at[me], at(target(o))).start()
            return 0

        lax.fori_loop(1, n, body, 0)

    def collect(buf, n, me, target, send_sem, recv_sem):
        def body(j, _):
            o = lax.rem(me + j, n)
            arrived = copy(buf.at[o], buf.at[o], send_sem.at[o], recv_sem.at[o], at(target(o)))
            arrived.wait_recv()
            return 0

        lax.fori_loop(1, n, body, 0)
        total = buf[0]
        for o in range(1, n):
            total = total + buf[o]
        return total

    def drain(buf, n, me, target, send_sem, recv_sem):
        def body(j, _):
            o = lax.rem(me + j, n)
            copy(buf.at[me], buf.at[me], send_sem.at[o], recv_sem.at[me], at(target(o))).wait_send()
            return 0

        lax.fori_loop(1, n, body, 0)

    def low_of(o):
        return seq - low + o

    def high_of(o):
        return o * 8 + low

    row_id = lax.broadcasted_iota(jnp.int32, (2, CHANNELS), 0)

    def pack_rows(first, second):
        return jnp.where(row_id == 0, first, second)

    group_a = lax.shift_right_logical(lax.broadcasted_iota(jnp.int32, (CHANNELS, CHANNELS), 0), 3)
    group_b = lax.shift_right_logical(lax.broadcasted_iota(jnp.int32, (CHANNELS, CHANNELS), 1), 3)
    same_group = jnp.where(group_a == group_b, 1.0, 0.0).astype(BF16)

    def group_sum(v):
        total = jnp.zeros_like(v)
        rest = v
        for _ in range(3):
            piece = rest.astype(BF16)
            rest = rest - piece.astype(F32)
            total = total + jnp.dot(piece, same_group, preferred_element_type=F32)
        return total

    load_x.wait()

    def stat_body(i, carry):
        a, b = carry
        blk = xv[pl.ds(i * COLS, COLS), :].astype(F32).reshape(COLS // 8, 8, CHANNELS)
        return a + jnp.sum(blk, axis=0), b + jnp.sum(blk * blk, axis=0)

    zero8 = jnp.zeros((8, CHANNELS), F32)
    a, b = lax.fori_loop(0, ROWS_DEV, stat_body, (zero8, zero8))
    stat_a[low] = pack_rows(jnp.sum(a, axis=0, keepdims=True), jnp.sum(b, axis=0, keepdims=True))
    pl.semaphore_wait(barrier, 15 + 4 + 1 + 2 + 7)

    exchange(stat_a, 8, low, low_of, sa_send, sa_recv)
    leg1_copy(0).start()
    far_copy(0).start()
    leg1_copy(1).start()

    @pl.when(x_high == 1)
    def send_own():
        for k in range(8):
            near_copy(k, True).start()

    load_wt.wait()
    load_wsp.wait()
    for k in range(3):
        wtt[k] = wt[k].T

    def turn_weight(i, _):
        wspt[pl.ds(i * CHANNELS, CHANNELS), :] = wsp[pl.ds((8 - i) * CHANNELS, CHANNELS), :].T
        return 0

    lax.fori_loop(0, 9, turn_weight, 0)

    stat_b[high] = collect(stat_a, 8, low, low_of, sa_send, sa_recv)
    exchange(stat_b, 16, high, high_of, sb_send, sb_recv)
    for k in (1, 2, 3):
        far_copy(k).start()
    load_g.wait()
    moments = group_sum(collect(stat_b, 16, high, high_of, sb_send, sb_recv)) * (1.0 / COUNT)
    mean = moments[0:1]
    rstd = lax.rsqrt(moments[1:2] - mean * mean + EPS)
    load_gain.wait()
    load_bias.wait()
    gain = affine[0]
    bias = affine[1]

    def forward(k):
        far_copy(k).wait_recv()

        @pl.when(x_high == 0)
        def pass_on():
            near_copy(k, False).start()


    col_id = lax.broadcasted_iota(jnp.int32, (COLS, CHANNELS), 0)

    def store_shifts(buf, padded_row, v):
        rows = pl.ds(padded_row * COLS, COLS)
        buf[rows, CHANNELS : 2 * CHANNELS] = v.astype(BF16)
        left = jnp.where(col_id == 0, 0.0, pltpu.roll(v, 1, 0))
        right = jnp.where(col_id == COLS - 1, 0.0, pltpu.roll(v, COLS - 1, 0))
        buf[rows, 0:CHANNELS] = left.astype(BF16)
        buf[rows, 2 * CHANNELS : 3 * CHANNELS] = right.astype(BF16)

    def normalize(rows):
        xhat = (xv[rows, :].astype(F32) - mean) * rstd
        pre = xhat * gain + bias
        return xhat, pre, jax.nn.sigmoid(pre)

    def act_row(r):
        _, pre, sigma = normalize(pl.ds(r * COLS, COLS))
        store_shifts(act3, r + 1, pre * sigma)

    middle = slice(CHANNELS, 2 * CHANNELS)

    def halo_copies(buf, halo, send_sem, recv_sem):
        first = copy(
            buf.at[pl.ds(COLS, COLS), middle], halo.at[1], send_sem.at[0], recv_sem.at[1], at(down)
        )
        last = copy(
            buf.at[pl.ds(PIXELS, COLS), middle], halo.at[0], send_sem.at[1], recv_sem.at[0], at(up)
        )
        return first, last

    def send_halo(buf, halo, send_sem, recv_sem):
        for c in halo_copies(buf, halo, send_sem, recv_sem):
            c.start()

    def take_halo(buf, halo, send_sem, recv_sem):
        for c in halo_copies(buf, halo, send_sem, recv_sem):
            c.wait_recv()
        keep_low = jnp.where(place > 0, 1.0, 0.0).astype(F32)
        keep_high = jnp.where(place < 3, 1.0, 0.0).astype(F32)
        store_shifts(buf, 0, halo[0].astype(F32) * keep_low)
        store_shifts(buf, ROWS_DEV + 1, halo[1].astype(F32) * keep_high)

    act_row(0)
    act_row(ROWS_DEV - 1)
    send_halo(act3, act_halo, ah_send, ah_recv)
    far_copy(4).start()
    far_copy(5).start()
    pass_detour(0)

    def act_body(r, _):
        act_row(r)
        return 0

    lax.fori_loop(1, ROWS_DEV - 1, act_body, 0)

    def convolve(buf, weights, i):
        total = None
        for dy in range(3):
            term = jnp.dot(
                buf[pl.ds(i * BLOCK + dy * COLS, BLOCK), :],
                weights[dy * 3 * CHANNELS : (dy + 1) * 3 * CHANNELS, :],
                preferred_element_type=F32,
            )
            total = term if total is None else total + term
        return total

    keep1 = jnp.where(frame < FRAMES - 1, 1.0, 0.0).astype(F32)
    keep2 = jnp.where(frame < FRAMES - 2, 1.0, 0.0).astype(F32)

    def cg_row(k):
        r = ORDER[k]
        near_copy(k, True).wait_recv()
        rows = pl.ds(r * COLS, COLS)
        total = jnp.dot(cots[0, rows, :], wtt[0], preferred_element_type=F32)
        total = total + keep1 * jnp.dot(cots[1, rows, :], wtt[1], preferred_element_type=F32)
        total = total + keep2 * jnp.dot(cots[2, rows, :], wtt[2], preferred_element_type=F32)
        store_shifts(cg3, r + 1, total.astype(BF16).astype(F32))

    def put(first_row, v, add):
        rows = pl.ds(first_row, v.shape[0])
        for half in range(2):
            w = v[:, half * 128 : (half + 1) * 128]
            part[half, rows, :] = part[half, rows, :] + w if add else w

    half_pixels = PIXELS // 2

    def temporal_half(h):
        pixels = slice(h * half_pixels, (h + 1) * half_pixels)
        for k, keep in enumerate((None, keep1, keep2)):
            v = jnp.dot(convt[:, pixels], cots[k, pixels, :], preferred_element_type=F32)
            put((9 + k) * CHANNELS, v if keep is None else v * keep, h > 0)

    def spatial_half(h, dy):
        begin = h * half_pixels
        v = lax.dot_general(
            act3[dy * COLS + begin : dy * COLS + begin + half_pixels, :],
            cg3[COLS + begin : COLS + begin + half_pixels, middle],
            (((0,), (0,)), ((), ())),
            preferred_element_type=F32,
        )
        put(dy * chunk_rows, v, h > 0)

    chunk_rows = PART

    def core_copy(i):
        rows = pl.ds(i * chunk_rows, chunk_rows)
        return copy(
            part.at[1 - core, rows], core_in.at[rows], core_send.at[i], core_recv.at[i],
            at(other_core),
        )

    forward(0)
    pass_detour(1)
    forward(1)
    forward(2)
    cg_row(0)
    cg_row(1)
    send_halo(cg3, cg_halo, ch_send, ch_recv)
    forward(3)
    take_halo(act3, act_halo, ah_send, ah_recv)

    def conv_body(i, _):
        conv[pl.ds(i * BLOCK, BLOCK), :] = convolve(act3, wsp, i).astype(BF16)
        return 0

    lax.fori_loop(0, PIXELS // BLOCK, conv_body, 0)
    forward(4)
    cg_row(2)

    def turn_conv(i, _):
        src = pl.ds(pl.multiple_of(i * 128, 128), 128)
        convt[:, src] = conv[src, :].T
        return 0

    lax.fori_loop(0, PIXELS // 128, turn_conv, 0)
    cg_row(3)
    forward(5)
    cg_row(4)
    forward(6)
    temporal_half(0)
    spatial_half(0, 0)
    forward(7)
    spatial_half(0, 1)
    spatial_half(0, 2)
    drain(stat_a, 8, low, low_of, sa_send, sa_recv)
    drain(stat_b, 16, high, high_of, sb_send, sb_recv)
    for c in halo_copies(act3, act_halo, ah_send, ah_recv):
        c.wait_send()
    cg_row(5)
    take_halo(cg3, cg_halo, ch_send, ch_recv)
    cg_row(6)
    cg_row(7)
    temporal_half(1)
    core_copy(3).start()
    for dy in PART_ORDER[1:]:
        spatial_half(1, dy)
        core_copy(dy).start()

    def back_block(i, carry):
        rows = pl.ds(i * BLOCK, BLOCK)
        xhat, pre, sigma = normalize(rows)
        v = convolve(cg3, wspt, i) * sigma * (1.0 + pre * (1.0 - sigma))
        pre_grad[rows, :] = v
        a, b = carry
        a = a + jnp.sum(v.reshape(BLOCK // 8, 8, CHANNELS), axis=0)
        b = b + jnp.sum((v * xhat).reshape(BLOCK // 8, 8, CHANNELS), axis=0)
        return a, b

    def first_axis(p):
        return ((x, at_x), (y, at_y))[p // 2]

    def second_axis(p):
        return ((y, at_y), (x, at_x))[p // 2]

    def loop3(me, body):
        def step(j, _):
            body(lax.rem(me + j, 4))
            return 0

        lax.fori_loop(1, 4, step, 0)

    def s1_copy(p, o):
        me, target = first_axis(p)
        return copy(
            part.at[core, pl.ds(p * PART + o * QUARTER, QUARTER)], in1.at[p, me],
            s1_send.at[p, o], s1_recv.at[p, me], target(o),
        )

    def s1_arrived(p, o):
        _, target = first_axis(p)
        return copy(in1.at[p, o], in1.at[p, o], s1_send.at[p, o], s1_recv.at[p, o], target(o))

    def s2_copy(p, o):
        me, target = second_axis(p)
        return copy(
            mid.at[p, pl.ds(o * SHARD, SHARD)], in2.at[p, me],
            s2_send.at[p, o], s2_recv.at[p, me], target(o),
        )

    def s2_arrived(p, o):
        _, target = second_axis(p)
        return copy(in2.at[p, o], in2.at[p, o], s2_send.at[p, o], s2_recv.at[p, o], target(o))

    def add_core(p):
        core_copy(p).wait_recv()
        rows = pl.ds(p * PART, PART)
        part[core, rows, :] = part[core, rows, :] + core_in[rows, :]
        loop3(first_axis(p)[0], lambda o: s1_copy(p, o).start())

    sums = (zero8, zero8)
    for i, p in enumerate(PART_ORDER):
        sums = back_block(i, sums)
        add_core(p)
    a, b = sums
    back_a[low] = pack_rows(jnp.sum(a, axis=0, keepdims=True), jnp.sum(b, axis=0, keepdims=True))
    exchange(back_a, 8, low, low_of, ba_send, ba_recv)

    def s1_finish(p):
        me, _ = first_axis(p)
        loop3(me, lambda o: s1_arrived(p, o).wait_recv())
        total = part[core, pl.ds(p * PART + me * QUARTER, QUARTER), :]
        for j in range(1, 4):
            total = total + in1[p, lax.rem(me + j, 4)]
        mid[p] = total
        loop3(second_axis(p)[0], lambda o: s2_copy(p, o).start())

    def s3_copy(o, slot):
        return copy(mid2.at[o // 2], in3.at[slot], s3_send.at[o], s3_recv.at[slot], at_z(o))

    def s2_finish(p):
        me, _ = second_axis(p)
        loop3(me, lambda o: s2_arrived(p, o).wait_recv())
        total = mid[p, pl.ds(me * SHARD, SHARD), :]
        for j in range(1, 4):
            total = total + in2[p, lax.rem(me + j, 4)]
        mid2[p] = total
        for o in (2 * p, 2 * p + 1):
            @pl.when(z != o)
            def send_shard():
                s3_copy(o, z).start()

    for k in range(8):
        near_copy(k, True).wait_send()
    for k in range(6):
        far_copy(k).wait_send()
    for i in range(2):
        leg1_copy(i).wait_send()
        leg2_copy(i).wait_send()
    for c in halo_copies(cg3, cg_halo, ch_send, ch_recv):
        c.wait_send()

    for p in PART_ORDER:
        s1_finish(p)

    for p in PART_ORDER:
        s2_finish(p)

    back_b[high] = collect(back_a, 8, low, low_of, ba_send, ba_recv)
    exchange(back_b, 16, high, high_of, bb_send, bb_recv)

    for p in PART_ORDER:
        core_copy(p).wait_send()
        loop3(first_axis(p)[0], lambda o: s1_copy(p, o).wait_send())
    drain(back_a, 8, low, low_of, ba_send, ba_recv)

    def quarter_at(p, first):
        return pl.multiple_of(p * PART + QUARTER * first, QUARTER)

    def shard_at(p, first, second):
        return pl.multiple_of(p * PART + QUARTER * first + SHARD * second, SHARD)

    def own_shard(p):
        return full.at[core, pl.ds(shard_at(p, first_axis(p)[0], second_axis(p)[0]), SHARD)]

    def g3_copy(p, o):
        rows = own_shard(p)
        return copy(rows, rows, g3_send.at[o], g3_recv.at[p], at_zh(o))

    def g2_copy(p, o, sender):
        rows = full.at[core, pl.ds(shard_at(p, first_axis(p)[0], sender), SHARD)]
        return copy(rows, rows, g2_send.at[p, o], g2_recv.at[p, sender], second_axis(p)[1](o))

    def g1_copy(p, o, sender):
        rows = full.at[core, pl.ds(quarter_at(p, sender), QUARTER)]
        return copy(rows, rows, g1_send.at[p, o], g1_recv.at[p, sender], first_axis(p)[1](o))

    def to_core(p, half):
        rows = full.at[half, pl.ds(p * PART, PART)]
        return copy(rows, rows, gc_send.at[p], gc_recv.at[p], at(other_core))

    def store_params(p, half, slot):
        rows = pl.ds(p * PART, PART)
        return pltpu.make_async_copy(
            full.at[half, rows], params_out.at[half, rows], store_sem.at[1 + slot * PARTS + p]
        )

    for p in PART_ORDER:
        @pl.when(zh == p)
        def finish_part():
            in3[z] = mid2[p]

            def arrived(j, _):
                o = lax.rem(z + j, 8)
                copy(in3.at[o], in3.at[o], s3_send.at[o], s3_recv.at[o], at_z(o)).wait_recv()
                return 0

            lax.fori_loop(1, 8, arrived, 0)
            total = in3[0]
            for o in range(1, 8):
                total = total + in3[o]
            where = pl.ds(shard_at(p, first_axis(p)[0], second_axis(p)[0]), SHARD)
            full[core, where, :] = (total * SCALE).astype(BF16)
            loop3(zh, lambda o: g3_copy(p, o).start())

    for p in PART_ORDER:
        @pl.when(zh != p)
        def take_part():
            g3_copy(p, zh + 1 - 2 * lax.rem(zh, 2)).wait_recv()

        me, _ = second_axis(p)
        loop3(me, lambda o: g2_copy(p, o, me).start())

    for p in PART_ORDER:
        loop3(second_axis(p)[0], lambda o: s2_copy(p, o).wait_send())

    for p in PART_ORDER:
        loop3(second_axis(p)[0], lambda o: g2_copy(p, o, o).wait_recv())
        me, _ = first_axis(p)
        loop3(me, lambda o: g1_copy(p, o, me).start())

    sums = collect(back_b, 16, high, high_of, bb_send, bb_recv)
    clip_sums[clip] = sums
    clip_copy = copy(
        clip_sums.at[clip], clip_sums.at[clip], clip_sem.at[0], clip_sem.at[1], (1 - clip, seq)
    )
    clip_copy.start()
    norm_sums = group_sum(sums * gain) * (1.0 / COUNT)
    m1 = norm_sums[0:1]
    m2 = norm_sums[1:2]

    def out_body(i, _):
        rows = pl.ds(i * COLS, COLS)
        xhat = (xv[rows, :].astype(F32) - mean) * rstd
        v = rstd * (pre_grad[rows, :] * gain - m1 - xhat * m2)
        grad_v[rows, :] = (cots[0, rows, :].astype(F32) + v).astype(BF16)
        return 0

    lax.fori_loop(0, ROWS_DEV, out_body, 0)
    store_grad = pltpu.make_async_copy(grad_v, grad_out, store_sem.at[0])
    store_grad.start()

    def s3_sent(j, _):
        s3_copy(lax.rem(z + j, 8), z).wait_send()
        return 0

    lax.fori_loop(1, 8, s3_sent, 0)
    drain(back_b, 16, high, high_of, bb_send, bb_recv)
    for p in PART_ORDER:
        @pl.when(zh == p)
        def sent_part():
            loop3(zh, lambda o: g3_copy(p, o).wait_send())

        loop3(second_axis(p)[0], lambda o: g2_copy(p, o, second_axis(p)[0]).wait_send())

    for p in PART_ORDER:
        loop3(first_axis(p)[0], lambda o: g1_copy(p, o, o).wait_recv())
        to_core(p, core).start()
        store_params(p, core, 0).start()

    for p in PART_ORDER:
        loop3(first_axis(p)[0], lambda o: g1_copy(p, o, first_axis(p)[0]).wait_send())

    for p in PART_ORDER:
        to_core(p, 1 - core).wait_recv()
        store_params(p, 1 - core, 1).start()
    copy(
        clip_sums.at[1 - clip], clip_sums.at[1 - clip], clip_sem.at[0], clip_sem.at[1],
        (1 - clip, seq),
    ).wait_recv()
    sums_v[...] = (clip_sums[0] + clip_sums[1]) * SCALE
    store_sums = pltpu.make_async_copy(sums_v, sums_out, store_sem.at[1 + 2 * PARTS])
    store_sums.start()

    clip_copy.wait_send()
    store_grad.wait()
    store_sums.wait()
    for p in PART_ORDER:
        to_core(p, core).wait_send()
        store_params(p, core, 0).wait()
        store_params(p, 1 - core, 1).wait()


def finish_kernel(
    grad, params, sums, grad_out, spatial, temporal, gain_out, bias_out,
    grad_v, params_v, out_v, sums_v, bias_v, gain_v, sem,
):
    load_grad = pltpu.make_async_copy(grad, grad_v, sem.at[0])
    store_grad = pltpu.make_async_copy(grad_v, grad_out, sem.at[9])

    def load(i):
        taps = pl.ds(3 * i, 3)
        return pltpu.make_async_copy(params.at[:, taps], params_v.at[:, taps], sem.at[1 + i])

    def store(i):
        target = spatial.at[pl.ds(3 * i, 3)] if i < 3 else temporal
        return pltpu.make_async_copy(out_v.at[pl.ds(3 * i, 3)], target, sem.at[5 + i])

    for i in range(4):
        load(i).start()
    load_grad.start()
    load_sums = pltpu.make_async_copy(sums, sums_v, sem.at[10])
    load_sums.start()
    store_bias = pltpu.make_async_copy(bias_v, bias_out, sem.at[11])
    store_gain = pltpu.make_async_copy(gain_v, gain_out, sem.at[12])
    for i in range(4):
        load(i).wait()
        for half in range(2):
            out_v[3 * i : 3 * i + 3, :, half * 128 : (half + 1) * 128] = params_v[
                half, 3 * i : 3 * i + 3
            ].astype(F32)
        store(i).start()
    load_grad.wait()
    store_grad.start()
    load_sums.wait()
    bias_v[...] = sums_v[0]
    gain_v[...] = sums_v[1]
    store_bias.start()
    store_gain.start()
    store_grad.wait()
    store_bias.wait()
    store_gain.wait()
    for i in range(4):
        store(i).wait()


def local(block_input, cotangent, group_norm_gain, group_norm_bias, w_spatial, w_temporal):
    any_space = pl.BlockSpec(memory_space=pl.ANY)
    dma = pltpu.SemaphoreType.DMA
    scratch = [
        pltpu.VMEM((PIXELS, CHANNELS), BF16),
        pltpu.VMEM((3, PIXELS, CHANNELS), BF16),
        pltpu.VMEM((PADDED, 3 * CHANNELS), BF16),
        pltpu.VMEM((PADDED, 3 * CHANNELS), BF16),
        pltpu.VMEM((PIXELS, CHANNELS), BF16),
        pltpu.VMEM((CHANNELS, PIXELS), BF16),
        pltpu.VMEM((9 * CHANNELS, CHANNELS), BF16),
        pltpu.VMEM((9 * CHANNELS, CHANNELS), BF16),
        pltpu.VMEM((3, CHANNELS, CHANNELS), BF16),
        pltpu.VMEM((3, CHANNELS, CHANNELS), BF16),
        pltpu.VMEM((PIXELS, CHANNELS), F32),
        pltpu.VMEM((2, COLS, CHANNELS), BF16),
        pltpu.VMEM((2, COLS, CHANNELS), BF16),
        pltpu.VMEM((8, 2, CHANNELS), F32),
        pltpu.VMEM((16, 2, CHANNELS), F32),
        pltpu.VMEM((8, 2, CHANNELS), F32),
        pltpu.VMEM((16, 2, CHANNELS), F32),
        pltpu.VMEM((2, 2, CHANNELS), F32),
        pltpu.VMEM((2, HALF_ROWS, 128), F32),
        pltpu.VMEM((HALF_ROWS, 128), F32),
        pltpu.VMEM((PARTS, 4, QUARTER, 128), F32),
        pltpu.VMEM((PARTS, QUARTER, 128), F32),
        pltpu.VMEM((PARTS, 4, SHARD, 128), F32),
        pltpu.VMEM((PARTS, SHARD, 128), F32),
        pltpu.VMEM((8, SHARD, 128), F32),
        pltpu.VMEM((2, HALF_ROWS, 128), BF16),
        pltpu.VMEM((PIXELS, CHANNELS), BF16),
        pltpu.VMEM((2, COLS, CHANNELS), BF16),
        pltpu.VMEM((2, 1, CHANNELS), F32),
        pltpu.VMEM((2, CHANNELS), F32),
        dma((6,)), dma((2 + 2 * PARTS,)),
        dma((8,)), dma((8,)), dma((8,)), dma((8,)),
        dma((2,)), dma((2,)), dma((2,)),
        dma((2,)), dma((2,)), dma((2,)), dma((2,)),
        dma((8,)), dma((8,)), dma((16,)), dma((16,)),
        dma((8,)), dma((8,)), dma((16,)), dma((16,)),
        dma((2,)),
        dma((4,)), dma((4,)),
        dma((4, 4)), dma((4, 4)), dma((4, 4)), dma((4, 4)),
        dma((8,)), dma((8,)),
        dma((4,)), dma((4,)), dma((4, 4)), dma((4, 4)), dma((4, 4)), dma((4, 4)),
        dma((4,)), dma((4,)),
    ]
    grad, params, sums = pl.pallas_call(
        kernel,
        out_shape=(
            jax.ShapeDtypeStruct((PIXELS, CHANNELS), BF16),
            jax.ShapeDtypeStruct((2, HALF_ROWS, 128), BF16),
            jax.ShapeDtypeStruct((2, CHANNELS), F32),
        ),
        in_specs=[any_space] * 6,
        out_specs=(any_space, any_space, any_space),
        scratch_shapes=scratch,
        compiler_params=pltpu.CompilerParams(
            collective_id=0, has_side_effects=True, vmem_limit_bytes=56 * 2**20
        ),
    )(
        block_input.reshape(PIXELS, CHANNELS),
        cotangent.reshape(PIXELS, CHANNELS),
        group_norm_gain.reshape(1, CHANNELS),
        group_norm_bias.reshape(1, CHANNELS),
        w_spatial.reshape(9 * CHANNELS, CHANNELS),
        w_temporal,
    )
    params = params.reshape(2, TAPS, CHANNELS, 128)
    grad, spatial, temporal, gain_grad, bias_grad = pl.pallas_call(
        finish_kernel,
        out_shape=(
            jax.ShapeDtypeStruct((PIXELS, CHANNELS), BF16),
            jax.ShapeDtypeStruct((9, CHANNELS, CHANNELS), F32),
            jax.ShapeDtypeStruct((3, CHANNELS, CHANNELS), F32),
            jax.ShapeDtypeStruct((CHANNELS,), F32),
            jax.ShapeDtypeStruct((CHANNELS,), F32),
        ),
        in_specs=[any_space] * 3,
        out_specs=(any_space,) * 5,
        scratch_shapes=[
            pltpu.VMEM((PIXELS, CHANNELS), BF16),
            pltpu.VMEM((2, TAPS, CHANNELS, 128), BF16),
            pltpu.VMEM((TAPS, CHANNELS, CHANNELS), F32),
            pltpu.VMEM((2, CHANNELS), F32),
            pltpu.VMEM((CHANNELS,), F32),
            pltpu.VMEM((CHANNELS,), F32),
            dma((13,)),
        ],
        compiler_params=pltpu.CompilerParams(vmem_limit_bytes=60 * 2**20),
    )(grad, params, sums)
    return (
        grad.reshape(1, ROWS_DEV, COLS, CHANNELS),
        spatial,
        temporal,
        gain_grad,
        bias_grad,
    )


def solution(mesh):
    return jax.shard_map(
        local,
        mesh=mesh,
        in_specs=(P("dp", "seq", None, None), P("dp", "seq", None, None), P(), P(), P(), P()),
        out_specs=(P("dp", "seq", None, None), P(), P(), P(), P()),
        check_vma=False,
    )
```

```python
import math

import jax
import jax.numpy as jnp
from jax import lax
from jax.experimental import pallas as pl
from jax.experimental.pallas import tpu as pltpu
from jax.sharding import PartitionSpec as P

F32 = jnp.float32
BF16 = jnp.bfloat16
MESH = pl.DeviceIdType.MESH

CHANNELS = 256
GROUP = 8
ROWS_DEV = 8
COLS = 160
PIXELS = ROWS_DEV * COLS
PADDED = PIXELS + 2 * COLS
SEQ = 128
FRAMES = 32
EPS = 1e-06
COUNT = FRAMES * 32 * COLS * GROUP
SCALE = 1.0 / math.sqrt(2 * FRAMES * 32 * COLS)

ORDER = (0, 7, 1, 2, 3, 4, 5, 6)
BLOCK = 2 * COLS

TAPS = 12
HALF_ROWS = TAPS * CHANNELS
PARTS = 4
PART = HALF_ROWS // PARTS
QUARTER = PART // 4
SHARD = QUARTER // 4
PART_ORDER = (3, 0, 2, 1)


def kernel(
    x_hbm, g_hbm, gain_hbm, bias_hbm, wsp_hbm, wt_hbm,
    grad_out, params_out, sums_out,
    xv, cots, act3, cg3, conv, convt, wsp, wspt, wt, wtt, pre_grad,
    act_halo, cg_halo, stat_a, stat_b, back_a, back_b, clip_sums,
    part, core_in, in1, mid, in2, mid2, in3, full, grad_v, passing, affine, sums_v,
    load_sem, store_sem, far_send, far_recv, near_send, near_recv, leg1_send, leg1_recv, leg2_send,
    ah_send, ah_recv, ch_send, ch_recv,
    sa_send, sa_recv, sb_send, sb_recv, ba_send, ba_recv, bb_send, bb_recv, clip_sem,
    core_send, core_recv, s1_send, s1_recv, s2_send, s2_recv, s3_send, s3_recv,
    g3_send, g3_recv, g2_send, g2_recv, g1_send, g1_recv, gc_send, gc_recv,
):
    clip = lax.axis_index("dp")
    seq = lax.axis_index("seq")
    core = lax.rem(seq, 2)
    x = lax.rem(seq // 2, 4)
    zh = lax.rem(seq // 8, 4)
    y = seq // 32
    low = lax.rem(seq, 8)
    high = seq // 8
    z = zh * 2 + clip
    slab = lax.rem(seq + 2, SEQ)
    place = lax.rem(slab, 4)
    frame = slab // 4

    def at(s):
        return (clip, s)

    def at_x(o):
        return (clip, seq + 2 * (o - x))

    def at_y(o):
        return (clip, seq + 32 * (o - y))

    def at_zh(o):
        return (clip, seq + 8 * (o - zh))

    def at_z(o):
        return (lax.rem(o, 2), seq + 8 * (o // 2 - zh))

    up = lax.rem(seq + 1, SEQ)
    down = lax.rem(seq + SEQ - 1, SEQ)
    far_to = lax.rem(seq + SEQ - 8, SEQ)
    far_from = lax.rem(seq + 8, SEQ)
    other_core = seq + 1 - 2 * core
    x_high = x // 2
    near_to = seq + 4 - 8 * x_high

    def copy(src, dst, send_sem, recv_sem, device):
        return pltpu.make_async_remote_copy(
            src_ref=src, dst_ref=dst, send_sem=send_sem, recv_sem=recv_sem,
            device_id=device, device_id_type=MESH,
        )

    load_x = pltpu.make_async_copy(x_hbm, xv, load_sem.at[0])
    load_g = pltpu.make_async_copy(g_hbm, cots.at[0], load_sem.at[1])
    load_wsp = pltpu.make_async_copy(wsp_hbm, wsp, load_sem.at[2])
    load_wt = pltpu.make_async_copy(wt_hbm, wt, load_sem.at[3])
    load_x.start()
    load_g.start()
    load_wsp.start()
    load_wt.start()
    load_gain = pltpu.make_async_copy(gain_hbm, affine.at[0], load_sem.at[4])
    load_bias = pltpu.make_async_copy(bias_hbm, affine.at[1], load_sem.at[5])
    load_gain.start()
    load_bias.start()

    barrier = pltpu.get_barrier_semaphore()

    def greet(device):
        pl.semaphore_signal(barrier, inc=1, device_id=device, device_id_type=MESH)

    def greet_low(j, _):
        greet(at(seq - low + lax.rem(low + j, 8)))
        return 0

    def greet_high(j, _):
        greet(at(lax.rem(high + j, 16) * 8 + low))
        return 0

    def greet_z(j, _):
        greet((1 - clip, seq + 8 * (j - zh)))
        return 0

    z_up = lax.rem(z + 3, 8)
    z_down = lax.rem(z + 5, 8)

    def wrapped(source_z):
        return 1 - jnp.minimum(source_z // 2, 1)

    def at_zy(zz, yy):
        return (lax.rem(zz, 2), seq + 8 * (zz // 2 - zh) + 32 * (yy - y))

    leg1_to = at_zy(z_up, y)
    leg2_to = at_zy(z_up, lax.rem(y + 4 - wrapped(z_down), 4))
    leg2_from = at_zy(z_down, lax.rem(y + wrapped(lax.rem(z + 2, 8)), 4))

    lax.fori_loop(1, 16, greet_high, 0)
    lax.fori_loop(0, 4, greet_z, 0)
    greet(leg2_from)
    greet(at(up))
    greet(at(down))
    lax.fori_loop(1, 8, greet_low, 0)

    def far_copy(k):
        rows = pl.ds(ORDER[k] * COLS, COLS)
        return copy(
            g_hbm.at[rows], cots.at[2, rows], far_send.at[k], far_recv.at[k], at(far_to)
        )

    def near_copy(k, own):
        rows = pl.ds(ORDER[k] * COLS, COLS)
        return copy(
            (g_hbm if own else cots.at[2]).at[rows], cots.at[1, rows],
            near_send.at[k], near_recv.at[k], at(near_to),
        )

    def leg1_copy(i):
        rows = pl.ds(ORDER[6 + i] * COLS, COLS)
        return copy(g_hbm.at[rows], passing.at[i], leg1_send.at[i], leg1_recv.at[i], leg1_to)

    def leg2_copy(i):
        rows = pl.ds(ORDER[6 + i] * COLS, COLS)
        return copy(
            passing.at[i], cots.at[2, rows], leg2_send.at[i], far_recv.at[6 + i], leg2_to
        )

    def pass_detour(i):
        leg1_copy(i).wait_recv()
        leg2_copy(i).start()

    def exchange(buf, n, me, target, send_sem, recv_sem):
        def body(j, _):
            o = lax.rem(me + j, n)
            copy(buf.at[me], buf.at[me], send_sem.at[o], recv_sem.at[me], at(target(o))).start()
            return 0

        lax.fori_loop(1, n, body, 0)

    def collect(buf, n, me, target, send_sem, recv_sem):
        def body(j, _):
            o = lax.rem(me + j, n)
            arrived = copy(buf.at[o], buf.at[o], send_sem.at[o], recv_sem.at[o], at(target(o)))
            arrived.wait_recv()
            return 0

        lax.fori_loop(1, n, body, 0)
        total = buf[0]
        for o in range(1, n):
            total = total + buf[o]
        return total

    def drain(buf, n, me, target, send_sem, recv_sem):
        def body(j, _):
            o = lax.rem(me + j, n)
            copy(buf.at[me], buf.at[me], send_sem.at[o], recv_sem.at[me], at(target(o))).wait_send()
            return 0

        lax.fori_loop(1, n, body, 0)

    def low_of(o):
        return seq - low + o

    def high_of(o):
        return o * 8 + low

    row_id = lax.broadcasted_iota(jnp.int32, (2, CHANNELS), 0)

    def pack_rows(first, second):
        return jnp.where(row_id == 0, first, second)

    group_a = lax.shift_right_logical(lax.broadcasted_iota(jnp.int32, (CHANNELS, CHANNELS), 0), 3)
    group_b = lax.shift_right_logical(lax.broadcasted_iota(jnp.int32, (CHANNELS, CHANNELS), 1), 3)
    same_group = jnp.where(group_a == group_b, 1.0, 0.0).astype(BF16)

    def group_sum(v):
        total = jnp.zeros_like(v)
        rest = v
        for _ in range(3):
            piece = rest.astype(BF16)
            rest = rest - piece.astype(F32)
            total = total + jnp.dot(piece, same_group, preferred_element_type=F32)
        return total

    load_x.wait()

    def stat_body(i, carry):
        a, b = carry
        blk = xv[pl.ds(i * COLS, COLS), :].astype(F32).reshape(COLS // 8, 8, CHANNELS)
        return a + jnp.sum(blk, axis=0), b + jnp.sum(blk * blk, axis=0)

    zero8 = jnp.zeros((8, CHANNELS), F32)
    a, b = lax.fori_loop(0, ROWS_DEV, stat_body, (zero8, zero8))
    stat_a[low] = pack_rows(jnp.sum(a, axis=0, keepdims=True), jnp.sum(b, axis=0, keepdims=True))
    pl.semaphore_wait(barrier, 15 + 4 + 1 + 2 + 7)

    exchange(stat_a, 8, low, low_of, sa_send, sa_recv)
    leg1_copy(0).start()
    far_copy(0).start()
    leg1_copy(1).start()

    @pl.when(x_high == 1)
    def send_own():
        for k in range(8):
            near_copy(k, True).start()

    load_wt.wait()
    load_wsp.wait()
    for k in range(3):
        wtt[k] = wt[k].T

    def turn_weight(i, _):
        wspt[pl.ds(i * CHANNELS, CHANNELS), :] = wsp[pl.ds((8 - i) * CHANNELS, CHANNELS), :].T
        return 0

    lax.fori_loop(0, 9, turn_weight, 0)

    stat_b[high] = collect(stat_a, 8, low, low_of, sa_send, sa_recv)
    exchange(stat_b, 16, high, high_of, sb_send, sb_recv)
    for k in (1, 2, 3):
        far_copy(k).start()
    load_g.wait()
    moments = group_sum(collect(stat_b, 16, high, high_of, sb_send, sb_recv)) * (1.0 / COUNT)
    mean = moments[0:1]
    rstd = lax.rsqrt(moments[1:2] - mean * mean + EPS)
    load_gain.wait()
    load_bias.wait()
    gain = affine[0]
    bias = affine[1]

    def forward(k):
        far_copy(k).wait_recv()

        @pl.when(x_high == 0)
        def pass_on():
            near_copy(k, False).start()


    col_id = lax.broadcasted_iota(jnp.int32, (COLS, CHANNELS), 0)

    def store_shifts(buf, padded_row, v):
        rows = pl.ds(padded_row * COLS, COLS)
        buf[rows, CHANNELS : 2 * CHANNELS] = v.astype(BF16)
        left = jnp.where(col_id == 0, 0.0, pltpu.roll(v, 1, 0))
        right = jnp.where(col_id == COLS - 1, 0.0, pltpu.roll(v, COLS - 1, 0))
        buf[rows, 0:CHANNELS] = left.astype(BF16)
        buf[rows, 2 * CHANNELS : 3 * CHANNELS] = right.astype(BF16)

    def normalize(rows):
        xhat = (xv[rows, :].astype(F32) - mean) * rstd
        pre = xhat * gain + bias
        return xhat, pre, jax.nn.sigmoid(pre)

    def act_row(r):
        _, pre, sigma = normalize(pl.ds(r * COLS, COLS))
        store_shifts(act3, r + 1, pre * sigma)

    middle = slice(CHANNELS, 2 * CHANNELS)

    def halo_copies(buf, halo, send_sem, recv_sem):
        first = copy(
            buf.at[pl.ds(COLS, COLS), middle], halo.at[1], send_sem.at[0], recv_sem.at[1], at(down)
        )
        last = copy(
            buf.at[pl.ds(PIXELS, COLS), middle], halo.at[0], send_sem.at[1], recv_sem.at[0], at(up)
        )
        return first, last

    def send_halo(buf, halo, send_sem, recv_sem):
        for c in halo_copies(buf, halo, send_sem, recv_sem):
            c.start()

    def take_halo(buf, halo, send_sem, recv_sem):
        for c in halo_copies(buf, halo, send_sem, recv_sem):
            c.wait_recv()
        keep_low = jnp.where(place > 0, 1.0, 0.0).astype(F32)
        keep_high = jnp.where(place < 3, 1.0, 0.0).astype(F32)
        store_shifts(buf, 0, halo[0].astype(F32) * keep_low)
        store_shifts(buf, ROWS_DEV + 1, halo[1].astype(F32) * keep_high)

    act_row(0)
    act_row(ROWS_DEV - 1)
    send_halo(act3, act_halo, ah_send, ah_recv)
    far_copy(4).start()
    far_copy(5).start()
    pass_detour(0)

    def act_body(r, _):
        act_row(r)
        return 0

    lax.fori_loop(1, ROWS_DEV - 1, act_body, 0)

    def convolve(buf, weights, i):
        total = None
        for dy in range(3):
            term = jnp.dot(
                buf[pl.ds(i * BLOCK + dy * COLS, BLOCK), :],
                weights[dy * 3 * CHANNELS : (dy + 1) * 3 * CHANNELS, :],
                preferred_element_type=F32,
            )
            total = term if total is None else total + term
        return total

    keep1 = jnp.where(frame < FRAMES - 1, 1.0, 0.0).astype(F32)
    keep2 = jnp.where(frame < FRAMES - 2, 1.0, 0.0).astype(F32)

    def cg_row(k):
        r = ORDER[k]
        near_copy(k, True).wait_recv()
        rows = pl.ds(r * COLS, COLS)
        total = jnp.dot(cots[0, rows, :], wtt[0], preferred_element_type=F32)
        total = total + keep1 * jnp.dot(cots[1, rows, :], wtt[1], preferred_element_type=F32)
        total = total + keep2 * jnp.dot(cots[2, rows, :], wtt[2], preferred_element_type=F32)
        store_shifts(cg3, r + 1, total.astype(BF16).astype(F32))

    def put(first_row, v, add):
        rows = pl.ds(first_row, v.shape[0])
        for half in range(2):
            w = v[:, half * 128 : (half + 1) * 128]
            part[half, rows, :] = part[half, rows, :] + w if add else w

    half_pixels = PIXELS // 2

    def temporal_half(h):
        pixels = slice(h * half_pixels, (h + 1) * half_pixels)
        for k, keep in enumerate((None, keep1, keep2)):
            v = jnp.dot(convt[:, pixels], cots[k, pixels, :], preferred_element_type=F32)
            put((9 + k) * CHANNELS, v if keep is None else v * keep, h > 0)

    def spatial_half(h, dy):
        begin = h * half_pixels
        v = lax.dot_general(
            act3[dy * COLS + begin : dy * COLS + begin + half_pixels, :],
            cg3[COLS + begin : COLS + begin + half_pixels, middle],
            (((0,), (0,)), ((), ())),
            preferred_element_type=F32,
        )
        put(dy * chunk_rows, v, h > 0)

    chunk_rows = PART

    def core_copy(i):
        rows = pl.ds(i * chunk_rows, chunk_rows)
        return copy(
            part.at[1 - core, rows], core_in.at[rows], core_send.at[i], core_recv.at[i],
            at(other_core),
        )

    forward(0)
    pass_detour(1)
    forward(1)
    forward(2)
    cg_row(0)
    cg_row(1)
    send_halo(cg3, cg_halo, ch_send, ch_recv)
    forward(3)
    take_halo(act3, act_halo, ah_send, ah_recv)

    def conv_body(i, _):
        conv[pl.ds(i * BLOCK, BLOCK), :] = convolve(act3, wsp, i).astype(BF16)
        return 0

    lax.fori_loop(0, PIXELS // BLOCK, conv_body, 0)
    forward(4)
    cg_row(2)

    def turn_conv(i, _):
        src = pl.ds(pl.multiple_of(i * 128, 128), 128)
        convt[:, src] = conv[src, :].T
        return 0

    lax.fori_loop(0, PIXELS // 128, turn_conv, 0)
    cg_row(3)
    forward(5)
    cg_row(4)
    forward(6)
    temporal_half(0)
    spatial_half(0, 0)
    forward(7)
    spatial_half(0, 1)
    spatial_half(0, 2)
    drain(stat_a, 8, low, low_of, sa_send, sa_recv)
    drain(stat_b, 16, high, high_of, sb_send, sb_recv)
    for c in halo_copies(act3, act_halo, ah_send, ah_recv):
        c.wait_send()
    cg_row(5)
    take_halo(cg3, cg_halo, ch_send, ch_recv)
    cg_row(6)
    cg_row(7)
    temporal_half(1)
    core_copy(3).start()
    for dy in PART_ORDER[1:]:
        spatial_half(1, dy)
        core_copy(dy).start()

    def back_block(i, carry):
        rows = pl.ds(i * BLOCK, BLOCK)
        xhat, pre, sigma = normalize(rows)
        v = convolve(cg3, wspt, i) * sigma * (1.0 + pre * (1.0 - sigma))
        pre_grad[rows, :] = v
        a, b = carry
        a = a + jnp.sum(v.reshape(BLOCK // 8, 8, CHANNELS), axis=0)
        b = b + jnp.sum((v * xhat).reshape(BLOCK // 8, 8, CHANNELS), axis=0)
        return a, b

    def first_axis(p):
        return ((x, at_x), (y, at_y))[p // 2]

    def second_axis(p):
        return ((y, at_y), (x, at_x))[p // 2]

    def loop3(me, body):
        def step(j, _):
            body(lax.rem(me + j, 4))
            return 0

        lax.fori_loop(1, 4, step, 0)

    def s1_copy(p, o):
        me, target = first_axis(p)
        return copy(
            part.at[core, pl.ds(p * PART + o * QUARTER, QUARTER)], in1.at[p, me],
            s1_send.at[p, o], s1_recv.at[p, me], target(o),
        )

    def s1_arrived(p, o):
        _, target = first_axis(p)
        return copy(in1.at[p, o], in1.at[p, o], s1_send.at[p, o], s1_recv.at[p, o], target(o))

    def s2_copy(p, o):
        me, target = second_axis(p)
        return copy(
            mid.at[p, pl.ds(o * SHARD, SHARD)], in2.at[p, me],
            s2_send.at[p, o], s2_recv.at[p, me], target(o),
        )

    def s2_arrived(p, o):
        _, target = second_axis(p)
        return copy(in2.at[p, o], in2.at[p, o], s2_send.at[p, o], s2_recv.at[p, o], target(o))

    def add_core(p):
        core_copy(p).wait_recv()
        rows = pl.ds(p * PART, PART)
        part[core, rows, :] = part[core, rows, :] + core_in[rows, :]
        loop3(first_axis(p)[0], lambda o: s1_copy(p, o).start())

    sums = (zero8, zero8)
    add_core(PART_ORDER[0])
    for i, p in enumerate(PART_ORDER[1:]):
        add_core(p)
        sums = back_block(i, sums)
    sums = back_block(PARTS - 1, sums)
    a, b = sums
    back_a[low] = pack_rows(jnp.sum(a, axis=0, keepdims=True), jnp.sum(b, axis=0, keepdims=True))
    exchange(back_a, 8, low, low_of, ba_send, ba_recv)

    def s1_finish(p):
        me, _ = first_axis(p)
        loop3(me, lambda o: s1_arrived(p, o).wait_recv())
        total = part[core, pl.ds(p * PART + me * QUARTER, QUARTER), :]
        for j in range(1, 4):
            total = total + in1[p, lax.rem(me + j, 4)]
        mid[p] = total
        loop3(second_axis(p)[0], lambda o: s2_copy(p, o).start())

    def s3_copy(o, slot):
        return copy(mid2.at[o // 2], in3.at[slot], s3_send.at[o], s3_recv.at[slot], at_z(o))

    def s2_finish(p):
        me, _ = second_axis(p)
        loop3(me, lambda o: s2_arrived(p, o).wait_recv())
        total = mid[p, pl.ds(me * SHARD, SHARD), :]
        for j in range(1, 4):
            total = total + in2[p, lax.rem(me + j, 4)]
        mid2[p] = total
        for o in (2 * p, 2 * p + 1):
            @pl.when(z != o)
            def send_shard():
                s3_copy(o, z).start()

    for k in range(8):
        near_copy(k, True).wait_send()
    for k in range(6):
        far_copy(k).wait_send()
    for i in range(2):
        leg1_copy(i).wait_send()
        leg2_copy(i).wait_send()
    for c in halo_copies(cg3, cg_halo, ch_send, ch_recv):
        c.wait_send()

    for p in PART_ORDER:
        s1_finish(p)

    for p in PART_ORDER:
        s2_finish(p)

    back_b[high] = collect(back_a, 8, low, low_of, ba_send, ba_recv)
    exchange(back_b, 16, high, high_of, bb_send, bb_recv)

    for p in PART_ORDER:
        core_copy(p).wait_send()
        loop3(first_axis(p)[0], lambda o: s1_copy(p, o).wait_send())
    drain(back_a, 8, low, low_of, ba_send, ba_recv)

    def quarter_at(p, first):
        return pl.multiple_of(p * PART + QUARTER * first, QUARTER)

    def shard_at(p, first, second):
        return pl.multiple_of(p * PART + QUARTER * first + SHARD * second, SHARD)

    def own_shard(p):
        return full.at[core, pl.ds(shard_at(p, first_axis(p)[0], second_axis(p)[0]), SHARD)]

    def g3_copy(p, o):
        rows = own_shard(p)
        return copy(rows, rows, g3_send.at[o], g3_recv.at[p], at_zh(o))

    def g2_copy(p, o, sender):
        rows = full.at[core, pl.ds(shard_at(p, first_axis(p)[0], sender), SHARD)]
        return copy(rows, rows, g2_send.at[p, o], g2_recv.at[p, sender], second_axis(p)[1](o))

    def g1_copy(p, o, sender):
        rows = full.at[core, pl.ds(quarter_at(p, sender), QUARTER)]
        return copy(rows, rows, g1_send.at[p, o], g1_recv.at[p, sender], first_axis(p)[1](o))

    def to_core(p, half):
        rows = full.at[half, pl.ds(p * PART, PART)]
        return copy(rows, rows, gc_send.at[p], gc_recv.at[p], at(other_core))

    def store_params(p, half, slot):
        rows = pl.ds(p * PART, PART)
        return pltpu.make_async_copy(
            full.at[half, rows], params_out.at[half, rows], store_sem.at[1 + slot * PARTS + p]
        )

    for p in PART_ORDER:
        @pl.when(zh == p)
        def finish_part():
            in3[z] = mid2[p]

            def arrived(j, _):
                o = lax.rem(z + j, 8)
                copy(in3.at[o], in3.at[o], s3_send.at[o], s3_recv.at[o], at_z(o)).wait_recv()
                return 0

            lax.fori_loop(1, 8, arrived, 0)
            total = in3[0]
            for o in range(1, 8):
                total = total + in3[o]
            where = pl.ds(shard_at(p, first_axis(p)[0], second_axis(p)[0]), SHARD)
            full[core, where, :] = (total * SCALE).astype(BF16)
            loop3(zh, lambda o: g3_copy(p, o).start())

    for p in PART_ORDER:
        @pl.when(zh != p)
        def take_part():
            g3_copy(p, zh + 1 - 2 * lax.rem(zh, 2)).wait_recv()

        me, _ = second_axis(p)
        loop3(me, lambda o: g2_copy(p, o, me).start())

    for p in PART_ORDER:
        loop3(second_axis(p)[0], lambda o: s2_copy(p, o).wait_send())

    for p in PART_ORDER:
        loop3(second_axis(p)[0], lambda o: g2_copy(p, o, o).wait_recv())
        me, _ = first_axis(p)
        loop3(me, lambda o: g1_copy(p, o, me).start())

    sums = collect(back_b, 16, high, high_of, bb_send, bb_recv)
    clip_sums[clip] = sums
    clip_copy = copy(
        clip_sums.at[clip], clip_sums.at[clip], clip_sem.at[0], clip_sem.at[1], (1 - clip, seq)
    )
    clip_copy.start()
    norm_sums = group_sum(sums * gain) * (1.0 / COUNT)
    m1 = norm_sums[0:1]
    m2 = norm_sums[1:2]

    def out_body(i, _):
        rows = pl.ds(i * COLS, COLS)
        xhat = (xv[rows, :].astype(F32) - mean) * rstd
        v = rstd * (pre_grad[rows, :] * gain - m1 - xhat * m2)
        grad_v[rows, :] = (cots[0, rows, :].astype(F32) + v).astype(BF16)
        return 0

    lax.fori_loop(0, ROWS_DEV, out_body, 0)
    store_grad = pltpu.make_async_copy(grad_v, grad_out, store_sem.at[0])
    store_grad.start()

    def s3_sent(j, _):
        s3_copy(lax.rem(z + j, 8), z).wait_send()
        return 0

    lax.fori_loop(1, 8, s3_sent, 0)
    drain(back_b, 16, high, high_of, bb_send, bb_recv)
    for p in PART_ORDER:
        @pl.when(zh == p)
        def sent_part():
            loop3(zh, lambda o: g3_copy(p, o).wait_send())

        loop3(second_axis(p)[0], lambda o: g2_copy(p, o, second_axis(p)[0]).wait_send())

    for p in PART_ORDER:
        loop3(first_axis(p)[0], lambda o: g1_copy(p, o, o).wait_recv())
        to_core(p, core).start()
        store_params(p, core, 0).start()

    for p in PART_ORDER:
        loop3(first_axis(p)[0], lambda o: g1_copy(p, o, first_axis(p)[0]).wait_send())

    for p in PART_ORDER:
        to_core(p, 1 - core).wait_recv()
        store_params(p, 1 - core, 1).start()
    copy(
        clip_sums.at[1 - clip], clip_sums.at[1 - clip], clip_sem.at[0], clip_sem.at[1],
        (1 - clip, seq),
    ).wait_recv()
    sums_v[...] = (clip_sums[0] + clip_sums[1]) * SCALE
    store_sums = pltpu.make_async_copy(sums_v, sums_out, store_sem.at[1 + 2 * PARTS])
    store_sums.start()

    clip_copy.wait_send()
    store_grad.wait()
    store_sums.wait()
    for p in PART_ORDER:
        to_core(p, core).wait_send()
        store_params(p, core, 0).wait()
        store_params(p, 1 - core, 1).wait()


def finish_kernel(
    grad, params, sums, grad_out, spatial, temporal, gain_out, bias_out,
    grad_v, params_v, out_v, sums_v, bias_v, gain_v, sem,
):
    load_grad = pltpu.make_async_copy(grad, grad_v, sem.at[0])
    store_grad = pltpu.make_async_copy(grad_v, grad_out, sem.at[9])

    def load(i):
        taps = pl.ds(3 * i, 3)
        return pltpu.make_async_copy(params.at[:, taps], params_v.at[:, taps], sem.at[1 + i])

    def store(i):
        target = spatial.at[pl.ds(3 * i, 3)] if i < 3 else temporal
        return pltpu.make_async_copy(out_v.at[pl.ds(3 * i, 3)], target, sem.at[5 + i])

    for i in range(4):
        load(i).start()
    load_grad.start()
    load_sums = pltpu.make_async_copy(sums, sums_v, sem.at[10])
    load_sums.start()
    store_bias = pltpu.make_async_copy(bias_v, bias_out, sem.at[11])
    store_gain = pltpu.make_async_copy(gain_v, gain_out, sem.at[12])
    for i in range(4):
        load(i).wait()
        for half in range(2):
            out_v[3 * i : 3 * i + 3, :, half * 128 : (half + 1) * 128] = params_v[
                half, 3 * i : 3 * i + 3
            ].astype(F32)
        store(i).start()
    load_grad.wait()
    store_grad.start()
    load_sums.wait()
    bias_v[...] = sums_v[0]
    gain_v[...] = sums_v[1]
    store_bias.start()
    store_gain.start()
    store_grad.wait()
    store_bias.wait()
    store_gain.wait()
    for i in range(4):
        store(i).wait()


def local(block_input, cotangent, group_norm_gain, group_norm_bias, w_spatial, w_temporal):
    any_space = pl.BlockSpec(memory_space=pl.ANY)
    dma = pltpu.SemaphoreType.DMA
    scratch = [
        pltpu.VMEM((PIXELS, CHANNELS), BF16),
        pltpu.VMEM((3, PIXELS, CHANNELS), BF16),
        pltpu.VMEM((PADDED, 3 * CHANNELS), BF16),
        pltpu.VMEM((PADDED, 3 * CHANNELS), BF16),
        pltpu.VMEM((PIXELS, CHANNELS), BF16),
        pltpu.VMEM((CHANNELS, PIXELS), BF16),
        pltpu.VMEM((9 * CHANNELS, CHANNELS), BF16),
        pltpu.VMEM((9 * CHANNELS, CHANNELS), BF16),
        pltpu.VMEM((3, CHANNELS, CHANNELS), BF16),
        pltpu.VMEM((3, CHANNELS, CHANNELS), BF16),
        pltpu.VMEM((PIXELS, CHANNELS), F32),
        pltpu.VMEM((2, COLS, CHANNELS), BF16),
        pltpu.VMEM((2, COLS, CHANNELS), BF16),
        pltpu.VMEM((8, 2, CHANNELS), F32),
        pltpu.VMEM((16, 2, CHANNELS), F32),
        pltpu.VMEM((8, 2, CHANNELS), F32),
        pltpu.VMEM((16, 2, CHANNELS), F32),
        pltpu.VMEM((2, 2, CHANNELS), F32),
        pltpu.VMEM((2, HALF_ROWS, 128), F32),
        pltpu.VMEM((HALF_ROWS, 128), F32),
        pltpu.VMEM((PARTS, 4, QUARTER, 128), F32),
        pltpu.VMEM((PARTS, QUARTER, 128), F32),
        pltpu.VMEM((PARTS, 4, SHARD, 128), F32),
        pltpu.VMEM((PARTS, SHARD, 128), F32),
        pltpu.VMEM((8, SHARD, 128), F32),
        pltpu.VMEM((2, HALF_ROWS, 128), BF16),
        pltpu.VMEM((PIXELS, CHANNELS), BF16),
        pltpu.VMEM((2, COLS, CHANNELS), BF16),
        pltpu.VMEM((2, 1, CHANNELS), F32),
        pltpu.VMEM((2, CHANNELS), F32),
        dma((6,)), dma((2 + 2 * PARTS,)),
        dma((8,)), dma((8,)), dma((8,)), dma((8,)),
        dma((2,)), dma((2,)), dma((2,)),
        dma((2,)), dma((2,)), dma((2,)), dma((2,)),
        dma((8,)), dma((8,)), dma((16,)), dma((16,)),
        dma((8,)), dma((8,)), dma((16,)), dma((16,)),
        dma((2,)),
        dma((4,)), dma((4,)),
        dma((4, 4)), dma((4, 4)), dma((4, 4)), dma((4, 4)),
        dma((8,)), dma((8,)),
        dma((4,)), dma((4,)), dma((4, 4)), dma((4, 4)), dma((4, 4)), dma((4, 4)),
        dma((4,)), dma((4,)),
    ]
    grad, params, sums = pl.pallas_call(
        kernel,
        out_shape=(
            jax.ShapeDtypeStruct((PIXELS, CHANNELS), BF16),
            jax.ShapeDtypeStruct((2, HALF_ROWS, 128), BF16),
            jax.ShapeDtypeStruct((2, CHANNELS), F32),
        ),
        in_specs=[any_space] * 6,
        out_specs=(any_space, any_space, any_space),
        scratch_shapes=scratch,
        compiler_params=pltpu.CompilerParams(
            collective_id=0, has_side_effects=True, vmem_limit_bytes=56 * 2**20
        ),
    )(
        block_input.reshape(PIXELS, CHANNELS),
        cotangent.reshape(PIXELS, CHANNELS),
        group_norm_gain.reshape(1, CHANNELS),
        group_norm_bias.reshape(1, CHANNELS),
        w_spatial.reshape(9 * CHANNELS, CHANNELS),
        w_temporal,
    )
    params = params.reshape(2, TAPS, CHANNELS, 128)
    grad, spatial, temporal, gain_grad, bias_grad = pl.pallas_call(
        finish_kernel,
        out_shape=(
            jax.ShapeDtypeStruct((PIXELS, CHANNELS), BF16),
            jax.ShapeDtypeStruct((9, CHANNELS, CHANNELS), F32),
            jax.ShapeDtypeStruct((3, CHANNELS, CHANNELS), F32),
            jax.ShapeDtypeStruct((CHANNELS,), F32),
            jax.ShapeDtypeStruct((CHANNELS,), F32),
        ),
        in_specs=[any_space] * 3,
        out_specs=(any_space,) * 5,
        scratch_shapes=[
            pltpu.VMEM((PIXELS, CHANNELS), BF16),
            pltpu.VMEM((2, TAPS, CHANNELS, 128), BF16),
            pltpu.VMEM((TAPS, CHANNELS, CHANNELS), F32),
            pltpu.VMEM((2, CHANNELS), F32),
            pltpu.VMEM((CHANNELS,), F32),
            pltpu.VMEM((CHANNELS,), F32),
            dma((13,)),
        ],
        compiler_params=pltpu.CompilerParams(vmem_limit_bytes=60 * 2**20),
    )(grad, params, sums)
    return (
        grad.reshape(1, ROWS_DEV, COLS, CHANNELS),
        spatial,
        temporal,
        gain_grad,
        bias_grad,
    )


def solution(mesh):
    return jax.shard_map(
        local,
        mesh=mesh,
        in_specs=(P("dp", "seq", None, None), P("dp", "seq", None, None), P(), P(), P(), P()),
        out_specs=(P("dp", "seq", None, None), P(), P(), P(), P()),
        check_vma=False,
    )
```
